32 devices in a mesh: groups: 2 (over x), ctx: 16 (over z, y, core).
Axes of the slice: x: 2, y: 2, z: 4, core: 2. Of those that a mesh axis runs over, the one named last changes fastest.
Arguments:
- query_vectors: bfloat16 [4096, 3584], P(('groups', 'ctx')), parts along dimension 0, may hold values from -6 to 6
- key_vectors: bfloat16 [4096, 512], P(('groups', 'ctx')), parts along dimension 0, may hold values from -6 to 6
- value_vectors: bfloat16 [4096, 512], P(('groups', 'ctx')), parts along dimension 0, may hold values from -6 to 6
- outputs: bfloat16 [4096, 3584], P(('groups', 'ctx')), parts along dimension 0, may hold values from -6 to 6
- output_grad: bfloat16 [4096, 3584], P(('groups', 'ctx')), parts along dimension 0, may hold values from -6 to 6
- log_normalizer: float32 [28, 4096], P(None, ('groups', 'ctx')), parts along dimension 1, may hold values from 2 to 5
- document_lengths: int32 [8], P('groups'), parts along dimension 0, may hold values from 1 to 1024, 2048 in all
Outputs:
- query_grad: bfloat16 [4096, 3584], P(('groups', 'ctx')), parts along dimension 0
- key_grad: bfloat16 [4096, 512], P(('groups', 'ctx')), parts along dimension 0
- value_grad: bfloat16 [4096, 512], P(('groups', 'ctx')), parts along dimension 0
The draws below stay inside these ranges and needn't reach their ends.
There are 2 independent parts, one for each index of `groups`. The reference program is written for one: setup_inputs(seed, part) draws one part's arguments, and reference() takes and returns one part's arrays. A program takes and returns all parts, laid end to end along the dimension named above; each array names one. Nothing has to cross between parts.
Inputs may be any that keep to these rules, and one draw needn't show every extreme that they name: `document_lengths`: the 4 documents lie end to end from position 0 and their lengths sum to 2048.
All inputs are finite; a program needn't handle non-finite values.
Results may differ from the reference program's by a relative error of at most 0.0052.
Values may be sent and summed in bfloat16 or wider, within the bound.
No kernel may reach another device: no remote copies, remote signals or barrier semaphores. Data moves between devices by JAX's collectives and lax.ppermute only.
A program may use at most 64 MiB of HBM per device.

```python
import math
import jax
import jax.numpy as jnp
import numpy as np
from jax import lax

QUERY_HEADS = 28
KEY_VALUE_HEADS = 4
HEAD_WIDTH = 128
BLOCK_TOKENS = 128
KW = 8
DOCS = 4
TOKENS = 2048
WINDOW = 896
MAXDOC = 1024


def shard_levels(rng, shape, cuts, smallest, largest):
    factor_of, own = 1.0, jax.random.fold_in(rng, 6)
    for axis_at, shards_of in cuts:
        steps = jnp.exp(jax.random.uniform(jax.random.fold_in(own, axis_at), (shards_of,), jnp.float32, smallest / len(cuts), largest / len(cuts)))
        factor_of = factor_of * jnp.repeat(steps, shape[axis_at] // shards_of).reshape([-1 if axis == axis_at else 1 for axis in range(len(shape))])
    return factor_of


def profile(amount, total, most, lean):
    portions = [(1 << 20) // math.isqrt(rank ** lean) + 1 for rank in range(2, amount + 1)]
    surplus, counts = total - most - (amount - 1), [1] * (amount - 1)
    while surplus > 0:
        free = [i for i in range(amount - 1) if counts[i] < most]
        pool, budget = sum([portions[i] for i in free]), surplus
        for i in free:
            addition = min(most - counts[i], max(1, budget * portions[i] // pool), surplus)
            counts[i] = counts[i] + addition
            surplus = surplus - addition
    return np.array([most] + counts)


def ragged_sizes(own_key, amount, total, reach, lean):
    if amount == 2:
        one = jax.random.randint(own_key, (), max(1, total - reach), min(reach, total - 1) + 1)
        return jnp.stack([one, total - one])
    sizes = jnp.asarray(profile(amount, total, reach, lean), jnp.int32)
    pairs = (amount - 1) // 2
    donor, receiver = sizes[1:1 + 2 * pairs:2], sizes[2:2 + 2 * pairs:2]
    room = jnp.minimum(donor - 1, reach - receiver)
    passed = jax.random.randint(jax.random.fold_in(own_key, 1), (pairs,), 0, 1 << 20) % (room + 1)
    sizes = sizes.at[1:1 + 2 * pairs:2].set(donor - passed).at[2:2 + 2 * pairs:2].set(receiver + passed)
    return sizes[jax.random.permutation(jax.random.fold_in(own_key, 2), amount)]


def normal_values(key, dims, spread, limit, shards=(), kind=jnp.bfloat16):
    array = spread * jax.random.normal(key, dims, jnp.float32)
    if shards:
        array = array * shard_levels(key, dims, shards, -0.22, 0.18)
    return jnp.clip(array, -limit, limit).astype(kind)


def setup_inputs(seed: int = 0, part: int = 0) -> dict:
    key_of = jax.random.split(jax.random.key(seed), 8)
    part_keys = jax.random.split(jax.random.fold_in(key_of[7], part), 8)
    return {
        "query_vectors": normal_values(part_keys[0], (TOKENS, QUERY_HEADS * HEAD_WIDTH), 1.0, 6.0, ((0, 16),)),
        "key_vectors": normal_values(part_keys[1], (TOKENS, KEY_VALUE_HEADS * HEAD_WIDTH), 1.0, 6.0, ((0, 16),)),
        "value_vectors": normal_values(part_keys[2], (TOKENS, KEY_VALUE_HEADS * HEAD_WIDTH), 1.0, 6.0, ((0, 16),)),
        "outputs": normal_values(part_keys[3], (TOKENS, QUERY_HEADS * HEAD_WIDTH), 1.0, 6.0, ((0, 16),)),
        "output_grad": normal_values(part_keys[4], (TOKENS, QUERY_HEADS * HEAD_WIDTH), 1.0, 6.0, ((0, 16),)),
        "log_normalizer": jnp.clip(2.0 + 3.0 * jax.random.uniform(part_keys[5], (QUERY_HEADS, TOKENS), jnp.float32) ** shard_levels(part_keys[5], (QUERY_HEADS, TOKENS), ((1, 16),), -0.2, 0.2), 2.0, 5.0),
        "document_lengths": ragged_sizes(part_keys[6], DOCS, TOKENS, MAXDOC, 2).astype(jnp.int32),
    }


def reference(query_vectors, key_vectors, value_vectors, outputs, output_grad, log_normalizer, document_lengths):
    per_group = QUERY_HEADS // KEY_VALUE_HEADS
    logit_scale = HEAD_WIDTH ** -0.5
    margin = (KW - 1) * BLOCK_TOKENS
    visible_mask = KW * BLOCK_TOKENS
    document_ends = jnp.cumsum(document_lengths).astype(jnp.int32)
    places = jnp.arange(TOKENS, dtype=jnp.int32)
    segments = jnp.sum((document_ends[None, :] <= places[:, None]).astype(jnp.int32), axis=1).astype(jnp.int32)
    pad_places = jnp.concatenate([jnp.full((margin,), -1, jnp.int32), places])
    pad_segments = jnp.concatenate([jnp.full((margin,), -1, jnp.int32), segments])
    pad_keys = jnp.concatenate([jnp.zeros((margin, KEY_VALUE_HEADS * HEAD_WIDTH), key_vectors.dtype), key_vectors])
    pad_values = jnp.concatenate([jnp.zeros((margin, KEY_VALUE_HEADS * HEAD_WIDTH), value_vectors.dtype), value_vectors])

    def step(carried, block):
        key_total, value_total = carried
        start = (block * BLOCK_TOKENS).astype(jnp.int32)
        query_rows = lax.dynamic_slice_in_dim(query_vectors, start, BLOCK_TOKENS, 0).astype(jnp.float32).reshape(BLOCK_TOKENS, KEY_VALUE_HEADS, per_group, HEAD_WIDTH)
        gradient_list = lax.dynamic_slice_in_dim(output_grad, start, BLOCK_TOKENS, 0).astype(jnp.float32).reshape(BLOCK_TOKENS, KEY_VALUE_HEADS, per_group, HEAD_WIDTH)
        forward = lax.dynamic_slice_in_dim(outputs, start, BLOCK_TOKENS, 0).astype(jnp.float32).reshape(BLOCK_TOKENS, KEY_VALUE_HEADS, per_group, HEAD_WIDTH)
        norms = lax.dynamic_slice_in_dim(log_normalizer, start, BLOCK_TOKENS, 1).reshape(KEY_VALUE_HEADS, per_group, BLOCK_TOKENS)
        delta = jnp.transpose(jnp.sum(gradient_list * forward, axis=3), (1, 2, 0))
        present_keys = lax.dynamic_slice_in_dim(pad_keys, start, visible_mask, 0).astype(jnp.float32).reshape(visible_mask, KEY_VALUE_HEADS, HEAD_WIDTH)
        present_values = lax.dynamic_slice_in_dim(pad_values, start, visible_mask, 0).astype(jnp.float32).reshape(visible_mask, KEY_VALUE_HEADS, HEAD_WIDTH)
        query_places = lax.dynamic_slice_in_dim(places, start, BLOCK_TOKENS, 0)
        query_segments = lax.dynamic_slice_in_dim(segments, start, BLOCK_TOKENS, 0)
        key_places = lax.dynamic_slice_in_dim(pad_places, start, visible_mask, 0)
        key_segments = lax.dynamic_slice_in_dim(pad_segments, start, visible_mask, 0)
        allowed = (query_segments[:, None] == key_segments[None, :]) & (key_places[None, :] <= query_places[:, None]) & (key_places[None, :] >= 0) & (query_places[:, None] - key_places[None, :] < WINDOW)
        logit_matrix = jnp.einsum("uwym,awm->wyua", query_rows, present_keys) * logit_scale
        softmax = jnp.where(allowed, jnp.exp(logit_matrix - norms[..., None]), jnp.float32(0.0))
        rounded_length = lax.optimization_barrier(softmax.astype(jnp.bfloat16)).astype(jnp.float32)
        value_portion = jnp.einsum("lojw,jlop->wlp", rounded_length, gradient_list).reshape(visible_mask, KEY_VALUE_HEADS * HEAD_WIDTH)
        value_path_gradient = jnp.einsum("uwym,awm->wyua", gradient_list, present_values)
        logit_gradient = lax.optimization_barrier((softmax * (value_path_gradient - delta[..., None])).astype(jnp.bfloat16)).astype(jnp.float32)
        query_portion = jnp.einsum("hvux,xho->uhvo", logit_gradient, present_keys).reshape(BLOCK_TOKENS, QUERY_HEADS * HEAD_WIDTH) * logit_scale
        key_portion = jnp.einsum("lojw,jlop->wlp", logit_gradient, query_rows).reshape(visible_mask, KEY_VALUE_HEADS * HEAD_WIDTH) * logit_scale
        key_total = lax.dynamic_update_slice_in_dim(key_total, lax.dynamic_slice_in_dim(key_total, start, visible_mask, 0) + key_portion, start, 0)
        value_total = lax.dynamic_update_slice_in_dim(value_total, lax.dynamic_slice_in_dim(value_total, start, visible_mask, 0) + value_portion, start, 0)
        return (key_total, value_total), query_portion.astype(jnp.bfloat16)

    empty = jnp.zeros((margin + TOKENS, KEY_VALUE_HEADS * HEAD_WIDTH), jnp.float32)
    (key_total, value_total), query_blocks = lax.scan(step, (empty, empty), jnp.arange(TOKENS // BLOCK_TOKENS, dtype=jnp.int32))
    query_grad = query_blocks.reshape(TOKENS, QUERY_HEADS * HEAD_WIDTH)
    return query_grad, key_total[margin:].astype(jnp.bfloat16), value_total[margin:].astype(jnp.bfloat16)
```

```python
import functools
import math

import jax
import jax.numpy as jnp
from jax import lax
from jax.experimental import pallas as pl
from jax.experimental.pallas import tpu as pltpu
from jax.sharding import PartitionSpec as P

HEAD_WIDTH = 128
KEY_VALUE_HEADS = 4
WINDOW = 896
SCALE = HEAD_WIDTH ** (-0.5)
LOG2E = math.log2(math.e)
HALF = KEY_VALUE_HEADS // 2


def shift_pairs(devices, chips):
    first, last = max(0, -2 * chips), min(devices, devices - 2 * chips)
    return [(source, source + 2 * chips) for source in range(first, last)]


def partner_pairs(devices):
    return [(source, source ^ 1) for source in range(devices)]


def stats_kernel(per_group, outputs_ref, grad_ref, norm_ref, stats_ref):
    ones = jnp.ones((8, 2 * HEAD_WIDTH), jnp.bfloat16)
    group = pl.program_id(0)
    for r in range(per_group):
        cols = slice(r * HEAD_WIDTH, (r + 1) * HEAD_WIDTH)
        product = outputs_ref[:, cols].astype(jnp.float32) * grad_ref[:, cols].astype(jnp.float32)
        high = product.astype(jnp.bfloat16)
        low = (product - high.astype(jnp.float32)).astype(jnp.bfloat16)
        delta = lax.dot_general(
            ones,
            jnp.concatenate([high, low], axis=1),
            (((1,), (1,)), ((), ())),
            preferred_element_type=jnp.float32,
        )
        stats_ref[0, 8 + r : 9 + r, :] = delta[0:1, :]
        stats_ref[0, r : r + 1, :] = norm_ref[pl.ds(group * per_group + r, 1), :] * LOG2E
    stats_ref[0, per_group:8, :] = jnp.zeros((8 - per_group, stats_ref.shape[2]), jnp.float32)
    stats_ref[0, 8 + per_group : 16, :] = jnp.zeros((8 - per_group, stats_ref.shape[2]), jnp.float32)


def tile_kernel(
    config,
    place_ref,
    length_ref,
    q_mine,
    q_other,
    g_mine,
    g_other,
    stats_mine,
    stats_other,
    kv_ref,
    *rest,
):
    per_group, distance, row_start, has_sum, last = config
    if has_sum:
        sum_ref, dkv_ref, dq_ref, q_scr, g_scr, stats_scr, dq_scr = rest
    else:
        dkv_ref, dq_ref, q_scr, g_scr, stats_scr, dq_scr = rest
    block = q_mine.shape[0]
    keys = kv_ref.shape[0]
    core = lax.rem(place_ref[0], 2)
    chip = lax.div(place_ref[0], 2)
    mine, other = core * block, (1 - core) * block
    query_start = chip * 2 * block
    key_start = query_start - distance * 2 * block + row_start

    q_positions = query_start + lax.broadcasted_iota(jnp.int32, (1, 2 * block), 1)
    lowest = jnp.maximum(q_positions - (WINDOW - 1), 0)
    first_lowest = jnp.maximum(query_start - (WINDOW - 1), 0)
    end = jnp.int32(0)
    for i in range(length_ref.shape[0]):
        end = end + length_ref[i]
        lowest = jnp.where(q_positions >= end, jnp.maximum(lowest, end), lowest)
        first_lowest = jnp.where(query_start >= end, jnp.maximum(first_lowest, end), first_lowest)
    needed = (key_start >= 0) & (key_start + keys - 1 >= first_lowest)

    @pl.when(needed)
    def _():
        q_scr[pl.ds(mine, block), :] = q_mine[...]
        q_scr[pl.ds(other, block), :] = q_other[...]
        g_scr[pl.ds(mine, block), :] = g_mine[...]
        g_scr[pl.ds(other, block), :] = g_other[...]
        stats_scr[:, pl.ds(pl.multiple_of(mine, 128), block)] = stats_mine[0]
        stats_scr[:, pl.ds(pl.multiple_of(other, 128), block)] = stats_other[0]
        k_positions = key_start + lax.broadcasted_iota(jnp.int32, (keys, 2 * block), 0)
        allowed = (k_positions >= lowest) & (k_positions <= q_positions)
        k = kv_ref[:, :HEAD_WIDTH]
        v = kv_ref[:, HEAD_WIDTH:]
        k_t = k.T
        dk = jnp.zeros((keys, HEAD_WIDTH), jnp.float32)
        dv = jnp.zeros((keys, HEAD_WIDTH), jnp.float32)
        nt = (((1,), (1,)), ((), ()))
        for r in range(per_group):
            cols = slice(r * HEAD_WIDTH, (r + 1) * HEAD_WIDTH)
            q = q_scr[:, cols]
            g = g_scr[:, cols]
            scores = lax.dot_general(k, q, nt, preferred_element_type=jnp.float32)
            weights = jnp.where(
                allowed, jnp.exp2(scores * (SCALE * LOG2E) - stats_scr[r : r + 1, :]), 0.0
            )
            dv = dv + jnp.dot(weights.astype(jnp.bfloat16), g, preferred_element_type=jnp.float32)
            through = lax.dot_general(v, g, nt, preferred_element_type=jnp.float32)
            ds = (weights * (through - stats_scr[8 + r : 9 + r, :])).astype(jnp.bfloat16)
            dk = dk + jnp.dot(ds, q, preferred_element_type=jnp.float32)
            dq = jnp.dot(k_t, ds, preferred_element_type=jnp.float32)
            if has_sum:
                dq = dq + sum_ref[r]
            if last:
                dq_scr[r] = dq
            else:
                dq_ref[r] = dq
        dkv_ref[:, :HEAD_WIDTH] = (dk * SCALE).astype(dkv_ref.dtype)
        dkv_ref[:, HEAD_WIDTH:] = dv.astype(dkv_ref.dtype)

    @pl.when(jnp.logical_not(needed))
    def _():
        dkv_ref[...] = jnp.zeros_like(dkv_ref)
        target = dq_scr if last else dq_ref
        target[...] = sum_ref[...] if has_sum else jnp.zeros_like(target)

    if last:
        for r in range(per_group):
            dq_ref[:, r * HEAD_WIDTH : (r + 1) * HEAD_WIDTH] = (dq_scr[r].T * SCALE).astype(dq_ref.dtype)


def tile_call(distance, row_start, place, lengths, queries, kv, dq_sum, last, dkv_type):
    q, q_other, g, stats, stats_other = queries
    block = q.shape[0]
    keys = kv.shape[0]
    per_group = q.shape[1] // HEAD_WIDTH // KEY_VALUE_HEADS
    width = per_group * HEAD_WIDTH
    in_specs = [
        pl.BlockSpec(memory_space=pltpu.SMEM),
        pl.BlockSpec((block, width), lambda i, p: (0, lax.rem(p[0], 2) * HALF + i)),
        pl.BlockSpec((block, width), lambda i, p: (0, i)),
        pl.BlockSpec((block, width), lambda i, p: (0, lax.rem(p[0], 2) * HALF + i)),
        pl.BlockSpec((block, width), lambda i, p: (0, HALF + i)),
        pl.BlockSpec((1, 16, block), lambda i, p: (lax.rem(p[0], 2) * HALF + i, 0, 0)),
        pl.BlockSpec((1, 16, block), lambda i, p: (i, 0, 0)),
        pl.BlockSpec((keys, 2 * HEAD_WIDTH), lambda i, p: (0, i)),
    ]
    args = [lengths, q, q_other, g, q_other, stats, stats_other, kv]
    sum_spec = pl.BlockSpec((per_group, HEAD_WIDTH, 2 * block), lambda i, p: (i, 0, 0))
    if dq_sum is not None:
        in_specs.append(sum_spec)
        args.append(dq_sum)
    if last:
        dq_shape = jax.ShapeDtypeStruct((2 * block, HALF * width), jnp.bfloat16)
        dq_spec = pl.BlockSpec((2 * block, width), lambda i, p: (0, i))
    else:
        dq_shape = jax.ShapeDtypeStruct((HALF * per_group, HEAD_WIDTH, 2 * block), jnp.float32)
        dq_spec = sum_spec
    config = (per_group, distance, row_start, dq_sum is not None, last)
    pairs = HALF * per_group * keys * 2 * block
    return pl.pallas_call(
        functools.partial(tile_kernel, config),
        grid_spec=pltpu.PrefetchScalarGridSpec(
            num_scalar_prefetch=1,
            grid=(HALF,),
            in_specs=in_specs,
            out_specs=[pl.BlockSpec((keys, 2 * HEAD_WIDTH), lambda i, p: (0, i)), dq_spec],
            scratch_shapes=[
                pltpu.VMEM((2 * block, width), jnp.bfloat16),
                pltpu.VMEM((2 * block, width), jnp.bfloat16),
                pltpu.VMEM((16, 2 * block), jnp.float32),
                pltpu.VMEM((per_group, HEAD_WIDTH, 2 * block), jnp.float32),
            ],
        ),
        out_shape=[jax.ShapeDtypeStruct((keys, HALF * 2 * HEAD_WIDTH), dkv_type), dq_shape],
        compiler_params=pltpu.CompilerParams(vmem_limit_bytes=32 * 1024 * 1024),
        cost_estimate=pl.CostEstimate(
            flops=10 * pairs * HEAD_WIDTH, bytes_accessed=8 << 20, transcendentals=pairs
        ),
    )(place, *args)


def body(q, k, v, outputs, grad, norms, lengths):
    block = q.shape[0]
    heads = norms.shape[0]
    per_group = heads // KEY_VALUE_HEADS
    width = per_group * HEAD_WIDTH
    devices = lax.axis_size("ctx")
    index = lax.axis_index("ctx").astype(jnp.int32)
    core = lax.rem(index, 2)
    place = index.reshape(1)
    to_partner = partner_pairs(devices)
    reach = -(-(WINDOW - 1) // block)
    farthest = (reach + 1) // 2

    def half(array, which):
        size = array.shape[1] // 2
        return lax.dynamic_slice_in_dim(array, which * size, size, 1)

    def key_half(which):
        k_half, v_half = half(k, which), half(v, which)
        pieces = []
        for g in range(HALF):
            cols = slice(g * HEAD_WIDTH, (g + 1) * HEAD_WIDTH)
            pieces += [k_half[:, cols], v_half[:, cols]]
        return jnp.concatenate(pieces, axis=1)

    kv_mine = key_half(core)
    kv_other = lax.ppermute(key_half(1 - core), "ctx", to_partner)
    kv = jnp.concatenate(
        [jnp.where(core == 0, kv_mine, kv_other), jnp.where(core == 0, kv_other, kv_mine)], axis=0
    )
    q_other = lax.ppermute(
        jnp.concatenate([half(q, 1 - core), half(grad, 1 - core)], axis=1), "ctx", to_partner
    )
    arrived = {}
    for distance in range(1, farthest + 1):
        rows = block if distance == farthest and reach % 2 else 0
        arrived[distance] = lax.ppermute(kv[rows:], "ctx", shift_pairs(devices, distance))

    stats = pl.pallas_call(
        functools.partial(stats_kernel, per_group),
        grid=(KEY_VALUE_HEADS,),
        in_specs=[
            pl.BlockSpec((block, width), lambda i: (0, i)),
            pl.BlockSpec((block, width), lambda i: (0, i)),
            pl.BlockSpec((heads, block), lambda i: (0, 0)),
        ],
        out_specs=pl.BlockSpec((1, 16, block), lambda i: (i, 0, 0)),
        out_shape=jax.ShapeDtypeStruct((KEY_VALUE_HEADS, 16, block), jnp.float32),
    )(outputs, grad, norms)
    stats_other = lax.ppermute(
        lax.dynamic_slice_in_dim(stats, (1 - core) * HALF, HALF, 0), "ctx", to_partner
    )
    queries = (q, q_other, grad, stats, stats_other)

    total, dq_sum = tile_call(0, 0, place, lengths, queries, kv, None, False, jnp.float32)
    for distance in range(1, farthest + 1):
        part = arrived[distance]
        rows = 2 * block - part.shape[0]
        dkv, dq_sum = tile_call(
            distance, rows, place, lengths, queries, part, dq_sum, distance == farthest, jnp.bfloat16
        )
        back = lax.ppermute(dkv, "ctx", shift_pairs(devices, -distance)).astype(jnp.float32)
        if rows:
            back = jnp.concatenate([jnp.zeros((rows, back.shape[1]), jnp.float32), back], axis=0)
        total = total + back

    dq = dq_sum
    dq_keep = lax.dynamic_slice_in_dim(dq, core * block, block, 0)
    dq_got = lax.ppermute(
        lax.dynamic_slice_in_dim(dq, (1 - core) * block, block, 0), "ctx", to_partner
    )
    query_grad = jnp.concatenate(
        [jnp.where(core == 0, dq_keep, dq_got), jnp.where(core == 0, dq_got, dq_keep)], axis=1
    )
    total = total.astype(jnp.bfloat16)
    keep = lax.dynamic_slice_in_dim(total, core * block, block, 0)
    got = lax.ppermute(
        lax.dynamic_slice_in_dim(total, (1 - core) * block, block, 0), "ctx", to_partner
    )
    low, high = jnp.where(core == 0, keep, got), jnp.where(core == 0, got, keep)
    pieces = [
        part[:, i * HEAD_WIDTH : (i + 1) * HEAD_WIDTH] for part in (low, high) for i in range(2 * HALF)
    ]
    return query_grad, jnp.concatenate(pieces[0::2], axis=1), jnp.concatenate(pieces[1::2], axis=1)


def solution(mesh):
    rows = P(("groups", "ctx"), None)
    return jax.shard_map(
        body,
        mesh=mesh,
        in_specs=(rows, rows, rows, rows, rows, P(None, ("groups", "ctx")), P("groups")),
        out_specs=(rows, rows, rows),
        check_vma=False,
    )
```

```python
import functools
import math

import jax
import jax.numpy as jnp
from jax import lax
from jax.experimental import pallas as pl
from jax.experimental.pallas import tpu as pltpu
from jax.sharding import PartitionSpec as P

HEAD_WIDTH = 128
KEY_VALUE_HEADS = 4
WINDOW = 896
SCALE = HEAD_WIDTH ** (-0.5)
LOG2E = math.log2(math.e)
HALF = KEY_VALUE_HEADS // 2

ANY = pl.BlockSpec(memory_space=pl.ANY)
VMEM = pl.BlockSpec(memory_space=pltpu.VMEM)
SMEM = pl.BlockSpec(memory_space=pltpu.SMEM)
NT = (((1,), (1,)), ((), ()))
NN = (((1,), (0,)), ((), ()))


def dot(a, b, dims):
    return lax.dot_general(a, b, dims, preferred_element_type=jnp.float32)


def shift_pairs(devices, chips):
    first, last = max(0, -2 * chips), min(devices, devices - 2 * chips)
    return [(source, source + 2 * chips) for source in range(first, last)]


def partner_pairs(devices):
    return [(source, source ^ 1) for source in range(devices)]


def lanes(start, size):
    return pl.ds(pl.multiple_of(start, 128), size)


def weight(cost):
    return pl.CostEstimate(flops=1000 + 1000000000 * cost, bytes_accessed=1000 + 3690000 * cost, transcendentals=0)


def small_call(kernel, out_shape, in_specs, out_specs, scratch, cost=0, vmem=8):
    return pl.pallas_call(
        kernel,
        out_shape=out_shape,
        in_specs=in_specs,
        out_specs=out_specs,
        scratch_shapes=scratch,
        compiler_params=pltpu.CompilerParams(vmem_limit_bytes=vmem * 1024 * 1024),
        cost_estimate=weight(cost),
    )


def run_copies(pairs, sems):
    copies = [pltpu.make_async_copy(a, b, sems.at[i]) for i, (a, b) in enumerate(pairs)]
    for copy in copies:
        copy.start()
    for copy in copies:
        copy.wait()


def pack_keys_kernel(place, k, v, keep, send, sems):
    core = lax.rem(place[0], 2)
    pairs = []
    for target, which in ((send, 1 - core), (keep, core)):
        for g in range(HALF):
            source = lanes((which * HALF + g) * HEAD_WIDTH, HEAD_WIDTH)
            pairs.append((k.at[:, source], target.at[:, pl.ds(2 * g * HEAD_WIDTH, HEAD_WIDTH)]))
            pairs.append((v.at[:, source], target.at[:, pl.ds((2 * g + 1) * HEAD_WIDTH, HEAD_WIDTH)]))
    run_copies(pairs, sems)


def join_keys_kernel(place, keep, other, joined, sems):
    core = lax.rem(place[0], 2)
    block = keep.shape[0]
    run_copies(
        [
            (keep, joined.at[pl.ds(pl.multiple_of(core * block, 128), block), :]),
            (other, joined.at[pl.ds(pl.multiple_of((1 - core) * block, 128), block), :]),
        ],
        sems,
    )


def pack_queries_kernel(place, q, grad, send, sems):
    core = lax.rem(place[0], 2)
    size = q.shape[1] // 2
    source = lanes((1 - core) * size, size)
    run_copies(
        [
            (q.at[:, source], send.at[:, pl.ds(0, size)]),
            (grad.at[:, source], send.at[:, pl.ds(size, size)]),
        ],
        sems,
    )


def stats_kernel(per_group, outputs, grad, norms, stats):
    ones = jnp.ones((8, 2 * HEAD_WIDTH), jnp.bfloat16)
    stats[...] = jnp.zeros_like(stats)
    for group in range(KEY_VALUE_HEADS):
        for r in range(per_group):
            head = group * per_group + r
            cols = slice(head * HEAD_WIDTH, (head + 1) * HEAD_WIDTH)
            product = outputs[:, cols].astype(jnp.float32) * grad[:, cols].astype(jnp.float32)
            high = product.astype(jnp.bfloat16)
            low = (product - high.astype(jnp.float32)).astype(jnp.bfloat16)
            delta = dot(ones, jnp.concatenate([high, low], axis=1), NT)
            stats[group, 8 + r : 9 + r, :] = delta[0:1, :]
            stats[group, r : r + 1, :] = norms[head : head + 1, :] * LOG2E


def tile(distance, row_start, query_rows, add, place, lengths, queries, stats, kv, dkv, dq):
    per_group = queries.shape[1] // 2 // HALF // HEAD_WIDTH
    width = per_group * HEAD_WIDTH
    tokens = queries.shape[0]
    keys = kv.shape[0]
    query_start = lax.div(place[0], 2) * tokens
    key_start = query_start - distance * tokens + row_start

    q_positions = query_start + lax.broadcasted_iota(jnp.int32, (1, query_rows), 1)
    lowest = jnp.maximum(q_positions - (WINDOW - 1), 0)
    first_lowest = jnp.maximum(query_start - (WINDOW - 1), 0)
    end = jnp.int32(0)
    for i in range(lengths.shape[0]):
        end = end + lengths[i]
        lowest = jnp.where(q_positions >= end, jnp.maximum(lowest, end), lowest)
        first_lowest = jnp.where(query_start >= end, jnp.maximum(first_lowest, end), first_lowest)
    needed = (key_start >= 0) & (key_start + keys - 1 >= first_lowest)

    @pl.when(needed)
    def _():
        k_positions = key_start + lax.broadcasted_iota(jnp.int32, (keys, query_rows), 0)
        allowed = (k_positions >= lowest) & (k_positions <= q_positions)
        allowed = jnp.concatenate([allowed] * per_group, axis=1)

        def group(g, carry):
            k = kv[:, lanes(2 * g * HEAD_WIDTH, HEAD_WIDTH)]
            v = kv[:, lanes((2 * g + 1) * HEAD_WIDTH, HEAD_WIDTH)]
            first = g * width
            q = jnp.concatenate(
                [queries[:query_rows, lanes(first + r * HEAD_WIDTH, HEAD_WIDTH)] for r in range(per_group)], 0
            )
            first = first + HALF * width
            grad = jnp.concatenate(
                [queries[:query_rows, lanes(first + r * HEAD_WIDTH, HEAD_WIDTH)] for r in range(per_group)], 0
            )
            norm = jnp.concatenate([stats[g, r : r + 1, :query_rows] for r in range(per_group)], 1)
            delta = jnp.concatenate([stats[g, 8 + r : 9 + r, :query_rows] for r in range(per_group)], 1)
            scores = dot(k, q, NT)
            weights = jnp.where(allowed, jnp.exp2(scores * (SCALE * LOG2E) - norm), 0.0)
            dv = dot(weights.astype(jnp.bfloat16), grad, NN)
            through = dot(v, grad, NT)
            ds = (weights * (through - delta)).astype(jnp.bfloat16)
            dk = dot(ds, q, NN)
            part = dot(k.T, ds, NN)
            for r in range(per_group):
                cols = slice(r * tokens, r * tokens + query_rows)
                piece = part[:, r * query_rows : (r + 1) * query_rows]
                dq[g, :, cols] = dq[g, :, cols] + piece if add else piece
            dkv[:, lanes(2 * g * HEAD_WIDTH, HEAD_WIDTH)] = (dk * SCALE).astype(dkv.dtype)
            dkv[:, lanes((2 * g + 1) * HEAD_WIDTH, HEAD_WIDTH)] = dv.astype(dkv.dtype)
            return carry

        lax.fori_loop(0, HALF, group, 0)

    @pl.when(jnp.logical_not(needed))
    def _():
        dkv[...] = jnp.zeros_like(dkv)


def own_kernel(place, lengths, q, grad, other, stats_mine, stats_other, kv, dkv, dq, queries, stats):
    core = lax.rem(place[0], 2)
    block = q.shape[0]
    size = q.shape[1] // 2
    mine = pl.ds(pl.multiple_of(core * block, 128), block)
    theirs = pl.ds(pl.multiple_of((1 - core) * block, 128), block)
    half = lanes(core * size, size)
    queries[mine, :size] = q[:, half]
    queries[mine, size:] = grad[:, half]
    queries[theirs, :] = other[...]
    for g in range(HALF):
        stats[g, :, mine] = stats_mine[core * HALF + g]
        stats[g, :, theirs] = stats_other[g]
    tile(0, 0, queries.shape[0], False, place, lengths, queries, stats, kv, dkv, dq)


def far_kernel(config, place, lengths, queries, stats, kv, dq_in, dkv, dq):
    distance, row_start, query_rows = config
    tile(distance, row_start, query_rows, True, place, lengths, queries, stats, kv, dkv, dq)


def far_call(distance, row_start, query_rows, place, lengths, queries, stats, kv, dq, cost=0):
    return pl.pallas_call(
        functools.partial(far_kernel, (distance, row_start, query_rows)),
        in_specs=[SMEM, SMEM, VMEM, VMEM, VMEM, VMEM],
        out_specs=[VMEM, VMEM],
        out_shape=[jax.ShapeDtypeStruct(kv.shape, jnp.bfloat16), jax.ShapeDtypeStruct(dq.shape, dq.dtype)],
        input_output_aliases={5: 1},
        compiler_params=pltpu.CompilerParams(vmem_limit_bytes=24 * 1024 * 1024),
        cost_estimate=weight(cost),
    )(place, lengths, queries, stats, kv, dq)


def finish_queries_kernel(place, dq, total, first, second, keep, send, out):
    out[...] = total[...] + first[...].astype(jnp.float32) + second[...].astype(jnp.float32)
    core = lax.rem(place[0], 2)
    block = keep.shape[0]
    tokens = 2 * block
    per_group = keep.shape[1] // HEAD_WIDTH // HALF
    for g in range(HALF):
        for r in range(per_group):
            cols = slice((g * per_group + r) * HEAD_WIDTH, (g * per_group + r + 1) * HEAD_WIDTH)
            for target, which in ((send, 1 - core), (keep, core)):
                start = r * tokens + which * block
                piece = (dq[g, :, lanes(start, block)] * SCALE).astype(jnp.bfloat16)
                target[:, cols] = piece.T


def join_queries_kernel(place, keep, other, joined, sems):
    core = lax.rem(place[0], 2)
    size = keep.shape[1]
    run_copies(
        [(keep, joined.at[:, lanes(core * size, size)]), (other, joined.at[:, lanes((1 - core) * size, size)])],
        sems,
    )


def last_sum_kernel(place, total, third, fourth, keep, send):
    core = lax.rem(place[0], 2)
    block = keep.shape[0]
    rows = total.shape[0] - fourth.shape[0]
    for target, which in ((send, 1 - core), (keep, core)):
        part = pl.ds(pl.multiple_of(which * block, 128), block)
        value = total[part, :] + third[part, :].astype(jnp.float32)
        if rows:
            late = jnp.where(which == 1, fourth[...].astype(jnp.float32), 0.0)
        else:
            late = fourth[part, :].astype(jnp.float32)
        target[...] = (value + late).astype(jnp.bfloat16)


def join_grads_kernel(place, keep, other, key_grad, value_grad):
    core = lax.rem(place[0], 2)
    for source, which in ((keep, core), (other, 1 - core)):
        for g in range(HALF):
            target = lanes((which * HALF + g) * HEAD_WIDTH, HEAD_WIDTH)
            key_grad[:, target] = source[:, 2 * g * HEAD_WIDTH : (2 * g + 1) * HEAD_WIDTH]
            value_grad[:, target] = source[:, (2 * g + 1) * HEAD_WIDTH : (2 * g + 2) * HEAD_WIDTH]


def body(q, k, v, outputs, grad, norms, lengths):
    block = q.shape[0]
    tokens = 2 * block
    heads = norms.shape[0]
    per_group = heads // KEY_VALUE_HEADS
    width = per_group * HEAD_WIDTH
    devices = lax.axis_size("ctx")
    place = lax.axis_index("ctx").astype(jnp.int32).reshape(1)
    to_partner = partner_pairs(devices)
    assert -(-(WINDOW - 1) // block) == 7, "window"

    def bf16(*shape):
        return jax.ShapeDtypeStruct(shape, jnp.bfloat16)

    def f32(*shape):
        return jax.ShapeDtypeStruct(shape, jnp.float32)

    def move(array, chips):
        return lax.ppermute(array, "ctx", shift_pairs(devices, chips))

    def swap(array):
        return lax.ppermute(array, "ctx", to_partner)

    dma = pltpu.SemaphoreType.DMA
    kv_width = HALF * 2 * HEAD_WIDTH
    kv_keep, kv_send = small_call(
        pack_keys_kernel,
        [bf16(block, kv_width)] * 2,
        [SMEM, ANY, ANY],
        [ANY, ANY],
        [dma((4 * HALF,))],
    )(place, k, v)
    kv_other = swap(kv_send)
    later, kv_keep = lax.optimization_barrier((place, kv_keep))
    q_send = small_call(
        pack_queries_kernel, bf16(block, q.shape[1]), [SMEM, ANY, ANY], ANY, [dma((2,))]
    )(later, q, grad)
    q_other = swap(q_send)
    kv = small_call(
        join_keys_kernel, bf16(tokens, kv_width), [SMEM, ANY, ANY], ANY, [dma((2,))]
    )(place, kv_keep, kv_other)
    kv2 = move(kv, 2)
    kv1 = move(kv, 1)

    stats_mine = small_call(
        functools.partial(stats_kernel, per_group),
        f32(KEY_VALUE_HEADS, 16, block),
        [VMEM, VMEM, VMEM],
        VMEM,
        [],
    )(outputs, grad, norms)
    core = lax.rem(place[0], 2)
    stats_other = swap(lax.dynamic_slice_in_dim(stats_mine, (1 - core) * HALF, HALF, 0))

    total, dq, queries, stats = pl.pallas_call(
        own_kernel,
        in_specs=[SMEM, SMEM] + [VMEM] * 6,
        out_specs=[VMEM] * 4,
        out_shape=[
            f32(tokens, kv_width),
            f32(HALF, HEAD_WIDTH, per_group * tokens),
            bf16(tokens, q.shape[1]),
            f32(HALF, 16, tokens),
        ],
        compiler_params=pltpu.CompilerParams(vmem_limit_bytes=24 * 1024 * 1024),
        cost_estimate=weight(0),
    )(place, lengths, q, grad, q_other, stats_mine, stats_other, kv)

    kv2, total = lax.optimization_barrier((kv2, total))
    kv3 = move(kv2, 1)
    kv4 = move(kv2[block:], 2)
    far = functools.partial(far_call, place=place, lengths=lengths, queries=queries, stats=stats)
    part2, dq = far(2, 0, tokens, kv=kv2, dq=dq)
    back2 = move(part2, -2)
    part1, dq = far(1, 0, tokens, kv=kv1, dq=dq)
    back1 = move(part1, -1)
    part3, dq = far(3, 0, tokens, kv=kv3, dq=dq)
    back3 = move(part3, -3)
    part4, dq = far(4, block, block, kv=kv4, dq=dq, cost=10)
    back4 = move(part4, -4)

    dq_keep, dq_send, total = small_call(
        finish_queries_kernel,
        [bf16(block, HALF * width)] * 2 + [f32(tokens, kv_width)],
        [SMEM] + [VMEM] * 4,
        [VMEM] * 3,
        [],
    )(place, dq, total, back2, back1)
    dq_other = swap(dq_send)
    query_grad = small_call(
        join_queries_kernel, bf16(block, q.shape[1]), [SMEM, ANY, ANY], ANY, [dma((2,))]
    )(place, dq_keep, dq_other)

    keep, send = small_call(
        last_sum_kernel, [bf16(block, kv_width)] * 2, [SMEM] + [VMEM] * 3, [VMEM, VMEM], [], 20
    )(place, total, back3, back4)
    key_grad, value_grad = small_call(
        join_grads_kernel, [bf16(block, kv_width)] * 2, [SMEM, VMEM, VMEM], [VMEM, VMEM], []
    )(place, keep, swap(send))
    return query_grad, key_grad, value_grad


def solution(mesh):
    rows = P(("groups", "ctx"), None)
    return jax.shard_map(
        body,
        mesh=mesh,
        in_specs=(rows, rows, rows, rows, rows, P(None, ("groups", "ctx")), P("groups")),
        out_specs=(rows, rows, rows),
        check_vma=False,
    )
```

```python
import functools
import math

import jax
import jax.numpy as jnp
from jax import lax
from jax.experimental import pallas as pl
from jax.experimental.pallas import tpu as pltpu
from jax.sharding import PartitionSpec as P

HEAD_WIDTH = 128
KEY_VALUE_HEADS = 4
WINDOW = 896
SCALE = HEAD_WIDTH ** (-0.5)
LOG2E = math.log2(math.e)
HALF = KEY_VALUE_HEADS // 2

ANY = pl.BlockSpec(memory_space=pl.ANY)
VMEM = pl.BlockSpec(memory_space=pltpu.VMEM)
SMEM = pl.BlockSpec(memory_space=pltpu.SMEM)
HBM = pl.BlockSpec(memory_space=pltpu.HBM)
NT = (((1,), (1,)), ((), ()))
NN = (((1,), (0,)), ((), ()))


def dot(a, b, dims):
    return lax.dot_general(a, b, dims, preferred_element_type=jnp.float32)


def shift_pairs(devices, chips):
    first, last = max(0, -2 * chips), min(devices, devices - 2 * chips)
    return [(source, source + 2 * chips) for source in range(first, last)]


def pair_pairs(devices):
    return [(source, source ^ 2) for source in range(devices)]


def partner_pairs(devices):
    return [(source, source ^ 1) for source in range(devices)]


def lanes(start, size):
    return pl.ds(pl.multiple_of(start, 128), size)


def weight(cost):
    return pl.CostEstimate(flops=1000 + 1000000000 * cost, bytes_accessed=1000 + 3690000 * cost, transcendentals=0)


def small_call(kernel, out_shape, in_specs, out_specs, scratch, cost=0, vmem=8):
    return pl.pallas_call(
        kernel,
        out_shape=out_shape,
        in_specs=in_specs,
        out_specs=out_specs,
        scratch_shapes=scratch,
        compiler_params=pltpu.CompilerParams(vmem_limit_bytes=vmem * 1024 * 1024),
        cost_estimate=weight(cost),
    )


def run_copies(pairs, sems):
    copies = [pltpu.make_async_copy(a, b, sems.at[i]) for i, (a, b) in enumerate(pairs)]
    for copy in copies:
        copy.start()
    for copy in copies:
        copy.wait()


def pack_kernel(place, k, v, q, grad, keep, send, q_send, sems):
    core = lax.rem(place[0], 2)
    pairs = []
    for target, which in ((send, 1 - core), (keep, core)):
        for g in range(HALF):
            source = lanes((which * HALF + g) * HEAD_WIDTH, HEAD_WIDTH)
            pairs.append((k.at[:, source], target.at[:, pl.ds(2 * g * HEAD_WIDTH, HEAD_WIDTH)]))
            pairs.append((v.at[:, source], target.at[:, pl.ds((2 * g + 1) * HEAD_WIDTH, HEAD_WIDTH)]))
    size = q.shape[1] // 2
    source = lanes((1 - core) * size, size)
    pairs.append((q.at[:, source], q_send.at[:, pl.ds(0, size)]))
    pairs.append((grad.at[:, source], q_send.at[:, pl.ds(size, size)]))
    run_copies(pairs, sems)


def join_keys_kernel(place, keep, other, joined, sems):
    core = lax.rem(place[0], 2)
    block = keep.shape[0]
    run_copies(
        [
            (keep, joined.at[pl.ds(pl.multiple_of(core * block, 128), block), :]),
            (other, joined.at[pl.ds(pl.multiple_of((1 - core) * block, 128), block), :]),
        ],
        sems,
    )


def stats_kernel(per_group, outputs, grad, norms, stats):
    ones = jnp.ones((8, 2 * HEAD_WIDTH), jnp.bfloat16)
    stats[...] = jnp.zeros_like(stats)
    for group in range(KEY_VALUE_HEADS):
        for r in range(per_group):
            head = group * per_group + r
            cols = slice(head * HEAD_WIDTH, (head + 1) * HEAD_WIDTH)
            product = outputs[:, cols].astype(jnp.float32) * grad[:, cols].astype(jnp.float32)
            high = product.astype(jnp.bfloat16)
            low = (product - high.astype(jnp.float32)).astype(jnp.bfloat16)
            delta = dot(ones, jnp.concatenate([high, low], axis=1), NT)
            stats[group, 8 + r : 9 + r, :] = delta[0:1, :]
            stats[group, r : r + 1, :] = norms[head : head + 1, :] * LOG2E


def tile(distance, row_start, query_rows, add, place, lengths, queries, stats, kv, dkv, dq):
    per_group = queries.shape[1] // 2 // HALF // HEAD_WIDTH
    width = per_group * HEAD_WIDTH
    tokens = queries.shape[0]
    keys = kv.shape[0]
    query_start = lax.div(place[0], 2) * tokens
    key_start = query_start - distance * tokens + row_start

    q_positions = query_start + lax.broadcasted_iota(jnp.int32, (1, query_rows), 1)
    lowest = jnp.maximum(q_positions - (WINDOW - 1), 0)
    first_lowest = jnp.maximum(query_start - (WINDOW - 1), 0)
    end = jnp.int32(0)
    for i in range(lengths.shape[0]):
        end = end + lengths[i]
        lowest = jnp.where(q_positions >= end, jnp.maximum(lowest, end), lowest)
        first_lowest = jnp.where(query_start >= end, jnp.maximum(first_lowest, end), first_lowest)
    needed = (key_start >= 0) & (key_start + keys - 1 >= first_lowest)

    @pl.when(needed)
    def _():
        k_positions = key_start + lax.broadcasted_iota(jnp.int32, (keys, query_rows), 0)
        allowed = (k_positions >= lowest) & (k_positions <= q_positions)
        allowed = jnp.concatenate([allowed] * per_group, axis=1)

        def group(g, carry):
            k = kv[:, lanes(2 * g * HEAD_WIDTH, HEAD_WIDTH)]
            v = kv[:, lanes((2 * g + 1) * HEAD_WIDTH, HEAD_WIDTH)]
            first = g * width
            q = jnp.concatenate(
                [queries[:query_rows, lanes(first + r * HEAD_WIDTH, HEAD_WIDTH)] for r in range(per_group)], 0
            )
            first = first + HALF * width
            grad = jnp.concatenate(
                [queries[:query_rows, lanes(first + r * HEAD_WIDTH, HEAD_WIDTH)] for r in range(per_group)], 0
            )
            norm = jnp.concatenate([stats[g, r : r + 1, :query_rows] for r in range(per_group)], 1)
            delta = jnp.concatenate([stats[g, 8 + r : 9 + r, :query_rows] for r in range(per_group)], 1)
            scores = dot(k, q, NT)
            weights = jnp.where(allowed, jnp.exp2(scores * (SCALE * LOG2E) - norm), 0.0)
            dv = dot(weights.astype(jnp.bfloat16), grad, NN)
            through = dot(v, grad, NT)
            ds = (weights * (through - delta)).astype(jnp.bfloat16)
            dk = dot(ds, q, NN)
            part = dot(k.T, ds, NN)
            for r in range(per_group):
                cols = slice(r * tokens, r * tokens + query_rows)
                piece = part[:, r * query_rows : (r + 1) * query_rows]
                dq[g, :, cols] = dq[g, :, cols] + piece if add else piece
            dkv[:, lanes(2 * g * HEAD_WIDTH, HEAD_WIDTH)] = (dk * SCALE).astype(dkv.dtype)
            dkv[:, lanes((2 * g + 1) * HEAD_WIDTH, HEAD_WIDTH)] = dv.astype(dkv.dtype)
            return carry

        lax.fori_loop(0, HALF, group, 0)

    @pl.when(jnp.logical_not(needed))
    def _():
        dkv[...] = jnp.zeros_like(dkv)
        if not add:
            dq[...] = jnp.zeros_like(dq)


def join_queries_in_kernel(place, q, grad, other, stats_mine, stats_other, queries, stats):
    core = lax.rem(place[0], 2)
    block = q.shape[0]
    size = q.shape[1] // 2
    mine = pl.ds(pl.multiple_of(core * block, 128), block)
    theirs = pl.ds(pl.multiple_of((1 - core) * block, 128), block)
    half = lanes(core * size, size)
    queries[mine, :size] = q[:, half]
    queries[mine, size:] = grad[:, half]
    queries[theirs, :] = other[...]
    for g in range(HALF):
        stats[g, :, mine] = stats_mine[core * HALF + g]
        stats[g, :, theirs] = stats_other[g]


def tile_kernel(config, *refs):
    distance, row_start, query_rows, add = config
    place, lengths, queries, stats, kv = refs[:5]
    dkv, dq = refs[-2:]
    tile(distance, row_start, query_rows, add, place, lengths, queries, stats, kv, dkv, dq)


def tile_call(distance, row_start, query_rows, place, lengths, queries, stats, kv, dq, kind=jnp.bfloat16, cost=0):
    add = dq is not None
    tokens, columns = queries.shape
    shape = (HALF, HEAD_WIDTH, columns // 2 // HALF // HEAD_WIDTH * tokens)
    return pl.pallas_call(
        functools.partial(tile_kernel, (distance, row_start, query_rows, add)),
        in_specs=[SMEM, SMEM] + [VMEM] * (4 if add else 3),
        out_specs=[VMEM, VMEM],
        out_shape=[jax.ShapeDtypeStruct(kv.shape, kind), jax.ShapeDtypeStruct(shape, jnp.float32)],
        input_output_aliases={5: 1} if add else {},
        compiler_params=pltpu.CompilerParams(vmem_limit_bytes=24 * 1024 * 1024),
        cost_estimate=weight(cost),
    )(place, lengths, queries, stats, kv, *([dq] if add else []))


def pass_on_kernel(place, second, swapped, third, fourth, out):
    odd = lax.rem(lax.div(place[0], 2), 2) == 1
    rows = second.shape[0] - fourth.shape[0]
    for part in (slice(0, rows), slice(rows, None)):
        value = second[part, :] + third[part, :].astype(jnp.float32)
        value = value + jnp.where(odd, swapped[part, :].astype(jnp.float32), 0.0)
        if part.start:
            value = value + fourth[...].astype(jnp.float32)
        out[part, :] = value.astype(out.dtype)


def finish_queries_kernel(place, dq, keep, send):
    core = lax.rem(place[0], 2)
    block = keep.shape[0]
    tokens = 2 * block
    per_group = keep.shape[1] // HEAD_WIDTH // HALF
    for g in range(HALF):
        for r in range(per_group):
            cols = slice((g * per_group + r) * HEAD_WIDTH, (g * per_group + r + 1) * HEAD_WIDTH)
            for target, which in ((send, 1 - core), (keep, core)):
                start = r * tokens + which * block
                piece = (dq[g, :, lanes(start, block)] * SCALE).astype(jnp.bfloat16)
                target[:, cols] = piece.T


def join_queries_kernel(place, keep, other, joined, sems):
    core = lax.rem(place[0], 2)
    size = keep.shape[1]
    run_copies(
        [(keep, joined.at[:, lanes(core * size, size)]), (other, joined.at[:, lanes((1 - core) * size, size)])],
        sems,
    )


def last_sum_kernel(place, total, swapped, home, keep, send):
    core = lax.rem(place[0], 2)
    even = lax.rem(lax.div(place[0], 2), 2) == 0
    block = keep.shape[0]
    for target, which in ((send, 1 - core), (keep, core)):
        part = pl.ds(pl.multiple_of(which * block, 128), block)
        value = total[part, :] + home[part, :].astype(jnp.float32)
        value = value + jnp.where(even, swapped[part, :].astype(jnp.float32), 0.0)
        target[...] = value.astype(jnp.bfloat16)


def join_grads_kernel(place, keep, other, key_grad, value_grad):
    core = lax.rem(place[0], 2)
    for source, which in ((keep, core), (other, 1 - core)):
        for g in range(HALF):
            target = lanes((which * HALF + g) * HEAD_WIDTH, HEAD_WIDTH)
            key_grad[:, target] = source[:, 2 * g * HEAD_WIDTH : (2 * g + 1) * HEAD_WIDTH]
            value_grad[:, target] = source[:, (2 * g + 1) * HEAD_WIDTH : (2 * g + 2) * HEAD_WIDTH]


def body(q, k, v, outputs, grad, norms, lengths):
    block = q.shape[0]
    tokens = 2 * block
    heads = norms.shape[0]
    per_group = heads // KEY_VALUE_HEADS
    width = per_group * HEAD_WIDTH
    devices = lax.axis_size("ctx")
    place = lax.axis_index("ctx").astype(jnp.int32).reshape(1)
    to_partner = partner_pairs(devices)
    assert -(-(WINDOW - 1) // block) == 7, "window"

    def bf16(*shape):
        return jax.ShapeDtypeStruct(shape, jnp.bfloat16)

    def f32(*shape):
        return jax.ShapeDtypeStruct(shape, jnp.float32)

    def move(array, chips):
        return lax.ppermute(array, "ctx", shift_pairs(devices, chips))

    def swap(array):
        return lax.ppermute(array, "ctx", to_partner)

    dma = pltpu.SemaphoreType.DMA
    kv_width = HALF * 2 * HEAD_WIDTH
    kv_keep, kv_send, q_send = small_call(
        pack_kernel,
        [bf16(block, kv_width)] * 2 + [bf16(block, q.shape[1])],
        [SMEM] + [HBM] * 4,
        [VMEM] * 3,
        [dma((4 * HALF + 2,))],
        vmem=60,
    )(place, k, v, q, grad)
    kv = small_call(
        join_keys_kernel, bf16(tokens, kv_width), [SMEM, VMEM, VMEM], VMEM, [dma((2,))]
    )(place, kv_keep, swap(kv_send))
    kv2 = move(kv, 2)
    kv1 = move(kv, 1)

    norms, kv = lax.optimization_barrier((norms, kv))
    stats_mine = small_call(
        functools.partial(stats_kernel, per_group),
        f32(KEY_VALUE_HEADS, 16, block),
        [VMEM, VMEM, VMEM],
        VMEM,
        [],
    )(outputs, grad, norms)
    q_other = swap(q_send)
    core = lax.rem(place[0], 2)
    stats_other = swap(lax.dynamic_slice_in_dim(stats_mine, (1 - core) * HALF, HALF, 0))

    kv2, stats_mine = lax.optimization_barrier((kv2, stats_mine))
    kv3 = move(kv2, 1)
    kv4 = move(kv2[block:], 2)
    later, kv2 = lax.optimization_barrier((place, kv2))
    queries, stats = small_call(
        join_queries_in_kernel,
        [bf16(tokens, q.shape[1]), f32(HALF, 16, tokens)],
        [SMEM] + [VMEM] * 5,
        [VMEM] * 2,
        [],
    )(later, q, grad, q_other, stats_mine, stats_other)
    far = functools.partial(tile_call, place=place, lengths=lengths, queries=queries, stats=stats)
    part1, dq = far(1, 0, tokens, kv=kv1, dq=None)
    swapped = lax.ppermute(part1, "ctx", pair_pairs(devices))
    kv3, kv4 = lax.optimization_barrier((kv3, kv4))
    part3, dq = far(3, 0, tokens, kv=kv3, dq=dq)
    part3 = move(part3, -1)
    part4, dq = far(4, block, block, kv=kv4, dq=dq)
    part4 = move(part4, -2)
    part2, dq = far(2, 0, tokens, kv=kv2, dq=dq, kind=jnp.float32)
    kv, swapped = lax.optimization_barrier((kv, swapped))
    total, dq = far(0, 0, tokens, kv=kv, dq=dq, kind=jnp.float32)
    part2, total = lax.optimization_barrier((part2, total))
    part2 = small_call(
        pass_on_kernel, bf16(tokens, kv_width), [SMEM] + [VMEM] * 4, VMEM, []
    )(place, part2, swapped, part3, part4)
    home = move(part2, -2)

    dq_keep, dq_send = small_call(
        finish_queries_kernel, [bf16(block, HALF * width)] * 2, [SMEM, VMEM], [VMEM, VMEM], []
    )(place, dq)
    dq_other = swap(dq_send)
    query_grad = small_call(
        join_queries_kernel, bf16(block, q.shape[1]), [SMEM, ANY, ANY], ANY, [dma((2,))]
    )(place, dq_keep, dq_other)

    keep, send = small_call(
        last_sum_kernel, [bf16(block, kv_width)] * 2, [SMEM] + [VMEM] * 3, [VMEM, VMEM], [], 20
    )(place, total, swapped, home)
    key_grad, value_grad = small_call(
        join_grads_kernel, [bf16(block, kv_width)] * 2, [SMEM, VMEM, VMEM], [VMEM, VMEM], []
    )(place, keep, swap(send))
    return query_grad, key_grad, value_grad


def solution(mesh):
    rows = P(("groups", "ctx"), None)
    return jax.shard_map(
        body,
        mesh=mesh,
        in_specs=(rows, rows, rows, rows, rows, P(None, ("groups", "ctx")), P("groups")),
        out_specs=(rows, rows, rows),
        check_vma=False,
    )
```

```python
import functools
import math

import jax
import jax.numpy as jnp
from jax import lax
from jax.experimental import pallas as pl
from jax.experimental.pallas import tpu as pltpu
from jax.sharding import PartitionSpec as P

HEAD_WIDTH = 128
KEY_VALUE_HEADS = 4
WINDOW = 896
SCALE = HEAD_WIDTH ** (-0.5)
LOG2E = math.log2(math.e)
HALF = KEY_VALUE_HEADS // 2

ANY = pl.BlockSpec(memory_space=pl.ANY)
VMEM = pl.BlockSpec(memory_space=pltpu.VMEM)
SMEM = pl.BlockSpec(memory_space=pltpu.SMEM)
HBM = pl.BlockSpec(memory_space=pltpu.HBM)
NT = (((1,), (1,)), ((), ()))
NN = (((1,), (0,)), ((), ()))


def dot(a, b, dims):
    return lax.dot_general(a, b, dims, preferred_element_type=jnp.float32)


def shift_pairs(devices, chips):
    first, last = max(0, -2 * chips), min(devices, devices - 2 * chips)
    return [(source, source + 2 * chips) for source in range(first, last)]


def pair_pairs(devices):
    return [(source, source ^ 2) for source in range(devices)]


def partner_pairs(devices):
    return [(source, source ^ 1) for source in range(devices)]


def lanes(start, size):
    return pl.ds(pl.multiple_of(start, 128), size)


def weight(cost):
    return pl.CostEstimate(flops=1000 + 1000000000 * cost, bytes_accessed=1000 + 3690000 * cost, transcendentals=0)


def small_call(kernel, out_shape, in_specs, out_specs, scratch, cost=0, vmem=8, aliases=None):
    return pl.pallas_call(
        kernel,
        out_shape=out_shape,
        in_specs=in_specs,
        out_specs=out_specs,
        scratch_shapes=scratch,
        input_output_aliases=aliases or {},
        compiler_params=pltpu.CompilerParams(vmem_limit_bytes=vmem * 1024 * 1024),
        cost_estimate=weight(cost),
    )


def run_copies(pairs, sems):
    copies = [pltpu.make_async_copy(a, b, sems.at[i]) for i, (a, b) in enumerate(pairs)]
    for copy in copies:
        copy.start()
    for copy in copies:
        copy.wait()


def pack_keys_kernel(place, k, v, joined, send, sems):
    core = lax.rem(place[0], 2)
    block = k.shape[0]
    keep = joined.at[pl.ds(pl.multiple_of(core * block, 128), block), :]
    pairs = []
    for target, which in ((send, 1 - core), (keep, core)):
        for g in range(HALF):
            source = lanes((which * HALF + g) * HEAD_WIDTH, HEAD_WIDTH)
            pairs.append((k.at[:, source], target.at[:, pl.ds(2 * g * HEAD_WIDTH, HEAD_WIDTH)]))
            pairs.append((v.at[:, source], target.at[:, pl.ds((2 * g + 1) * HEAD_WIDTH, HEAD_WIDTH)]))
    run_copies(pairs, sems)


def pack_queries_kernel(place, q, grad, send, sems):
    core = lax.rem(place[0], 2)
    size = q.shape[1] // 2
    source = lanes((1 - core) * size, size)
    run_copies(
        [
            (q.at[:, source], send.at[:, pl.ds(0, size)]),
            (grad.at[:, source], send.at[:, pl.ds(size, size)]),
        ],
        sems,
    )


def join_keys_kernel(place, other, _, joined, sems):
    core = lax.rem(place[0], 2)
    block = other.shape[0]
    run_copies([(other, joined.at[pl.ds(pl.multiple_of((1 - core) * block, 128), block), :])], sems)


def stats_kernel(per_group, outputs, grad, norms, stats):
    ones = jnp.ones((8, 2 * HEAD_WIDTH), jnp.bfloat16)
    stats[...] = jnp.zeros_like(stats)
    for group in range(KEY_VALUE_HEADS):
        for r in range(per_group):
            head = group * per_group + r
            cols = slice(head * HEAD_WIDTH, (head + 1) * HEAD_WIDTH)
            product = outputs[:, cols].astype(jnp.float32) * grad[:, cols].astype(jnp.float32)
            high = product.astype(jnp.bfloat16)
            low = (product - high.astype(jnp.float32)).astype(jnp.bfloat16)
            delta = dot(ones, jnp.concatenate([high, low], axis=1), NT)
            stats[group, 8 + r : 9 + r, :] = delta[0:1, :]
            stats[group, r : r + 1, :] = norms[head : head + 1, :] * LOG2E


def tile(distance, row_start, query_rows, add, place, lengths, queries, stats, kv, dkv, dq):
    per_group = queries.shape[1] // 2 // HALF // HEAD_WIDTH
    width = per_group * HEAD_WIDTH
    tokens = queries.shape[0]
    keys = kv.shape[0]
    query_start = lax.div(place[0], 2) * tokens
    key_start = query_start - distance * tokens + row_start

    q_positions = query_start + lax.broadcasted_iota(jnp.int32, (1, query_rows), 1)
    lowest = jnp.maximum(q_positions - (WINDOW - 1), 0)
    first_lowest = jnp.maximum(query_start - (WINDOW - 1), 0)
    end = jnp.int32(0)
    for i in range(lengths.shape[0]):
        end = end + lengths[i]
        lowest = jnp.where(q_positions >= end, jnp.maximum(lowest, end), lowest)
        first_lowest = jnp.where(query_start >= end, jnp.maximum(first_lowest, end), first_lowest)
    needed = (key_start >= 0) & (key_start + keys - 1 >= first_lowest)

    @pl.when(needed)
    def _():
        k_positions = key_start + lax.broadcasted_iota(jnp.int32, (keys, query_rows), 0)
        allowed = (k_positions >= lowest) & (k_positions <= q_positions)
        allowed = jnp.concatenate([allowed] * per_group, axis=1)

        def group(g, carry):
            k = kv[:, lanes(2 * g * HEAD_WIDTH, HEAD_WIDTH)]
            v = kv[:, lanes((2 * g + 1) * HEAD_WIDTH, HEAD_WIDTH)]
            first = g * width
            q = jnp.concatenate(
                [queries[:query_rows, lanes(first + r * HEAD_WIDTH, HEAD_WIDTH)] for r in range(per_group)], 0
            )
            first = first + HALF * width
            grad = jnp.concatenate(
                [queries[:query_rows, lanes(first + r * HEAD_WIDTH, HEAD_WIDTH)] for r in range(per_group)], 0
            )
            norm = jnp.concatenate([stats[g, r : r + 1, :query_rows] for r in range(per_group)], 1)
            delta = jnp.concatenate([stats[g, 8 + r : 9 + r, :query_rows] for r in range(per_group)], 1)
            scores = dot(k, q, NT)
            weights = jnp.where(allowed, jnp.exp2(scores * (SCALE * LOG2E) - norm), 0.0)
            dv = dot(weights.astype(jnp.bfloat16), grad, NN)
            through = dot(v, grad, NT)
            ds = (weights * (through - delta)).astype(jnp.bfloat16)
            dk = dot(ds, q, NN)
            part = dot(k.T, ds, NN)
            for r in range(per_group):
                cols = slice(r * tokens, r * tokens + query_rows)
                piece = part[:, r * query_rows : (r + 1) * query_rows]
                dq[g, :, cols] = dq[g, :, cols] + piece if add else piece
            dkv[:, lanes(2 * g * HEAD_WIDTH, HEAD_WIDTH)] = (dk * SCALE).astype(dkv.dtype)
            dkv[:, lanes((2 * g + 1) * HEAD_WIDTH, HEAD_WIDTH)] = dv.astype(dkv.dtype)
            return carry

        lax.fori_loop(0, HALF, group, 0)

    @pl.when(jnp.logical_not(needed))
    def _():
        dkv[...] = jnp.zeros_like(dkv)
        if not add:
            dq[...] = jnp.zeros_like(dq)


def join_queries_in_kernel(place, q, grad, other, stats_mine, stats_other, queries, stats):
    core = lax.rem(place[0], 2)
    block = q.shape[0]
    size = q.shape[1] // 2
    mine = pl.ds(pl.multiple_of(core * block, 128), block)
    theirs = pl.ds(pl.multiple_of((1 - core) * block, 128), block)
    half = lanes(core * size, size)
    queries[mine, :size] = q[:, half]
    queries[mine, size:] = grad[:, half]
    queries[theirs, :] = other[...]
    for g in range(HALF):
        stats[g, :, mine] = stats_mine[core * HALF + g]
        stats[g, :, theirs] = stats_other[g]


def tile_kernel(config, *refs):
    distance, row_start, query_rows, add = config
    place, lengths, queries, stats, kv = refs[:5]
    dkv, dq = refs[-2:]
    tile(distance, row_start, query_rows, add, place, lengths, queries, stats, kv, dkv, dq)


def tile_call(distance, row_start, query_rows, place, lengths, queries, stats, kv, dq, kind=jnp.bfloat16, cost=0):
    add = dq is not None
    tokens, columns = queries.shape
    shape = (HALF, HEAD_WIDTH, columns // 2 // HALF // HEAD_WIDTH * tokens)
    return pl.pallas_call(
        functools.partial(tile_kernel, (distance, row_start, query_rows, add)),
        in_specs=[SMEM, SMEM] + [VMEM] * (4 if add else 3),
        out_specs=[VMEM, VMEM],
        out_shape=[jax.ShapeDtypeStruct(kv.shape, kind), jax.ShapeDtypeStruct(shape, jnp.float32)],
        input_output_aliases={5: 1} if add else {},
        compiler_params=pltpu.CompilerParams(vmem_limit_bytes=24 * 1024 * 1024),
        cost_estimate=weight(cost),
    )(place, lengths, queries, stats, kv, *([dq] if add else []))


def pass_on_kernel(place, second, swapped, third, fourth, out):
    odd = lax.rem(lax.div(place[0], 2), 2) == 1
    rows = second.shape[0] - fourth.shape[0]
    for part in (slice(0, rows), slice(rows, None)):
        value = second[part, :] + third[part, :].astype(jnp.float32)
        value = value + jnp.where(odd, swapped[part, :].astype(jnp.float32), 0.0)
        if part.start:
            value = value + fourth[...].astype(jnp.float32)
        out[part, :] = value.astype(out.dtype)


def finish_queries_kernel(place, dq, keep, send):
    core = lax.rem(place[0], 2)
    block = keep.shape[0]
    tokens = 2 * block
    per_group = keep.shape[1] // HEAD_WIDTH // HALF
    for g in range(HALF):
        for r in range(per_group):
            cols = slice((g * per_group + r) * HEAD_WIDTH, (g * per_group + r + 1) * HEAD_WIDTH)
            for target, which in ((send, 1 - core), (keep, core)):
                start = r * tokens + which * block
                piece = (dq[g, :, lanes(start, block)] * SCALE).astype(jnp.bfloat16)
                target[:, cols] = piece.T


def join_queries_kernel(place, keep, other, joined, sems):
    core = lax.rem(place[0], 2)
    size = keep.shape[1]
    run_copies(
        [(keep, joined.at[:, lanes(core * size, size)]), (other, joined.at[:, lanes((1 - core) * size, size)])],
        sems,
    )


def last_sum_kernel(place, total, swapped, home, keep, send):
    core = lax.rem(place[0], 2)
    even = lax.rem(lax.div(place[0], 2), 2) == 0
    block = keep.shape[0]
    for target, which in ((send, 1 - core), (keep, core)):
        part = pl.ds(pl.multiple_of(which * block, 128), block)
        value = total[part, :] + home[part, :].astype(jnp.float32)
        value = value + jnp.where(even, swapped[part, :].astype(jnp.float32), 0.0)
        target[...] = value.astype(jnp.bfloat16)


def join_grads_kernel(place, keep, other, key_grad, value_grad):
    core = lax.rem(place[0], 2)
    for source, which in ((keep, core), (other, 1 - core)):
        for g in range(HALF):
            target = lanes((which * HALF + g) * HEAD_WIDTH, HEAD_WIDTH)
            key_grad[:, target] = source[:, 2 * g * HEAD_WIDTH : (2 * g + 1) * HEAD_WIDTH]
            value_grad[:, target] = source[:, (2 * g + 1) * HEAD_WIDTH : (2 * g + 2) * HEAD_WIDTH]


def body(q, k, v, outputs, grad, norms, lengths):
    block = q.shape[0]
    tokens = 2 * block
    heads = norms.shape[0]
    per_group = heads // KEY_VALUE_HEADS
    width = per_group * HEAD_WIDTH
    devices = lax.axis_size("ctx")
    place = lax.axis_index("ctx").astype(jnp.int32).reshape(1)
    to_partner = partner_pairs(devices)
    assert -(-(WINDOW - 1) // block) == 7, "window"

    def bf16(*shape):
        return jax.ShapeDtypeStruct(shape, jnp.bfloat16)

    def f32(*shape):
        return jax.ShapeDtypeStruct(shape, jnp.float32)

    def move(array, chips):
        return lax.ppermute(array, "ctx", shift_pairs(devices, chips))

    def swap(array):
        return lax.ppermute(array, "ctx", to_partner)

    dma = pltpu.SemaphoreType.DMA
    kv_width = HALF * 2 * HEAD_WIDTH
    kv_mine, kv_send = small_call(
        pack_keys_kernel,
        [bf16(tokens, kv_width), bf16(block, kv_width)],
        [SMEM, HBM, HBM],
        [ANY, ANY],
        [dma((4 * HALF,))],
        vmem=60,
    )(place, k, v)
    kv = small_call(
        join_keys_kernel,
        bf16(tokens, kv_width),
        [SMEM, ANY, ANY],
        ANY,
        [dma((1,))],
        aliases={2: 0},
    )(place, swap(kv_send), kv_mine)
    kv2 = move(kv, 2)
    kv1 = move(kv, 1)

    norms, kv = lax.optimization_barrier((norms, kv))
    stats_mine = small_call(
        functools.partial(stats_kernel, per_group),
        f32(KEY_VALUE_HEADS, 16, block),
        [VMEM, VMEM, VMEM],
        VMEM,
        [],
        50,
    )(outputs, grad, norms)
    later, kv = lax.optimization_barrier((place, kv))
    q_send = small_call(
        pack_queries_kernel, bf16(block, q.shape[1]), [SMEM, HBM, HBM], VMEM, [dma((2,))], 0, vmem=56
    )(later, q, grad)
    q_other = swap(q_send)
    core = lax.rem(place[0], 2)
    stats_other = swap(lax.dynamic_slice_in_dim(stats_mine, (1 - core) * HALF, HALF, 0))

    queries, stats = small_call(
        join_queries_in_kernel,
        [bf16(tokens, q.shape[1]), f32(HALF, 16, tokens)],
        [SMEM] + [VMEM] * 5,
        [VMEM] * 2,
        [],
    )(place, q, grad, q_other, stats_mine, stats_other)
    kv2, stats = lax.optimization_barrier((kv2, stats))
    kv3 = move(kv2, 1)
    kv4 = move(kv2[block:], 2)
    far = functools.partial(tile_call, place=place, lengths=lengths, queries=queries, stats=stats)
    part1, dq = far(1, 0, tokens, kv=kv1, dq=None)
    swapped = lax.ppermute(part1, "ctx", pair_pairs(devices))
    kv3, kv4 = lax.optimization_barrier((kv3, kv4))
    part3, dq = far(3, 0, tokens, kv=kv3, dq=dq)
    part3 = move(part3, -1)
    part4, dq = far(4, block, block, kv=kv4, dq=dq)
    part4 = move(part4, -2)
    part2, dq = far(2, 0, tokens, kv=kv2, dq=dq, kind=jnp.float32)
    part2 = small_call(
        pass_on_kernel, bf16(tokens, kv_width), [SMEM] + [VMEM] * 4, VMEM, []
    )(place, part2, swapped, part3, part4)
    home = move(part2, -2)
    kv, part2 = lax.optimization_barrier((kv, part2))
    total, dq = far(0, 0, tokens, kv=kv, dq=dq, kind=jnp.float32)

    dq_keep, dq_send = small_call(
        finish_queries_kernel, [bf16(block, HALF * width)] * 2, [SMEM, VMEM], [VMEM, VMEM], []
    )(place, dq)
    dq_other = swap(dq_send)
    query_grad = small_call(
        join_queries_kernel, bf16(block, q.shape[1]), [SMEM, ANY, ANY], ANY, [dma((2,))]
    )(place, dq_keep, dq_other)

    keep, send = small_call(
        last_sum_kernel, [bf16(block, kv_width)] * 2, [SMEM] + [VMEM] * 3, [VMEM, VMEM], [], 20
    )(place, total, swapped, home)
    send = swap(send)
    send, query_grad = lax.optimization_barrier((send, query_grad))
    key_grad, value_grad = small_call(
        join_grads_kernel, [bf16(block, kv_width)] * 2, [SMEM, VMEM, VMEM], [VMEM, VMEM], []
    )(place, keep, send)
    return query_grad, key_grad, value_grad


def solution(mesh):
    rows = P(("groups", "ctx"), None)
    return jax.shard_map(
        body,
        mesh=mesh,
        in_specs=(rows, rows, rows, rows, rows, P(None, ("groups", "ctx")), P("groups")),
        out_specs=(rows, rows, rows),
        check_vma=False,
    )
```

```python
import functools
import math

import jax
import jax.numpy as jnp
from jax import lax
from jax.experimental import pallas as pl
from jax.experimental.pallas import tpu as pltpu
from jax.sharding import PartitionSpec as P

HEAD_WIDTH = 128
KEY_VALUE_HEADS = 4
WINDOW = 896
SCALE = HEAD_WIDTH ** (-0.5)
LOG2E = math.log2(math.e)
HALF = KEY_VALUE_HEADS // 2

ANY = pl.BlockSpec(memory_space=pl.ANY)
VMEM = pl.BlockSpec(memory_space=pltpu.VMEM)
SMEM = pl.BlockSpec(memory_space=pltpu.SMEM)
HBM = pl.BlockSpec(memory_space=pltpu.HBM)
NT = (((1,), (1,)), ((), ()))
NN = (((1,), (0,)), ((), ()))


def dot(a, b, dims):
    return lax.dot_general(a, b, dims, preferred_element_type=jnp.float32)


def shift_pairs(devices, chips):
    first, last = max(0, -2 * chips), min(devices, devices - 2 * chips)
    return [(source, source + 2 * chips) for source in range(first, last)]


def pair_pairs(devices):
    return [(source, source ^ 2) for source in range(devices)]


def partner_pairs(devices):
    return [(source, source ^ 1) for source in range(devices)]


def lanes(start, size):
    return pl.ds(pl.multiple_of(start, 128), size)


def weight(cost):
    return pl.CostEstimate(flops=1000 + 1000000000 * cost, bytes_accessed=1000 + 3690000 * cost, transcendentals=0)


def small_call(kernel, out_shape, in_specs, out_specs, scratch, cost=0, vmem=8, aliases=None):
    return pl.pallas_call(
        kernel,
        out_shape=out_shape,
        in_specs=in_specs,
        out_specs=out_specs,
        scratch_shapes=scratch,
        input_output_aliases=aliases or {},
        compiler_params=pltpu.CompilerParams(vmem_limit_bytes=vmem * 1024 * 1024),
        cost_estimate=weight(cost),
    )


def run_copies(pairs, sems):
    copies = [pltpu.make_async_copy(a, b, sems.at[i]) for i, (a, b) in enumerate(pairs)]
    for copy in copies:
        copy.start()
    for copy in copies:
        copy.wait()


def join_keys_kernel(place, k, v, k_other, v_other, joined):
    core = lax.rem(place[0], 2)
    block = k.shape[0]
    for k_part, v_part, which in ((k, v, core), (k_other, v_other, 1 - core)):
        rows = pl.ds(pl.multiple_of(which * block, 128), block)
        for g in range(HALF):
            source = lanes((core * HALF + g) * HEAD_WIDTH, HEAD_WIDTH)
            joined[rows, 2 * g * HEAD_WIDTH : (2 * g + 1) * HEAD_WIDTH] = k_part[:, source]
            joined[rows, (2 * g + 1) * HEAD_WIDTH : (2 * g + 2) * HEAD_WIDTH] = v_part[:, source]


def stats_kernel(per_group, outputs, grad, norms, stats):
    ones = jnp.ones((8, 2 * HEAD_WIDTH), jnp.bfloat16)
    stats[...] = jnp.zeros_like(stats)
    for group in range(KEY_VALUE_HEADS):
        for r in range(per_group):
            head = group * per_group + r
            cols = slice(head * HEAD_WIDTH, (head + 1) * HEAD_WIDTH)
            product = outputs[:, cols].astype(jnp.float32) * grad[:, cols].astype(jnp.float32)
            high = product.astype(jnp.bfloat16)
            low = (product - high.astype(jnp.float32)).astype(jnp.bfloat16)
            delta = dot(ones, jnp.concatenate([high, low], axis=1), NT)
            stats[group, 8 + r : 9 + r, :] = delta[0:1, :]
            stats[group, r : r + 1, :] = norms[head : head + 1, :] * LOG2E


def tile(distance, row_start, query_rows, add, place, lengths, queries, stats, kv, dkv, dq):
    per_group = queries.shape[1] // 2 // HALF // HEAD_WIDTH
    width = per_group * HEAD_WIDTH
    tokens = queries.shape[0]
    keys = kv.shape[0]
    query_start = lax.div(place[0], 2) * tokens
    key_start = query_start - distance * tokens + row_start

    q_positions = query_start + lax.broadcasted_iota(jnp.int32, (1, query_rows), 1)
    lowest = jnp.maximum(q_positions - (WINDOW - 1), 0)
    first_lowest = jnp.maximum(query_start - (WINDOW - 1), 0)
    end = jnp.int32(0)
    for i in range(lengths.shape[0]):
        end = end + lengths[i]
        lowest = jnp.where(q_positions >= end, jnp.maximum(lowest, end), lowest)
        first_lowest = jnp.where(query_start >= end, jnp.maximum(first_lowest, end), first_lowest)
    needed = (key_start >= 0) & (key_start + keys - 1 >= first_lowest)

    @pl.when(needed)
    def _():
        k_positions = key_start + lax.broadcasted_iota(jnp.int32, (keys, query_rows), 0)
        allowed = (k_positions >= lowest) & (k_positions <= q_positions)
        allowed = jnp.concatenate([allowed] * per_group, axis=1)

        def group(g, carry):
            k = kv[:, lanes(2 * g * HEAD_WIDTH, HEAD_WIDTH)]
            v = kv[:, lanes((2 * g + 1) * HEAD_WIDTH, HEAD_WIDTH)]
            first = g * width
            q = jnp.concatenate(
                [queries[:query_rows, lanes(first + r * HEAD_WIDTH, HEAD_WIDTH)] for r in range(per_group)], 0
            )
            first = first + HALF * width
            grad = jnp.concatenate(
                [queries[:query_rows, lanes(first + r * HEAD_WIDTH, HEAD_WIDTH)] for r in range(per_group)], 0
            )
            norm = jnp.concatenate([stats[g, r : r + 1, :query_rows] for r in range(per_group)], 1)
            delta = jnp.concatenate([stats[g, 8 + r : 9 + r, :query_rows] for r in range(per_group)], 1)
            scores = dot(k, q, NT)
            weights = jnp.where(allowed, jnp.exp2(scores * (SCALE * LOG2E) - norm), 0.0)
            dv = dot(weights.astype(jnp.bfloat16), grad, NN)
            through = dot(v, grad, NT)
            ds = (weights * (through - delta)).astype(jnp.bfloat16)
            dk = dot(ds, q, NN)
            part = dot(k.T, ds, NN)
            for r in range(per_group):
                cols = slice(r * tokens, r * tokens + query_rows)
                piece = part[:, r * query_rows : (r + 1) * query_rows]
                dq[g, :, cols] = dq[g, :, cols] + piece if add else piece
            dkv[:, lanes(2 * g * HEAD_WIDTH, HEAD_WIDTH)] = (dk * SCALE).astype(dkv.dtype)
            dkv[:, lanes((2 * g + 1) * HEAD_WIDTH, HEAD_WIDTH)] = dv.astype(dkv.dtype)
            return carry

        lax.fori_loop(0, HALF, group, 0)

    @pl.when(jnp.logical_not(needed))
    def _():
        dkv[...] = jnp.zeros_like(dkv)
        if not add:
            dq[...] = jnp.zeros_like(dq)


def join_queries_in_kernel(
    place, q, grad, q_other, grad_other, stats_mine, stats_other, queries, stats
):
    core = lax.rem(place[0], 2)
    block = q.shape[0]
    size = q.shape[1] // 2
    half = lanes(core * size, size)
    for q_part, grad_part, stats_part, which in (
        (q, grad, stats_mine, core),
        (q_other, grad_other, stats_other, 1 - core),
    ):
        rows = pl.ds(pl.multiple_of(which * block, 128), block)
        queries[rows, :size] = q_part[:, half]
        queries[rows, size:] = grad_part[:, half]
        for g in range(HALF):
            stats[g, :, rows] = stats_part[core * HALF + g]


def tile_kernel(config, *refs):
    distance, row_start, query_rows, add = config
    place, lengths, queries, stats, kv = refs[:5]
    dkv, dq = refs[-2:]
    tile(distance, row_start, query_rows, add, place, lengths, queries, stats, kv, dkv, dq)


def tile_call(distance, row_start, query_rows, place, lengths, queries, stats, kv, dq, kind=jnp.bfloat16, cost=0):
    add = dq is not None
    tokens, columns = queries.shape
    shape = (HALF, HEAD_WIDTH, columns // 2 // HALF // HEAD_WIDTH * tokens)
    return pl.pallas_call(
        functools.partial(tile_kernel, (distance, row_start, query_rows, add)),
        in_specs=[SMEM, SMEM] + [VMEM] * (4 if add else 3),
        out_specs=[VMEM, VMEM],
        out_shape=[jax.ShapeDtypeStruct(kv.shape, kind), jax.ShapeDtypeStruct(shape, jnp.float32)],
        input_output_aliases={5: 1} if add else {},
        compiler_params=pltpu.CompilerParams(vmem_limit_bytes=24 * 1024 * 1024),
        cost_estimate=weight(cost),
    )(place, lengths, queries, stats, kv, *([dq] if add else []))


def pass_on_kernel(place, second, swapped, third, fourth, out):
    odd = lax.rem(lax.div(place[0], 2), 2) == 1
    rows = second.shape[0] - fourth.shape[0]
    for part in (slice(0, rows), slice(rows, None)):
        value = second[part, :] + third[part, :].astype(jnp.float32)
        value = value + jnp.where(odd, swapped[part, :].astype(jnp.float32), 0.0)
        if part.start:
            value = value + fourth[...].astype(jnp.float32)
        out[part, :] = value.astype(out.dtype)


def finish_queries_kernel(place, dq, keep, send):
    core = lax.rem(place[0], 2)
    block = keep.shape[0]
    tokens = 2 * block
    per_group = keep.shape[1] // HEAD_WIDTH // HALF
    for g in range(HALF):
        for r in range(per_group):
            cols = slice((g * per_group + r) * HEAD_WIDTH, (g * per_group + r + 1) * HEAD_WIDTH)
            for target, which in ((send, 1 - core), (keep, core)):
                start = r * tokens + which * block
                piece = (dq[g, :, lanes(start, block)] * SCALE).astype(jnp.bfloat16)
                target[:, cols] = piece.T


def join_queries_kernel(place, keep, other, joined, sems):
    core = lax.rem(place[0], 2)
    size = keep.shape[1]
    run_copies(
        [(keep, joined.at[:, lanes(core * size, size)]), (other, joined.at[:, lanes((1 - core) * size, size)])],
        sems,
    )


def last_sum_kernel(place, total, swapped, home, keep, send):
    core = lax.rem(place[0], 2)
    even = lax.rem(lax.div(place[0], 2), 2) == 0
    block = keep.shape[0]
    for target, which in ((send, 1 - core), (keep, core)):
        part = pl.ds(pl.multiple_of(which * block, 128), block)
        value = total[part, :] + home[part, :].astype(jnp.float32)
        value = value + jnp.where(even, swapped[part, :].astype(jnp.float32), 0.0)
        target[...] = value.astype(jnp.bfloat16)


def join_grads_kernel(place, keep, other, key_grad, value_grad):
    core = lax.rem(place[0], 2)
    for source, which in ((keep, core), (other, 1 - core)):
        for g in range(HALF):
            target = lanes((which * HALF + g) * HEAD_WIDTH, HEAD_WIDTH)
            key_grad[:, target] = source[:, 2 * g * HEAD_WIDTH : (2 * g + 1) * HEAD_WIDTH]
            value_grad[:, target] = source[:, (2 * g + 1) * HEAD_WIDTH : (2 * g + 2) * HEAD_WIDTH]


def body(q, k, v, outputs, grad, norms, lengths):
    block = q.shape[0]
    tokens = 2 * block
    heads = norms.shape[0]
    per_group = heads // KEY_VALUE_HEADS
    width = per_group * HEAD_WIDTH
    devices = lax.axis_size("ctx")
    place = lax.axis_index("ctx").astype(jnp.int32).reshape(1)
    to_partner = partner_pairs(devices)
    assert -(-(WINDOW - 1) // block) == 7, "window"

    def bf16(*shape):
        return jax.ShapeDtypeStruct(shape, jnp.bfloat16)

    def f32(*shape):
        return jax.ShapeDtypeStruct(shape, jnp.float32)

    def move(array, chips):
        return lax.ppermute(array, "ctx", shift_pairs(devices, chips))

    def swap(array):
        return lax.ppermute(array, "ctx", to_partner)

    dma = pltpu.SemaphoreType.DMA
    kv_width = HALF * 2 * HEAD_WIDTH
    kv = small_call(
        join_keys_kernel, bf16(tokens, kv_width), [SMEM] + [VMEM] * 4, VMEM, []
    )(place, k, v, swap(k), swap(v))
    kv2 = move(kv, 2)
    kv1 = move(kv, 1)

    norms, kv = lax.optimization_barrier((norms, kv))
    stats_mine = small_call(
        functools.partial(stats_kernel, per_group),
        f32(KEY_VALUE_HEADS, 16, block),
        [VMEM, VMEM, VMEM],
        VMEM,
        [],
        50,
    )(outputs, grad, norms)
    stats_other = swap(stats_mine)
    q_late, grad_late, kv = lax.optimization_barrier((q, grad, kv))
    q_other, grad_other = swap(q_late), swap(grad_late)
    queries, stats = small_call(
        join_queries_in_kernel,
        [bf16(tokens, q.shape[1]), f32(HALF, 16, tokens)],
        [SMEM] + [VMEM] * 6,
        [VMEM] * 2,
        [],
    )(place, q, grad, q_other, grad_other, stats_mine, stats_other)
    kv2, stats = lax.optimization_barrier((kv2, stats))
    kv3 = move(kv2, 1)
    kv4 = move(kv2[block:], 2)
    far = functools.partial(tile_call, place=place, lengths=lengths, queries=queries, stats=stats)
    part1, dq = far(1, 0, tokens, kv=kv1, dq=None)
    swapped = lax.ppermute(part1, "ctx", pair_pairs(devices))
    kv3, kv4 = lax.optimization_barrier((kv3, kv4))
    part3, dq = far(3, 0, tokens, kv=kv3, dq=dq)
    part3 = move(part3, -1)
    part4, dq = far(4, block, block, kv=kv4, dq=dq)
    part4 = move(part4, -2)
    part2, dq = far(2, 0, tokens, kv=kv2, dq=dq, kind=jnp.float32)
    part2 = small_call(
        pass_on_kernel, bf16(tokens, kv_width), [SMEM] + [VMEM] * 4, VMEM, []
    )(place, part2, swapped, part3, part4)
    home = move(part2, -2)
    kv, part2 = lax.optimization_barrier((kv, part2))
    total, dq = far(0, 0, tokens, kv=kv, dq=dq, kind=jnp.float32)

    dq_keep, dq_send = small_call(
        finish_queries_kernel, [bf16(block, HALF * width)] * 2, [SMEM, VMEM], [VMEM, VMEM], []
    )(place, dq)
    dq_other = swap(dq_send)
    query_grad = small_call(
        join_queries_kernel, bf16(block, q.shape[1]), [SMEM, ANY, ANY], ANY, [dma((2,))]
    )(place, dq_keep, dq_other)

    keep, send = small_call(
        last_sum_kernel, [bf16(block, kv_width)] * 2, [SMEM] + [VMEM] * 3, [VMEM, VMEM], [], 20
    )(place, total, swapped, home)
    send = swap(send)
    send, query_grad = lax.optimization_barrier((send, query_grad))
    key_grad, value_grad = small_call(
        join_grads_kernel, [bf16(block, kv_width)] * 2, [SMEM, VMEM, VMEM], [VMEM, VMEM], []
    )(place, keep, send)
    return query_grad, key_grad, value_grad


def solution(mesh):
    rows = P(("groups", "ctx"), None)
    return jax.shard_map(
        body,
        mesh=mesh,
        in_specs=(rows, rows, rows, rows, rows, P(None, ("groups", "ctx")), P("groups")),
        out_specs=(rows, rows, rows),
        check_vma=False,
    )
```

```python
import functools
import math

import jax
import jax.numpy as jnp
from jax import lax
from jax.experimental import pallas as pl
from jax.experimental.pallas import tpu as pltpu
from jax.sharding import PartitionSpec as P

HEAD_WIDTH = 128
KEY_VALUE_HEADS = 4
WINDOW = 896
SCALE = HEAD_WIDTH ** (-0.5)
LOG2E = math.log2(math.e)
HALF = KEY_VALUE_HEADS // 2

ANY = pl.BlockSpec(memory_space=pl.ANY)
VMEM = pl.BlockSpec(memory_space=pltpu.VMEM)
SMEM = pl.BlockSpec(memory_space=pltpu.SMEM)
HBM = pl.BlockSpec(memory_space=pltpu.HBM)
NT = (((1,), (1,)), ((), ()))
NN = (((1,), (0,)), ((), ()))


def dot(a, b, dims):
    return lax.dot_general(a, b, dims, preferred_element_type=jnp.float32)


def shift_pairs(devices, chips):
    first, last = max(0, -2 * chips), min(devices, devices - 2 * chips)
    return [(source, source + 2 * chips) for source in range(first, last)]


def pair_pairs(devices):
    return [(source, source ^ 2) for source in range(devices)]


def partner_pairs(devices):
    return [(source, source ^ 1) for source in range(devices)]


def lanes(start, size):
    return pl.ds(pl.multiple_of(start, 128), size)


def weight(cost):
    return pl.CostEstimate(flops=1000 + 1000000000 * cost, bytes_accessed=1000 + 3690000 * cost, transcendentals=0)


def small_call(kernel, out_shape, in_specs, out_specs, scratch, cost=0, vmem=8, aliases=None):
    return pl.pallas_call(
        kernel,
        out_shape=out_shape,
        in_specs=in_specs,
        out_specs=out_specs,
        scratch_shapes=scratch,
        input_output_aliases=aliases or {},
        compiler_params=pltpu.CompilerParams(vmem_limit_bytes=vmem * 1024 * 1024),
        cost_estimate=weight(cost),
    )


def run_copies(pairs, sems):
    copies = [pltpu.make_async_copy(a, b, sems.at[i]) for i, (a, b) in enumerate(pairs)]
    for copy in copies:
        copy.start()
    for copy in copies:
        copy.wait()


def own_keys_kernel(place, k, v, own):
    core = lax.rem(place[0], 2)
    for g in range(HALF):
        source = lanes((core * HALF + g) * HEAD_WIDTH, HEAD_WIDTH)
        own[:, 2 * g * HEAD_WIDTH : (2 * g + 1) * HEAD_WIDTH] = k[:, source]
        own[:, (2 * g + 1) * HEAD_WIDTH : (2 * g + 2) * HEAD_WIDTH] = v[:, source]


def join_keys_kernel(place, own, k_other, v_other, joined):
    core = lax.rem(place[0], 2)
    block = own.shape[0]
    joined[pl.ds(pl.multiple_of(core * block, 128), block), :] = own[...]
    rows = pl.ds(pl.multiple_of((1 - core) * block, 128), block)
    for g in range(HALF):
        source = lanes((core * HALF + g) * HEAD_WIDTH, HEAD_WIDTH)
        joined[rows, 2 * g * HEAD_WIDTH : (2 * g + 1) * HEAD_WIDTH] = k_other[:, source]
        joined[rows, (2 * g + 1) * HEAD_WIDTH : (2 * g + 2) * HEAD_WIDTH] = v_other[:, source]


def stats_kernel(per_group, outputs, grad, norms, stats):
    ones = jnp.ones((8, 2 * HEAD_WIDTH), jnp.bfloat16)
    stats[...] = jnp.zeros_like(stats)
    for group in range(KEY_VALUE_HEADS):
        for r in range(per_group):
            head = group * per_group + r
            cols = slice(head * HEAD_WIDTH, (head + 1) * HEAD_WIDTH)
            product = outputs[:, cols].astype(jnp.float32) * grad[:, cols].astype(jnp.float32)
            high = product.astype(jnp.bfloat16)
            low = (product - high.astype(jnp.float32)).astype(jnp.bfloat16)
            delta = dot(ones, jnp.concatenate([high, low], axis=1), NT)
            stats[group, 8 + r : 9 + r, :] = delta[0:1, :]
            stats[group, r : r + 1, :] = norms[head : head + 1, :] * LOG2E


def tile(distance, row_start, query_rows, add, place, lengths, queries, stats, kv, dkv, dq):
    per_group = queries.shape[1] // 2 // HALF // HEAD_WIDTH
    width = per_group * HEAD_WIDTH
    tokens = queries.shape[0]
    keys = kv.shape[0]
    query_start = lax.div(place[0], 2) * tokens
    key_start = query_start - distance * tokens + row_start

    q_positions = query_start + lax.broadcasted_iota(jnp.int32, (1, query_rows), 1)
    lowest = jnp.maximum(q_positions - (WINDOW - 1), 0)
    first_lowest = jnp.maximum(query_start - (WINDOW - 1), 0)
    end = jnp.int32(0)
    for i in range(lengths.shape[0]):
        end = end + lengths[i]
        lowest = jnp.where(q_positions >= end, jnp.maximum(lowest, end), lowest)
        first_lowest = jnp.where(query_start >= end, jnp.maximum(first_lowest, end), first_lowest)
    needed = (key_start >= 0) & (key_start + keys - 1 >= first_lowest)

    @pl.when(needed)
    def _():
        k_positions = key_start + lax.broadcasted_iota(jnp.int32, (keys, query_rows), 0)
        allowed = (k_positions >= lowest) & (k_positions <= q_positions)
        allowed = jnp.concatenate([allowed] * per_group, axis=1)

        def group(g, carry):
            k = kv[:, lanes(2 * g * HEAD_WIDTH, HEAD_WIDTH)]
            v = kv[:, lanes((2 * g + 1) * HEAD_WIDTH, HEAD_WIDTH)]
            first = g * width
            q = jnp.concatenate(
                [queries[:query_rows, lanes(first + r * HEAD_WIDTH, HEAD_WIDTH)] for r in range(per_group)], 0
            )
            first = first + HALF * width
            grad = jnp.concatenate(
                [queries[:query_rows, lanes(first + r * HEAD_WIDTH, HEAD_WIDTH)] for r in range(per_group)], 0
            )
            norm = jnp.concatenate([stats[g, r : r + 1, :query_rows] for r in range(per_group)], 1)
            delta = jnp.concatenate([stats[g, 8 + r : 9 + r, :query_rows] for r in range(per_group)], 1)
            scores = dot(k, q, NT)
            weights = jnp.where(allowed, jnp.exp2(scores * (SCALE * LOG2E) - norm), 0.0)
            dv = dot(weights.astype(jnp.bfloat16), grad, NN)
            through = dot(v, grad, NT)
            ds = (weights * (through - delta)).astype(jnp.bfloat16)
            dk = dot(ds, q, NN)
            part = dot(k.T, ds, NN)
            for r in range(per_group):
                cols = slice(r * tokens, r * tokens + query_rows)
                piece = part[:, r * query_rows : (r + 1) * query_rows]
                dq[g, :, cols] = dq[g, :, cols] + piece if add else piece
            dkv[:, lanes(2 * g * HEAD_WIDTH, HEAD_WIDTH)] = (dk * SCALE).astype(dkv.dtype)
            dkv[:, lanes((2 * g + 1) * HEAD_WIDTH, HEAD_WIDTH)] = dv.astype(dkv.dtype)
            return carry

        lax.fori_loop(0, HALF, group, 0)

    @pl.when(jnp.logical_not(needed))
    def _():
        dkv[...] = jnp.zeros_like(dkv)
        if not add:
            dq[...] = jnp.zeros_like(dq)


def join_queries_in_kernel(
    place, q, grad, q_other, grad_other, stats_mine, stats_other, queries, stats
):
    core = lax.rem(place[0], 2)
    block = q.shape[0]
    size = q.shape[1] // 2
    half = lanes(core * size, size)
    for q_part, grad_part, stats_part, which in (
        (q, grad, stats_mine, core),
        (q_other, grad_other, stats_other, 1 - core),
    ):
        rows = pl.ds(pl.multiple_of(which * block, 128), block)
        queries[rows, :size] = q_part[:, half]
        queries[rows, size:] = grad_part[:, half]
        for g in range(HALF):
            stats[g, :, rows] = stats_part[core * HALF + g]


def tile_kernel(config, *refs):
    distance, row_start, query_rows, add = config
    place, lengths, queries, stats, kv = refs[:5]
    dkv, dq = refs[-2:]
    tile(distance, row_start, query_rows, add, place, lengths, queries, stats, kv, dkv, dq)


def tile_call(distance, row_start, query_rows, place, lengths, queries, stats, kv, dq, kind=jnp.bfloat16, cost=0):
    add = dq is not None
    tokens, columns = queries.shape
    shape = (HALF, HEAD_WIDTH, columns // 2 // HALF // HEAD_WIDTH * tokens)
    return pl.pallas_call(
        functools.partial(tile_kernel, (distance, row_start, query_rows, add)),
        in_specs=[SMEM, SMEM] + [VMEM] * (4 if add else 3),
        out_specs=[VMEM, VMEM],
        out_shape=[jax.ShapeDtypeStruct(kv.shape, kind), jax.ShapeDtypeStruct(shape, jnp.float32)],
        input_output_aliases={5: 1} if add else {},
        compiler_params=pltpu.CompilerParams(vmem_limit_bytes=24 * 1024 * 1024),
        cost_estimate=weight(cost),
    )(place, lengths, queries, stats, kv, *([dq] if add else []))


def pass_on_kernel(place, second, swapped, third, fourth, out):
    odd = lax.rem(lax.div(place[0], 2), 2) == 1
    rows = second.shape[0] - fourth.shape[0]
    for part in (slice(0, rows), slice(rows, None)):
        value = second[part, :] + third[part, :].astype(jnp.float32)
        value = value + jnp.where(odd, swapped[part, :].astype(jnp.float32), 0.0)
        if part.start:
            value = value + fourth[...].astype(jnp.float32)
        out[part, :] = value.astype(out.dtype)


def finish_queries_kernel(place, dq, keep, send):
    core = lax.rem(place[0], 2)
    block = keep.shape[0]
    tokens = 2 * block
    per_group = keep.shape[1] // HEAD_WIDTH // HALF
    for g in range(HALF):
        for r in range(per_group):
            cols = slice((g * per_group + r) * HEAD_WIDTH, (g * per_group + r + 1) * HEAD_WIDTH)
            for target, which in ((send, 1 - core), (keep, core)):
                start = r * tokens + which * block
                piece = (dq[g, :, lanes(start, block)] * SCALE).astype(jnp.bfloat16)
                target[:, cols] = piece.T


def join_queries_kernel(place, keep, other, joined, sems):
    core = lax.rem(place[0], 2)
    size = keep.shape[1]
    run_copies(
        [(keep, joined.at[:, lanes(core * size, size)]), (other, joined.at[:, lanes((1 - core) * size, size)])],
        sems,
    )


def last_sum_kernel(place, total, swapped, home, keep, send):
    core = lax.rem(place[0], 2)
    even = lax.rem(lax.div(place[0], 2), 2) == 0
    block = keep.shape[0]
    for target, which in ((send, 1 - core), (keep, core)):
        part = pl.ds(pl.multiple_of(which * block, 128), block)
        value = total[part, :] + home[part, :].astype(jnp.float32)
        value = value + jnp.where(even, swapped[part, :].astype(jnp.float32), 0.0)
        target[...] = value.astype(jnp.bfloat16)


def join_grads_kernel(place, keep, other, key_grad, value_grad):
    core = lax.rem(place[0], 2)
    for source, which in ((keep, core), (other, 1 - core)):
        for g in range(HALF):
            target = lanes((which * HALF + g) * HEAD_WIDTH, HEAD_WIDTH)
            key_grad[:, target] = source[:, 2 * g * HEAD_WIDTH : (2 * g + 1) * HEAD_WIDTH]
            value_grad[:, target] = source[:, (2 * g + 1) * HEAD_WIDTH : (2 * g + 2) * HEAD_WIDTH]


def body(q, k, v, outputs, grad, norms, lengths):
    block = q.shape[0]
    tokens = 2 * block
    heads = norms.shape[0]
    per_group = heads // KEY_VALUE_HEADS
    width = per_group * HEAD_WIDTH
    devices = lax.axis_size("ctx")
    place = lax.axis_index("ctx").astype(jnp.int32).reshape(1)
    to_partner = partner_pairs(devices)
    assert -(-(WINDOW - 1) // block) == 7, "window"

    def bf16(*shape):
        return jax.ShapeDtypeStruct(shape, jnp.bfloat16)

    def f32(*shape):
        return jax.ShapeDtypeStruct(shape, jnp.float32)

    def move(array, chips):
        return lax.ppermute(array, "ctx", shift_pairs(devices, chips))

    def swap(array):
        return lax.ppermute(array, "ctx", to_partner)

    dma = pltpu.SemaphoreType.DMA
    kv_width = HALF * 2 * HEAD_WIDTH
    own = small_call(
        own_keys_kernel, bf16(block, kv_width), [SMEM, VMEM, VMEM], VMEM, [], 0
    )(place, k, v)
    kv = small_call(
        join_keys_kernel, bf16(tokens, kv_width), [SMEM] + [VMEM] * 3, VMEM, [], 20
    )(place, own, swap(k), swap(v))
    kv2 = move(kv, 2)
    kv1 = move(kv, 1)

    norms, kv = lax.optimization_barrier((norms, kv))
    stats_mine = small_call(
        functools.partial(stats_kernel, per_group),
        f32(KEY_VALUE_HEADS, 16, block),
        [VMEM, VMEM, VMEM],
        VMEM,
        [],
        50,
    )(outputs, grad, norms)
    stats_other = swap(stats_mine)
    q_late, grad_late, kv = lax.optimization_barrier((q, grad, kv))
    q_other, grad_other = swap(q_late), swap(grad_late)
    queries, stats = small_call(
        join_queries_in_kernel,
        [bf16(tokens, q.shape[1]), f32(HALF, 16, tokens)],
        [SMEM] + [VMEM] * 6,
        [VMEM] * 2,
        [],
    )(place, q, grad, q_other, grad_other, stats_mine, stats_other)
    kv2, stats = lax.optimization_barrier((kv2, stats))
    kv3 = move(kv2, 1)
    kv4 = move(kv2[block:], 2)
    far = functools.partial(tile_call, place=place, lengths=lengths, queries=queries, stats=stats)
    part1, dq = far(1, 0, tokens, kv=kv1, dq=None, cost=0)
    swapped = lax.ppermute(part1, "ctx", pair_pairs(devices))
    kv3, kv4 = lax.optimization_barrier((kv3, kv4))
    part3, dq = far(3, 0, tokens, kv=kv3, dq=dq)
    part3 = move(part3, -1)
    part4, dq = far(4, block, block, kv=kv4, dq=dq)
    part4 = move(part4, -2)
    part2, dq = far(2, 0, tokens, kv=kv2, dq=dq, kind=jnp.float32)
    part2 = small_call(
        pass_on_kernel, bf16(tokens, kv_width), [SMEM] + [VMEM] * 4, VMEM, []
    )(place, part2, swapped, part3, part4)
    home = move(part2, -2)
    kv, part2 = lax.optimization_barrier((kv, part2))
    total, dq = far(0, 0, tokens, kv=kv, dq=dq, kind=jnp.float32)

    dq_keep, dq_send = small_call(
        finish_queries_kernel, [bf16(block, HALF * width)] * 2, [SMEM, VMEM], [VMEM, VMEM], []
    )(place, dq)
    dq_other = swap(dq_send)
    query_grad = small_call(
        join_queries_kernel, bf16(block, q.shape[1]), [SMEM, ANY, ANY], ANY, [dma((2,))]
    )(place, dq_keep, dq_other)

    keep, send = small_call(
        last_sum_kernel, [bf16(block, kv_width)] * 2, [SMEM] + [VMEM] * 3, [VMEM, VMEM], [], 20
    )(place, total, swapped, home)
    send = swap(send)
    send, query_grad = lax.optimization_barrier((send, query_grad))
    key_grad, value_grad = small_call(
        join_grads_kernel, [bf16(block, kv_width)] * 2, [SMEM, VMEM, VMEM], [VMEM, VMEM], []
    )(place, keep, send)
    return query_grad, key_grad, value_grad


def solution(mesh):
    rows = P(("groups", "ctx"), None)
    return jax.shard_map(
        body,
        mesh=mesh,
        in_specs=(rows, rows, rows, rows, rows, P(None, ("groups", "ctx")), P("groups")),
        out_specs=(rows, rows, rows),
        check_vma=False,
    )
```

```python
import functools
import math

import jax
import jax.numpy as jnp
from jax import lax
from jax.experimental import pallas as pl
from jax.experimental.pallas import tpu as pltpu
from jax.sharding import PartitionSpec as P

HEAD_WIDTH = 128
KEY_VALUE_HEADS = 4
WINDOW = 896
SCALE = HEAD_WIDTH ** (-0.5)
LOG2E = math.log2(math.e)
HALF = KEY_VALUE_HEADS // 2

ANY = pl.BlockSpec(memory_space=pl.ANY)
VMEM = pl.BlockSpec(memory_space=pltpu.VMEM)
SMEM = pl.BlockSpec(memory_space=pltpu.SMEM)
HBM = pl.BlockSpec(memory_space=pltpu.HBM)
NT = (((1,), (1,)), ((), ()))
NN = (((1,), (0,)), ((), ()))


def dot(a, b, dims):
    return lax.dot_general(a, b, dims, preferred_element_type=jnp.float32)


def shift_pairs(devices, chips):
    first, last = max(0, -2 * chips), min(devices, devices - 2 * chips)
    return [(source, source + 2 * chips) for source in range(first, last)]


def pair_pairs(devices):
    return [(source, source ^ 2) for source in range(devices)]


def partner_pairs(devices):
    return [(source, source ^ 1) for source in range(devices)]


def lanes(start, size):
    return pl.ds(pl.multiple_of(start, 128), size)


def weight(cost):
    return pl.CostEstimate(flops=1000 + 1000000000 * cost, bytes_accessed=1000 + 3690000 * cost, transcendentals=0)


def small_call(kernel, out_shape, in_specs, out_specs, scratch, cost=0, vmem=8, aliases=None):
    return pl.pallas_call(
        kernel,
        out_shape=out_shape,
        in_specs=in_specs,
        out_specs=out_specs,
        scratch_shapes=scratch,
        input_output_aliases=aliases or {},
        compiler_params=pltpu.CompilerParams(vmem_limit_bytes=vmem * 1024 * 1024),
        cost_estimate=weight(cost),
    )


def run_copies(pairs, sems):
    copies = [pltpu.make_async_copy(a, b, sems.at[i]) for i, (a, b) in enumerate(pairs)]
    for copy in copies:
        copy.start()
    for copy in copies:
        copy.wait()


def own_keys_kernel(place, k, v, own):
    core = lax.rem(place[0], 2)
    for g in range(HALF):
        source = lanes((core * HALF + g) * HEAD_WIDTH, HEAD_WIDTH)
        own[:, 2 * g * HEAD_WIDTH : (2 * g + 1) * HEAD_WIDTH] = k[:, source]
        own[:, (2 * g + 1) * HEAD_WIDTH : (2 * g + 2) * HEAD_WIDTH] = v[:, source]


def join_keys_kernel(place, own, k_other, v_other, joined):
    core = lax.rem(place[0], 2)
    block = own.shape[0]
    joined[pl.ds(pl.multiple_of(core * block, 128), block), :] = own[...]
    rows = pl.ds(pl.multiple_of((1 - core) * block, 128), block)
    for g in range(HALF):
        source = lanes((core * HALF + g) * HEAD_WIDTH, HEAD_WIDTH)
        joined[rows, 2 * g * HEAD_WIDTH : (2 * g + 1) * HEAD_WIDTH] = k_other[:, source]
        joined[rows, (2 * g + 1) * HEAD_WIDTH : (2 * g + 2) * HEAD_WIDTH] = v_other[:, source]


def stats_kernel(per_group, outputs, grad, norms, stats):
    ones = jnp.ones((8, 2 * HEAD_WIDTH), jnp.bfloat16)
    stats[...] = jnp.zeros_like(stats)
    for group in range(KEY_VALUE_HEADS):
        for r in range(per_group):
            head = group * per_group + r
            cols = slice(head * HEAD_WIDTH, (head + 1) * HEAD_WIDTH)
            product = outputs[:, cols].astype(jnp.float32) * grad[:, cols].astype(jnp.float32)
            high = product.astype(jnp.bfloat16)
            low = (product - high.astype(jnp.float32)).astype(jnp.bfloat16)
            delta = dot(ones, jnp.concatenate([high, low], axis=1), NT)
            stats[group, 8 + r : 9 + r, :] = delta[0:1, :]
            stats[group, r : r + 1, :] = norms[head : head + 1, :] * LOG2E


def tile(distance, row_start, query_rows, add, place, lengths, queries, stats, kv, dkv, dq):
    per_group = queries.shape[1] // 2 // HALF // HEAD_WIDTH
    width = per_group * HEAD_WIDTH
    tokens = queries.shape[0]
    keys = kv.shape[0]
    query_start = lax.div(place[0], 2) * tokens
    key_start = query_start - distance * tokens + row_start

    q_positions = query_start + lax.broadcasted_iota(jnp.int32, (1, query_rows), 1)
    lowest = jnp.maximum(q_positions - (WINDOW - 1), 0)
    first_lowest = jnp.maximum(query_start - (WINDOW - 1), 0)
    end = jnp.int32(0)
    for i in range(lengths.shape[0]):
        end = end + lengths[i]
        lowest = jnp.where(q_positions >= end, jnp.maximum(lowest, end), lowest)
        first_lowest = jnp.where(query_start >= end, jnp.maximum(first_lowest, end), first_lowest)
    needed = (key_start >= 0) & (key_start + keys - 1 >= first_lowest)

    @pl.when(needed)
    def _():
        k_positions = key_start + lax.broadcasted_iota(jnp.int32, (keys, query_rows), 0)
        allowed = (k_positions >= lowest) & (k_positions <= q_positions)
        allowed = jnp.concatenate([allowed] * per_group, axis=1)

        def group(g, carry):
            k = kv[:, lanes(2 * g * HEAD_WIDTH, HEAD_WIDTH)]
            v = kv[:, lanes((2 * g + 1) * HEAD_WIDTH, HEAD_WIDTH)]
            first = g * width
            q = jnp.concatenate(
                [queries[:query_rows, lanes(first + r * HEAD_WIDTH, HEAD_WIDTH)] for r in range(per_group)], 0
            )
            first = first + HALF * width
            grad = jnp.concatenate(
                [queries[:query_rows, lanes(first + r * HEAD_WIDTH, HEAD_WIDTH)] for r in range(per_group)], 0
            )
            norm = jnp.concatenate([stats[g, r : r + 1, :query_rows] for r in range(per_group)], 1)
            delta = jnp.concatenate([stats[g, 8 + r : 9 + r, :query_rows] for r in range(per_group)], 1)
            scores = dot(k, q, NT)
            weights = jnp.where(allowed, jnp.exp2(scores * (SCALE * LOG2E) - norm), 0.0)
            dv = dot(weights.astype(jnp.bfloat16), grad, NN)
            through = dot(v, grad, NT)
            ds = (weights * (through - delta)).astype(jnp.bfloat16)
            dk = dot(ds, q, NN)
            part = dot(k.T, ds, NN)
            for r in range(per_group):
                cols = slice(r * tokens, r * tokens + query_rows)
                piece = part[:, r * query_rows : (r + 1) * query_rows]
                dq[g, :, cols] = dq[g, :, cols] + piece if add else piece
            dkv[:, lanes(2 * g * HEAD_WIDTH, HEAD_WIDTH)] = (dk * SCALE).astype(dkv.dtype)
            dkv[:, lanes((2 * g + 1) * HEAD_WIDTH, HEAD_WIDTH)] = dv.astype(dkv.dtype)
            return carry

        lax.fori_loop(0, HALF, group, 0)

    @pl.when(jnp.logical_not(needed))
    def _():
        dkv[...] = jnp.zeros_like(dkv)
        if not add:
            dq[...] = jnp.zeros_like(dq)


def join_queries_in_kernel(
    place, q, grad, q_other, grad_other, stats_mine, stats_other, queries, stats
):
    core = lax.rem(place[0], 2)
    block = q.shape[0]
    size = q.shape[1] // 2
    half = lanes(core * size, size)
    for q_part, grad_part, stats_part, which in (
        (q, grad, stats_mine, core),
        (q_other, grad_other, stats_other, 1 - core),
    ):
        rows = pl.ds(pl.multiple_of(which * block, 128), block)
        queries[rows, :size] = q_part[:, half]
        queries[rows, size:] = grad_part[:, half]
        for g in range(HALF):
            stats[g, :, rows] = stats_part[core * HALF + g]


def tile_kernel(config, *refs):
    distance, row_start, query_rows, add = config
    place, lengths, queries, stats, kv = refs[:5]
    dkv, dq = refs[-2:]
    tile(distance, row_start, query_rows, add, place, lengths, queries, stats, kv, dkv, dq)


def tile_call(distance, row_start, query_rows, place, lengths, queries, stats, kv, dq, kind=jnp.bfloat16, cost=0):
    add = dq is not None
    tokens, columns = queries.shape
    shape = (HALF, HEAD_WIDTH, columns // 2 // HALF // HEAD_WIDTH * tokens)
    return pl.pallas_call(
        functools.partial(tile_kernel, (distance, row_start, query_rows, add)),
        in_specs=[SMEM, SMEM] + [VMEM] * (4 if add else 3),
        out_specs=[VMEM, VMEM],
        out_shape=[jax.ShapeDtypeStruct(kv.shape, kind), jax.ShapeDtypeStruct(shape, jnp.float32)],
        input_output_aliases={5: 1} if add else {},
        compiler_params=pltpu.CompilerParams(vmem_limit_bytes=24 * 1024 * 1024),
        cost_estimate=weight(cost),
    )(place, lengths, queries, stats, kv, *([dq] if add else []))


def early_sum_kernel(place, second, swapped, fourth, out):
    odd = lax.rem(lax.div(place[0], 2), 2) == 1
    rows = second.shape[0] - fourth.shape[0]
    value = second[...] + jnp.where(odd, swapped[...].astype(jnp.float32), 0.0)
    out[:rows, :] = value[:rows]
    out[rows:, :] = value[rows:] + fourth[...].astype(jnp.float32)


def pass_on_kernel(second, third, out):
    out[...] = (second[...] + third[...].astype(jnp.float32)).astype(out.dtype)


def finish_queries_kernel(place, dq, keep, send):
    core = lax.rem(place[0], 2)
    block = keep.shape[0]
    tokens = 2 * block
    per_group = keep.shape[1] // HEAD_WIDTH // HALF
    for g in range(HALF):
        for r in range(per_group):
            cols = slice((g * per_group + r) * HEAD_WIDTH, (g * per_group + r + 1) * HEAD_WIDTH)
            for target, which in ((send, 1 - core), (keep, core)):
                start = r * tokens + which * block
                piece = (dq[g, :, lanes(start, block)] * SCALE).astype(jnp.bfloat16)
                target[:, cols] = piece.T


def join_queries_kernel(place, keep, other, joined, sems):
    core = lax.rem(place[0], 2)
    size = keep.shape[1]
    run_copies(
        [(keep, joined.at[:, lanes(core * size, size)]), (other, joined.at[:, lanes((1 - core) * size, size)])],
        sems,
    )


def last_sum_kernel(place, total, swapped, home, keep, send):
    core = lax.rem(place[0], 2)
    even = lax.rem(lax.div(place[0], 2), 2) == 0
    block = keep.shape[0]
    for target, which in ((send, 1 - core), (keep, core)):
        part = pl.ds(pl.multiple_of(which * block, 128), block)
        value = total[part, :] + home[part, :].astype(jnp.float32)
        value = value + jnp.where(even, swapped[part, :].astype(jnp.float32), 0.0)
        target[...] = value.astype(jnp.bfloat16)


def join_grads_kernel(place, keep, other, key_grad, value_grad):
    core = lax.rem(place[0], 2)
    for source, which in ((keep, core), (other, 1 - core)):
        for g in range(HALF):
            target = lanes((which * HALF + g) * HEAD_WIDTH, HEAD_WIDTH)
            key_grad[:, target] = source[:, 2 * g * HEAD_WIDTH : (2 * g + 1) * HEAD_WIDTH]
            value_grad[:, target] = source[:, (2 * g + 1) * HEAD_WIDTH : (2 * g + 2) * HEAD_WIDTH]


def body(q, k, v, outputs, grad, norms, lengths):
    block = q.shape[0]
    tokens = 2 * block
    heads = norms.shape[0]
    per_group = heads // KEY_VALUE_HEADS
    width = per_group * HEAD_WIDTH
    devices = lax.axis_size("ctx")
    place = lax.axis_index("ctx").astype(jnp.int32).reshape(1)
    to_partner = partner_pairs(devices)
    assert -(-(WINDOW - 1) // block) == 7, "window"

    def bf16(*shape):
        return jax.ShapeDtypeStruct(shape, jnp.bfloat16)

    def f32(*shape):
        return jax.ShapeDtypeStruct(shape, jnp.float32)

    def move(array, chips):
        return lax.ppermute(array, "ctx", shift_pairs(devices, chips))

    def swap(array):
        return lax.ppermute(array, "ctx", to_partner)

    dma = pltpu.SemaphoreType.DMA
    kv_width = HALF * 2 * HEAD_WIDTH
    own = small_call(
        own_keys_kernel, bf16(block, kv_width), [SMEM, VMEM, VMEM], VMEM, [], 0
    )(place, k, v)
    kv = small_call(
        join_keys_kernel, bf16(tokens, kv_width), [SMEM] + [VMEM] * 3, VMEM, [], 20
    )(place, own, swap(k), swap(v))
    kv2 = move(kv, 2)
    kv1 = move(kv, 1)

    norms, kv = lax.optimization_barrier((norms, kv))
    stats_mine = small_call(
        functools.partial(stats_kernel, per_group),
        f32(KEY_VALUE_HEADS, 16, block),
        [VMEM, VMEM, VMEM],
        VMEM,
        [],
        50,
    )(outputs, grad, norms)
    stats_other = swap(stats_mine)
    q_late, grad_late, kv = lax.optimization_barrier((q, grad, kv))
    q_other, grad_other = swap(q_late), swap(grad_late)
    queries, stats = small_call(
        join_queries_in_kernel,
        [bf16(tokens, q.shape[1]), f32(HALF, 16, tokens)],
        [SMEM] + [VMEM] * 6,
        [VMEM] * 2,
        [],
        2,
    )(place, q, grad, q_other, grad_other, stats_mine, stats_other)
    kv2, stats = lax.optimization_barrier((kv2, stats))
    kv4 = move(kv2[block:], 2)
    kv3 = move(kv2, 1)
    far = functools.partial(tile_call, place=place, lengths=lengths, queries=queries, stats=stats)
    part1, dq = far(1, 0, tokens, kv=kv1, dq=None, cost=0)
    swapped = lax.ppermute(part1, "ctx", pair_pairs(devices))
    part4, dq = far(4, block, block, kv=kv4, dq=dq, cost=1)
    part4 = move(part4, -2)
    part3, dq = far(3, 0, tokens, kv=kv3, dq=dq, cost=0)
    part3 = move(part3, -1)
    part2, dq = far(2, 0, tokens, kv=kv2, dq=dq, kind=jnp.float32)
    part2 = small_call(
        early_sum_kernel, f32(tokens, kv_width), [SMEM] + [VMEM] * 3, VMEM, [], 2
    )(place, part2, swapped, part4)
    part2 = small_call(
        pass_on_kernel, bf16(tokens, kv_width), [VMEM, VMEM], VMEM, []
    )(part2, part3)
    home = move(part2, -2)
    kv, part2 = lax.optimization_barrier((kv, part2))
    total, dq = far(0, 0, tokens, kv=kv, dq=dq, kind=jnp.float32)

    dq_keep, dq_send = small_call(
        finish_queries_kernel, [bf16(block, HALF * width)] * 2, [SMEM, VMEM], [VMEM, VMEM], []
    )(place, dq)
    dq_other = swap(dq_send)
    query_grad = small_call(
        join_queries_kernel, bf16(block, q.shape[1]), [SMEM, ANY, ANY], ANY, [dma((2,))]
    )(place, dq_keep, dq_other)

    keep, send = small_call(
        last_sum_kernel, [bf16(block, kv_width)] * 2, [SMEM] + [VMEM] * 3, [VMEM, VMEM], [], 20
    )(place, total, swapped, home)
    send = swap(send)
    send, query_grad = lax.optimization_barrier((send, query_grad))
    key_grad, value_grad = small_call(
        join_grads_kernel, [bf16(block, kv_width)] * 2, [SMEM, VMEM, VMEM], [VMEM, VMEM], []
    )(place, keep, send)
    return query_grad, key_grad, value_grad


def solution(mesh):
    rows = P(("groups", "ctx"), None)
    return jax.shard_map(
        body,
        mesh=mesh,
        in_specs=(rows, rows, rows, rows, rows, P(None, ("groups", "ctx")), P("groups")),
        out_specs=(rows, rows, rows),
        check_vma=False,
    )
```

```python
import functools
import math

import jax
import jax.numpy as jnp
from jax import lax
from jax.experimental import pallas as pl
from jax.experimental.pallas import tpu as pltpu
from jax.sharding import PartitionSpec as P

HEAD_WIDTH = 128
KEY_VALUE_HEADS = 4
WINDOW = 896
SCALE = HEAD_WIDTH ** (-0.5)
LOG2E = math.log2(math.e)
HALF = KEY_VALUE_HEADS // 2

ANY = pl.BlockSpec(memory_space=pl.ANY)
VMEM = pl.BlockSpec(memory_space=pltpu.VMEM)
SMEM = pl.BlockSpec(memory_space=pltpu.SMEM)
HBM = pl.BlockSpec(memory_space=pltpu.HBM)
NT = (((1,), (1,)), ((), ()))
NN = (((1,), (0,)), ((), ()))


def dot(a, b, dims):
    return lax.dot_general(a, b, dims, preferred_element_type=jnp.float32)


def shift_pairs(devices, chips):
    first, last = max(0, -2 * chips), min(devices, devices - 2 * chips)
    return [(source, source + 2 * chips) for source in range(first, last)]


def pair_pairs(devices):
    return [(source, source ^ 2) for source in range(devices)]


def partner_pairs(devices):
    return [(source, source ^ 1) for source in range(devices)]


def lanes(start, size):
    return pl.ds(pl.multiple_of(start, 128), size)


def weight(cost):
    return pl.CostEstimate(flops=1000 + 1000000000 * cost, bytes_accessed=1000 + 3690000 * cost, transcendentals=0)


def small_call(kernel, out_shape, in_specs, out_specs, scratch, cost=0, vmem=8, aliases=None):
    return pl.pallas_call(
        kernel,
        out_shape=out_shape,
        in_specs=in_specs,
        out_specs=out_specs,
        scratch_shapes=scratch,
        input_output_aliases=aliases or {},
        compiler_params=pltpu.CompilerParams(vmem_limit_bytes=vmem * 1024 * 1024),
        cost_estimate=weight(cost),
    )


def run_copies(pairs, sems):
    copies = [pltpu.make_async_copy(a, b, sems.at[i]) for i, (a, b) in enumerate(pairs)]
    for copy in copies:
        copy.start()
    for copy in copies:
        copy.wait()


def own_keys_kernel(place, k, v, own):
    core = lax.rem(place[0], 2)
    for g in range(HALF):
        source = lanes((core * HALF + g) * HEAD_WIDTH, HEAD_WIDTH)
        own[:, 2 * g * HEAD_WIDTH : (2 * g + 1) * HEAD_WIDTH] = k[:, source]
        own[:, (2 * g + 1) * HEAD_WIDTH : (2 * g + 2) * HEAD_WIDTH] = v[:, source]


def join_keys_kernel(place, own, k_other, v_other, joined):
    core = lax.rem(place[0], 2)
    block = own.shape[0]
    joined[pl.ds(pl.multiple_of(core * block, 128), block), :] = own[...]
    rows = pl.ds(pl.multiple_of((1 - core) * block, 128), block)
    for g in range(HALF):
        source = lanes((core * HALF + g) * HEAD_WIDTH, HEAD_WIDTH)
        joined[rows, 2 * g * HEAD_WIDTH : (2 * g + 1) * HEAD_WIDTH] = k_other[:, source]
        joined[rows, (2 * g + 1) * HEAD_WIDTH : (2 * g + 2) * HEAD_WIDTH] = v_other[:, source]


def stats_kernel(per_group, outputs, grad, norms, stats):
    ones = jnp.ones((8, 2 * HEAD_WIDTH), jnp.bfloat16)
    stats[...] = jnp.zeros_like(stats)
    for group in range(KEY_VALUE_HEADS):
        for r in range(per_group):
            head = group * per_group + r
            cols = slice(head * HEAD_WIDTH, (head + 1) * HEAD_WIDTH)
            product = outputs[:, cols].astype(jnp.float32) * grad[:, cols].astype(jnp.float32)
            high = product.astype(jnp.bfloat16)
            low = (product - high.astype(jnp.float32)).astype(jnp.bfloat16)
            delta = dot(ones, jnp.concatenate([high, low], axis=1), NT)
            stats[group, 8 + r : 9 + r, :] = delta[0:1, :]
            stats[group, r : r + 1, :] = norms[head : head + 1, :] * LOG2E


def tile(distance, row_start, query_rows, add, queries, stats, kv, dkv, dq):
    per_group = queries.shape[1] // 2 // HALF // HEAD_WIDTH
    width = per_group * HEAD_WIDTH
    tokens = queries.shape[0]
    keys = kv.shape[0]
    key_start = row_start - distance * tokens
    q_positions = lax.broadcasted_iota(jnp.int32, (1, query_rows), 1)
    lowest = stats[0, per_group : per_group + 1, :query_rows].astype(jnp.int32)
    needed = jnp.min(stats[0, per_group : per_group + 1, :HEAD_WIDTH]) <= key_start + keys - 1

    @pl.when(needed)
    def _():
        k_positions = key_start + lax.broadcasted_iota(jnp.int32, (keys, query_rows), 0)
        allowed = (k_positions >= lowest) & (k_positions <= q_positions)
        allowed = jnp.concatenate([allowed] * per_group, axis=1)

        def group(g, carry):
            k = kv[:, lanes(2 * g * HEAD_WIDTH, HEAD_WIDTH)]
            v = kv[:, lanes((2 * g + 1) * HEAD_WIDTH, HEAD_WIDTH)]
            first = g * width
            q = jnp.concatenate(
                [queries[:query_rows, lanes(first + r * HEAD_WIDTH, HEAD_WIDTH)] for r in range(per_group)], 0
            )
            first = first + HALF * width
            grad = jnp.concatenate(
                [queries[:query_rows, lanes(first + r * HEAD_WIDTH, HEAD_WIDTH)] for r in range(per_group)], 0
            )
            norm = jnp.concatenate([stats[g, r : r + 1, :query_rows] for r in range(per_group)], 1)
            delta = jnp.concatenate([stats[g, 8 + r : 9 + r, :query_rows] for r in range(per_group)], 1)
            scores = dot(k, q, NT)
            weights = jnp.where(allowed, jnp.exp2(scores * (SCALE * LOG2E) - norm), 0.0)
            dv = dot(weights.astype(jnp.bfloat16), grad, NN)
            through = dot(v, grad, NT)
            ds = (weights * (through - delta)).astype(jnp.bfloat16)
            dk = dot(ds, q, NN)
            part = dot(k.T, ds, NN)
            for r in range(per_group):
                cols = slice(r * tokens, r * tokens + query_rows)
                piece = part[:, r * query_rows : (r + 1) * query_rows]
                dq[g, :, cols] = dq[g, :, cols] + piece if add else piece
            dkv[:, lanes(2 * g * HEAD_WIDTH, HEAD_WIDTH)] = (dk * SCALE).astype(dkv.dtype)
            dkv[:, lanes((2 * g + 1) * HEAD_WIDTH, HEAD_WIDTH)] = dv.astype(dkv.dtype)
            return carry

        lax.fori_loop(0, HALF, group, 0)

    @pl.when(jnp.logical_not(needed))
    def _():
        dkv[...] = jnp.zeros_like(dkv)
        if not add:
            dq[...] = jnp.zeros_like(dq)


def join_queries_in_kernel(
    place, lengths, q, grad, q_other, grad_other, stats_mine, stats_other, queries, stats
):
    core = lax.rem(place[0], 2)
    block = q.shape[0]
    per_group = q.shape[1] // HEAD_WIDTH // KEY_VALUE_HEADS
    size = q.shape[1] // 2
    half = lanes(core * size, size)
    for q_part, grad_part, stats_part, which in (
        (q, grad, stats_mine, core),
        (q_other, grad_other, stats_other, 1 - core),
    ):
        rows = pl.ds(pl.multiple_of(which * block, 128), block)
        queries[rows, :size] = q_part[:, half]
        queries[rows, size:] = grad_part[:, half]
        for g in range(HALF):
            stats[g, :, rows] = stats_part[core * HALF + g]
    start = lax.div(place[0], 2) * 2 * block
    positions = start + lax.broadcasted_iota(jnp.int32, (1, 2 * block), 1)
    lowest = jnp.maximum(positions - (WINDOW - 1), 0)
    end = jnp.int32(0)
    for i in range(lengths.shape[0]):
        end = end + lengths[i]
        lowest = jnp.where(positions >= end, jnp.maximum(lowest, end), lowest)
    stats[0, per_group : per_group + 1, :] = (lowest - start).astype(jnp.float32)


def tile_kernel(config, *refs):
    distance, row_start, query_rows, add = config
    queries, stats, kv = refs[:3]
    dkv, dq = refs[-2:]
    tile(distance, row_start, query_rows, add, queries, stats, kv, dkv, dq)


def tile_call(distance, row_start, query_rows, queries, stats, kv, dq, kind=jnp.bfloat16, cost=0):
    add = dq is not None
    tokens, columns = queries.shape
    shape = (HALF, HEAD_WIDTH, columns // 2 // HALF // HEAD_WIDTH * tokens)
    return pl.pallas_call(
        functools.partial(tile_kernel, (distance, row_start, query_rows, add)),
        in_specs=[VMEM] * (4 if add else 3),
        out_specs=[VMEM, VMEM],
        out_shape=[jax.ShapeDtypeStruct(kv.shape, kind), jax.ShapeDtypeStruct(shape, jnp.float32)],
        input_output_aliases={3: 1} if add else {},
        compiler_params=pltpu.CompilerParams(vmem_limit_bytes=24 * 1024 * 1024),
        cost_estimate=weight(cost),
    )(queries, stats, kv, *([dq] if add else []))


def early_sum_kernel(place, second, swapped, fourth, out):
    odd = lax.rem(lax.div(place[0], 2), 2) == 1
    rows = second.shape[0] - fourth.shape[0]
    value = second[...] + jnp.where(odd, swapped[...].astype(jnp.float32), 0.0)
    out[:rows, :] = value[:rows]
    out[rows:, :] = value[rows:] + fourth[...].astype(jnp.float32)


def pass_on_kernel(second, third, out):
    out[...] = (second[...] + third[...].astype(jnp.float32)).astype(out.dtype)


def finish_queries_kernel(place, dq, keep, send):
    core = lax.rem(place[0], 2)
    block = keep.shape[0]
    tokens = 2 * block
    per_group = keep.shape[1] // HEAD_WIDTH // HALF
    for g in range(HALF):
        for r in range(per_group):
            cols = slice((g * per_group + r) * HEAD_WIDTH, (g * per_group + r + 1) * HEAD_WIDTH)
            for target, which in ((send, 1 - core), (keep, core)):
                start = r * tokens + which * block
                piece = (dq[g, :, lanes(start, block)] * SCALE).astype(jnp.bfloat16)
                target[:, cols] = piece.T


def join_queries_kernel(place, keep, other, joined, sems):
    core = lax.rem(place[0], 2)
    size = keep.shape[1]
    run_copies(
        [(keep, joined.at[:, lanes(core * size, size)]), (other, joined.at[:, lanes((1 - core) * size, size)])],
        sems,
    )


def last_sum_kernel(place, total, swapped, home, keep, send):
    core = lax.rem(place[0], 2)
    even = lax.rem(lax.div(place[0], 2), 2) == 0
    block = keep.shape[0]
    for target, which in ((send, 1 - core), (keep, core)):
        part = pl.ds(pl.multiple_of(which * block, 128), block)
        value = total[part, :] + home[part, :].astype(jnp.float32)
        value = value + jnp.where(even, swapped[part, :].astype(jnp.float32), 0.0)
        target[...] = value.astype(jnp.bfloat16)


def join_grads_kernel(place, keep, other, key_grad, value_grad):
    core = lax.rem(place[0], 2)
    for source, which in ((keep, core), (other, 1 - core)):
        for g in range(HALF):
            target = lanes((which * HALF + g) * HEAD_WIDTH, HEAD_WIDTH)
            key_grad[:, target] = source[:, 2 * g * HEAD_WIDTH : (2 * g + 1) * HEAD_WIDTH]
            value_grad[:, target] = source[:, (2 * g + 1) * HEAD_WIDTH : (2 * g + 2) * HEAD_WIDTH]


def body(q, k, v, outputs, grad, norms, lengths):
    block = q.shape[0]
    tokens = 2 * block
    heads = norms.shape[0]
    per_group = heads // KEY_VALUE_HEADS
    width = per_group * HEAD_WIDTH
    devices = lax.axis_size("ctx")
    place = lax.axis_index("ctx").astype(jnp.int32).reshape(1)
    to_partner = partner_pairs(devices)
    assert -(-(WINDOW - 1) // block) == 7, "window"

    def bf16(*shape):
        return jax.ShapeDtypeStruct(shape, jnp.bfloat16)

    def f32(*shape):
        return jax.ShapeDtypeStruct(shape, jnp.float32)

    def move(array, chips):
        return lax.ppermute(array, "ctx", shift_pairs(devices, chips))

    def swap(array):
        return lax.ppermute(array, "ctx", to_partner)

    dma = pltpu.SemaphoreType.DMA
    kv_width = HALF * 2 * HEAD_WIDTH
    own = small_call(
        own_keys_kernel, bf16(block, kv_width), [SMEM, VMEM, VMEM], VMEM, [], 0
    )(place, k, v)
    kv = small_call(
        join_keys_kernel, bf16(tokens, kv_width), [SMEM] + [VMEM] * 3, VMEM, [], 20
    )(place, own, swap(k), swap(v))
    kv2 = move(kv, 2)
    kv1 = move(kv, 1)

    norms, kv = lax.optimization_barrier((norms, kv))
    stats_mine = small_call(
        functools.partial(stats_kernel, per_group),
        f32(KEY_VALUE_HEADS, 16, block),
        [VMEM, VMEM, VMEM],
        VMEM,
        [],
        50,
    )(outputs, grad, norms)
    stats_other = swap(stats_mine)
    q_late, grad_late, kv = lax.optimization_barrier((q, grad, kv))
    q_other, grad_other = swap(q_late), swap(grad_late)
    queries, stats = small_call(
        join_queries_in_kernel,
        [bf16(tokens, q.shape[1]), f32(HALF, 16, tokens)],
        [SMEM, SMEM] + [VMEM] * 6,
        [VMEM] * 2,
        [],
        2,
    )(place, lengths, q, grad, q_other, grad_other, stats_mine, stats_other)
    kv2, stats = lax.optimization_barrier((kv2, stats))
    kv3 = move(kv2, 1)
    kv4 = move(kv2[block:], 2)
    far = functools.partial(tile_call, queries=queries, stats=stats)
    part1, dq = far(1, 0, tokens, kv=kv1, dq=None, cost=0)
    swapped = lax.ppermute(part1, "ctx", pair_pairs(devices))
    part3, dq = far(3, 0, tokens, kv=kv3, dq=dq, cost=0)
    part3 = move(part3, -1)
    part4, dq = far(4, block, block, kv=kv4, dq=dq, cost=0)
    part4 = move(part4, -2)
    part2, dq = far(2, 0, tokens, kv=kv2, dq=dq, kind=jnp.float32)
    part2 = small_call(
        early_sum_kernel, f32(tokens, kv_width), [SMEM] + [VMEM] * 3, VMEM, [], 0
    )(place, part2, swapped, part4)
    part2 = small_call(
        pass_on_kernel, bf16(tokens, kv_width), [VMEM, VMEM], VMEM, []
    )(part2, part3)
    home = move(part2, -2)
    kv, part2 = lax.optimization_barrier((kv, part2))
    total, dq = far(0, 0, tokens, kv=kv, dq=dq, kind=jnp.float32)

    dq_keep, dq_send = small_call(
        finish_queries_kernel, [bf16(block, HALF * width)] * 2, [SMEM, VMEM], [VMEM, VMEM], []
    )(place, dq)
    dq_other = swap(dq_send)
    query_grad = small_call(
        join_queries_kernel, bf16(block, q.shape[1]), [SMEM, ANY, ANY], ANY, [dma((2,))]
    )(place, dq_keep, dq_other)

    keep, send = small_call(
        last_sum_kernel, [bf16(block, kv_width)] * 2, [SMEM] + [VMEM] * 3, [VMEM, VMEM], [], 20
    )(place, total, swapped, home)
    send = swap(send)
    send, query_grad = lax.optimization_barrier((send, query_grad))
    key_grad, value_grad = small_call(
        join_grads_kernel, [bf16(block, kv_width)] * 2, [SMEM, VMEM, VMEM], [VMEM, VMEM], []
    )(place, keep, send)
    return query_grad, key_grad, value_grad


def solution(mesh):
    rows = P(("groups", "ctx"), None)
    return jax.shard_map(
        body,
        mesh=mesh,
        in_specs=(rows, rows, rows, rows, rows, P(None, ("groups", "ctx")), P("groups")),
        out_specs=(rows, rows, rows),
        check_vma=False,
    )
```

```python
import functools
import math

import jax
import jax.numpy as jnp
from jax import lax
from jax.experimental import pallas as pl
from jax.experimental.pallas import tpu as pltpu
from jax.sharding import PartitionSpec as P

HEAD_WIDTH = 128
KEY_VALUE_HEADS = 4
WINDOW = 896
SCALE = HEAD_WIDTH ** (-0.5)
LOG2E = math.log2(math.e)
HALF = KEY_VALUE_HEADS // 2

ANY = pl.BlockSpec(memory_space=pl.ANY)
VMEM = pl.BlockSpec(memory_space=pltpu.VMEM)
SMEM = pl.BlockSpec(memory_space=pltpu.SMEM)
HBM = pl.BlockSpec(memory_space=pltpu.HBM)
NT = (((1,), (1,)), ((), ()))
NN = (((1,), (0,)), ((), ()))


def dot(a, b, dims):
    return lax.dot_general(a, b, dims, preferred_element_type=jnp.float32)


def shift_pairs(devices, chips):
    first, last = max(0, -2 * chips), min(devices, devices - 2 * chips)
    return [(source, source + 2 * chips) for source in range(first, last)]


def pair_pairs(devices):
    return [(source, source ^ 2) for source in range(devices)]


def partner_pairs(devices):
    return [(source, source ^ 1) for source in range(devices)]


def cross_pairs(devices, chips):
    return [(source, target ^ 1) for source, target in shift_pairs(devices, chips)]


def half_rows(place, block, other):
    which = lax.rem(place[0], 2)
    return pl.ds(pl.multiple_of((1 - which if other else which) * block, 128), block)


def lanes(start, size):
    return pl.ds(pl.multiple_of(start, 128), size)


def weight(cost):
    return pl.CostEstimate(flops=1000 + 1000000000 * cost, bytes_accessed=1000 + 3690000 * cost, transcendentals=0)


def small_call(kernel, out_shape, in_specs, out_specs, scratch, cost=0, vmem=8, aliases=None):
    return pl.pallas_call(
        kernel,
        out_shape=out_shape,
        in_specs=in_specs,
        out_specs=out_specs,
        scratch_shapes=scratch,
        input_output_aliases=aliases or {},
        compiler_params=pltpu.CompilerParams(vmem_limit_bytes=vmem * 1024 * 1024),
        cost_estimate=weight(cost),
    )


def run_copies(pairs, sems):
    copies = [pltpu.make_async_copy(a, b, sems.at[i]) for i, (a, b) in enumerate(pairs)]
    for copy in copies:
        copy.start()
    for copy in copies:
        copy.wait()


def own_keys_kernel(place, k, v, own):
    core = lax.rem(place[0], 2)
    for g in range(HALF):
        source = lanes((core * HALF + g) * HEAD_WIDTH, HEAD_WIDTH)
        own[:, 2 * g * HEAD_WIDTH : (2 * g + 1) * HEAD_WIDTH] = k[:, source]
        own[:, (2 * g + 1) * HEAD_WIDTH : (2 * g + 2) * HEAD_WIDTH] = v[:, source]


def join_keys_kernel(place, own, k_other, v_other, joined):
    core = lax.rem(place[0], 2)
    block = own.shape[0]
    joined[pl.ds(pl.multiple_of(core * block, 128), block), :] = own[...]
    rows = pl.ds(pl.multiple_of((1 - core) * block, 128), block)
    for g in range(HALF):
        source = lanes((core * HALF + g) * HEAD_WIDTH, HEAD_WIDTH)
        joined[rows, 2 * g * HEAD_WIDTH : (2 * g + 1) * HEAD_WIDTH] = k_other[:, source]
        joined[rows, (2 * g + 1) * HEAD_WIDTH : (2 * g + 2) * HEAD_WIDTH] = v_other[:, source]


def stats_kernel(per_group, outputs, grad, norms, stats):
    ones = jnp.ones((8, 2 * HEAD_WIDTH), jnp.bfloat16)
    stats[...] = jnp.zeros_like(stats)
    for group in range(KEY_VALUE_HEADS):
        for r in range(per_group):
            head = group * per_group + r
            cols = slice(head * HEAD_WIDTH, (head + 1) * HEAD_WIDTH)
            product = outputs[:, cols].astype(jnp.float32) * grad[:, cols].astype(jnp.float32)
            high = product.astype(jnp.bfloat16)
            low = (product - high.astype(jnp.float32)).astype(jnp.bfloat16)
            delta = dot(ones, jnp.concatenate([high, low], axis=1), NT)
            stats[group, 8 + r : 9 + r, :] = delta[0:1, :]
            stats[group, r : r + 1, :] = norms[head : head + 1, :] * LOG2E


def tile(distance, row_start, query_rows, add, groups, queries, stats, kv, dkv, dq):
    per_group = queries.shape[1] // 2 // HALF // HEAD_WIDTH
    width = per_group * HEAD_WIDTH
    tokens = queries.shape[0]
    keys = kv.shape[0]
    key_start = row_start - distance * tokens
    q_positions = lax.broadcasted_iota(jnp.int32, (1, query_rows), 1)
    lowest = stats[0, per_group : per_group + 1, :query_rows].astype(jnp.int32)
    needed = jnp.min(stats[0, per_group : per_group + 1, :HEAD_WIDTH]) <= key_start + keys - 1

    @pl.when(needed)
    def _():
        k_positions = key_start + lax.broadcasted_iota(jnp.int32, (keys, query_rows), 0)
        allowed = (k_positions >= lowest) & (k_positions <= q_positions)
        allowed = jnp.concatenate([allowed] * per_group, axis=1)

        def group(g, carry):
            k = kv[:, lanes(2 * g * HEAD_WIDTH, HEAD_WIDTH)]
            v = kv[:, lanes((2 * g + 1) * HEAD_WIDTH, HEAD_WIDTH)]
            first = g * width
            q = jnp.concatenate(
                [queries[:query_rows, lanes(first + r * HEAD_WIDTH, HEAD_WIDTH)] for r in range(per_group)], 0
            )
            first = first + HALF * width
            grad = jnp.concatenate(
                [queries[:query_rows, lanes(first + r * HEAD_WIDTH, HEAD_WIDTH)] for r in range(per_group)], 0
            )
            norm = jnp.concatenate([stats[g, r : r + 1, :query_rows] for r in range(per_group)], 1)
            delta = jnp.concatenate([stats[g, 8 + r : 9 + r, :query_rows] for r in range(per_group)], 1)
            scores = dot(k, q, NT)
            weights = jnp.where(allowed, jnp.exp2(scores * (SCALE * LOG2E) - norm), 0.0)
            dv = dot(weights.astype(jnp.bfloat16), grad, NN)
            through = dot(v, grad, NT)
            ds = (weights * (through - delta)).astype(jnp.bfloat16)
            dk = dot(ds, q, NN)
            part = dot(k.T, ds, NN)
            for r in range(per_group):
                cols = slice(r * tokens, r * tokens + query_rows)
                piece = part[:, r * query_rows : (r + 1) * query_rows]
                dq[g, :, cols] = dq[g, :, cols] + piece if add else piece
            place = g - groups[0]
            dkv[:, lanes(2 * place * HEAD_WIDTH, HEAD_WIDTH)] = (dk * SCALE).astype(dkv.dtype)
            dkv[:, lanes((2 * place + 1) * HEAD_WIDTH, HEAD_WIDTH)] = dv.astype(dkv.dtype)
            return carry

        lax.fori_loop(groups[0], groups[1], group, 0)
        if not add:
            for g in range(HALF):
                if not groups[0] <= g < groups[1]:
                    dq[g] = jnp.zeros_like(dq[g])

    @pl.when(jnp.logical_not(needed))
    def _():
        dkv[...] = jnp.zeros_like(dkv)
        if not add:
            dq[...] = jnp.zeros_like(dq)


def join_queries_in_kernel(
    place, lengths, q, grad, q_other, grad_other, stats_mine, stats_other, queries, stats
):
    core = lax.rem(place[0], 2)
    block = q.shape[0]
    per_group = q.shape[1] // HEAD_WIDTH // KEY_VALUE_HEADS
    size = q.shape[1] // 2
    half = lanes(core * size, size)
    for q_part, grad_part, stats_part, which in (
        (q, grad, stats_mine, core),
        (q_other, grad_other, stats_other, 1 - core),
    ):
        rows = pl.ds(pl.multiple_of(which * block, 128), block)
        queries[rows, :size] = q_part[:, half]
        queries[rows, size:] = grad_part[:, half]
        for g in range(HALF):
            stats[g, :, rows] = stats_part[core * HALF + g]
    start = lax.div(place[0], 2) * 2 * block
    positions = start + lax.broadcasted_iota(jnp.int32, (1, 2 * block), 1)
    lowest = jnp.maximum(positions - (WINDOW - 1), 0)
    end = jnp.int32(0)
    for i in range(lengths.shape[0]):
        end = end + lengths[i]
        lowest = jnp.where(positions >= end, jnp.maximum(lowest, end), lowest)
    stats[0, per_group : per_group + 1, :] = (lowest - start).astype(jnp.float32)


def tile_kernel(config, *refs):
    distance, row_start, query_rows, add, groups = config
    queries, stats, kv = refs[:3]
    dkv, dq = refs[-2:]
    tile(distance, row_start, query_rows, add, groups, queries, stats, kv, dkv, dq)


def tile_call(
    distance, row_start, query_rows, queries, stats, kv, dq, kind=jnp.bfloat16, cost=0, groups=(0, HALF)
):
    add = dq is not None
    tokens, columns = queries.shape
    shape = (HALF, HEAD_WIDTH, columns // 2 // HALF // HEAD_WIDTH * tokens)
    return pl.pallas_call(
        functools.partial(tile_kernel, (distance, row_start, query_rows, add, groups)),
        in_specs=[VMEM] * (4 if add else 3),
        out_specs=[VMEM, VMEM],
        out_shape=[
            jax.ShapeDtypeStruct((kv.shape[0], (groups[1] - groups[0]) * 2 * HEAD_WIDTH), kind),
            jax.ShapeDtypeStruct(shape, jnp.float32),
        ],
        input_output_aliases={3: 1} if add else {},
        compiler_params=pltpu.CompilerParams(vmem_limit_bytes=24 * 1024 * 1024),
        cost_estimate=weight(cost),
    )(queries, stats, kv, *([dq] if add else []))


def split_kernel(place, whole, same, cross):
    for target, other in ((same, False), (cross, True)):
        target[...] = whole[half_rows(place, same.shape[0], other), :]


def gather_kernel(other, place, second, swapped, third, out):
    rows = half_rows(place, out.shape[0], other)
    odd = lax.rem(lax.div(place[0], 2), 2) == 1
    value = second[rows, :] + jnp.where(odd, swapped[rows, :].astype(jnp.float32), 0.0)
    out[...] = value + third[...].astype(jnp.float32)


def pass_on_kernel(other, place, value, fourth, out):
    which = lax.rem(place[0], 2)
    late = (1 - which if other else which) == 1
    out[...] = (value[...] + jnp.where(late, fourth[...].astype(jnp.float32), 0.0)).astype(out.dtype)


def finish_queries_kernel(place, dq, keep, send):
    core = lax.rem(place[0], 2)
    block = keep.shape[0]
    tokens = 2 * block
    per_group = keep.shape[1] // HEAD_WIDTH // HALF
    for g in range(HALF):
        for r in range(per_group):
            cols = slice((g * per_group + r) * HEAD_WIDTH, (g * per_group + r + 1) * HEAD_WIDTH)
            for target, which in ((send, 1 - core), (keep, core)):
                start = r * tokens + which * block
                piece = (dq[g, :, lanes(start, block)] * SCALE).astype(jnp.bfloat16)
                target[:, cols] = piece.T


def join_queries_kernel(place, keep, other, joined, sems):
    core = lax.rem(place[0], 2)
    size = keep.shape[1]
    run_copies(
        [(keep, joined.at[:, lanes(core * size, size)]), (other, joined.at[:, lanes((1 - core) * size, size)])],
        sems,
    )


def chip_sum_kernel(place, first, second, swapped, keep, send):
    even = lax.rem(lax.div(place[0], 2), 2) == 0
    for target, other in ((keep, False), (send, True)):
        rows = half_rows(place, keep.shape[0], other)
        total = jnp.concatenate([first[rows, :], second[rows, :]], axis=1)
        target[...] = total + jnp.where(even, swapped[rows, :].astype(jnp.float32), 0.0)


def last_sum_kernel(place, keep, same, got, cross, key_grad, value_grad):
    core = lax.rem(place[0], 2)
    for mine, home, which in ((keep, same, core), (got, cross, 1 - core)):
        value = (mine[...] + home[...].astype(jnp.float32)).astype(jnp.bfloat16)
        for g in range(HALF):
            target = lanes((which * HALF + g) * HEAD_WIDTH, HEAD_WIDTH)
            key_grad[:, target] = value[:, 2 * g * HEAD_WIDTH : (2 * g + 1) * HEAD_WIDTH]
            value_grad[:, target] = value[:, (2 * g + 1) * HEAD_WIDTH : (2 * g + 2) * HEAD_WIDTH]


def body(q, k, v, outputs, grad, norms, lengths):
    block = q.shape[0]
    tokens = 2 * block
    heads = norms.shape[0]
    per_group = heads // KEY_VALUE_HEADS
    width = per_group * HEAD_WIDTH
    devices = lax.axis_size("ctx")
    place = lax.axis_index("ctx").astype(jnp.int32).reshape(1)
    to_partner = partner_pairs(devices)
    assert -(-(WINDOW - 1) // block) == 7, "window"

    def bf16(*shape):
        return jax.ShapeDtypeStruct(shape, jnp.bfloat16)

    def f32(*shape):
        return jax.ShapeDtypeStruct(shape, jnp.float32)

    def move(array, chips):
        return lax.ppermute(array, "ctx", shift_pairs(devices, chips))

    def swap(array):
        return lax.ppermute(array, "ctx", to_partner)

    dma = pltpu.SemaphoreType.DMA
    kv_width = HALF * 2 * HEAD_WIDTH
    own = small_call(
        own_keys_kernel, bf16(block, kv_width), [SMEM, VMEM, VMEM], VMEM, [], 0
    )(place, k, v)
    kv = small_call(
        join_keys_kernel, bf16(tokens, kv_width), [SMEM] + [VMEM] * 3, VMEM, [], 20
    )(place, own, swap(k), swap(v))
    kv2 = move(kv, 2)
    kv1 = move(kv, 1)

    norms, kv = lax.optimization_barrier((norms, kv))
    stats_mine = small_call(
        functools.partial(stats_kernel, per_group),
        f32(KEY_VALUE_HEADS, 16, block),
        [VMEM, VMEM, VMEM],
        VMEM,
        [],
        50,
    )(outputs, grad, norms)
    stats_other = swap(stats_mine)
    q_late, grad_late, kv = lax.optimization_barrier((q, grad, kv))
    q_other, grad_other = swap(q_late), swap(grad_late)
    queries, stats = small_call(
        join_queries_in_kernel,
        [bf16(tokens, q.shape[1]), f32(HALF, 16, tokens)],
        [SMEM, SMEM] + [VMEM] * 6,
        [VMEM] * 2,
        [],
        2,
    )(place, lengths, q, grad, q_other, grad_other, stats_mine, stats_other)
    far = functools.partial(tile_call, queries=queries, stats=stats)
    first, dq = far(0, 0, tokens, kv=kv, dq=None, kind=jnp.float32, groups=(0, 1), cost=0)
    kv2, first = lax.optimization_barrier((kv2, first))
    kv3 = move(kv2, 1)
    kv4 = move(kv2[block:], 2)
    part1, dq = far(1, 0, tokens, kv=kv1, dq=dq, cost=0)
    second, dq = far(0, 0, tokens, kv=kv, dq=dq, kind=jnp.float32, groups=(1, HALF), cost=0)
    swapped = lax.ppermute(part1, "ctx", pair_pairs(devices))
    part3, dq = far(3, 0, tokens, kv=kv3, dq=dq, cost=0)
    third_same, third_cross = small_call(
        split_kernel, [bf16(block, kv_width)] * 2, [SMEM, VMEM], [VMEM, VMEM], []
    )(place, part3)
    third_same = move(third_same, -1)
    third_cross = move(third_cross, -1)
    part4, dq = far(4, block, block, kv=kv4, dq=dq, cost=2)
    part4 = move(part4, -2)
    part2, dq = far(2, 0, tokens, kv=kv2, dq=dq, kind=jnp.float32)
    homes = []
    for other, third in ((False, third_same), (True, third_cross)):
        value = small_call(
            functools.partial(gather_kernel, other),
            f32(block, kv_width),
            [SMEM] + [VMEM] * 3,
            VMEM,
            [],
            0 if other else 0,
        )(place, part2, swapped, third)
        piece = small_call(
            functools.partial(pass_on_kernel, other),
            bf16(block, kv_width),
            [SMEM, VMEM, VMEM],
            VMEM,
            [],
            8 if other else 0,
        )(place, value, part4)
        pairs = (cross_pairs if other else shift_pairs)(devices, -2)
        homes.append(lax.ppermute(piece, "ctx", pairs))
    same_home, cross_home = homes
    dq_keep, dq_send = small_call(
        finish_queries_kernel, [bf16(block, HALF * width)] * 2, [SMEM, VMEM], [VMEM, VMEM], []
    )(place, dq)
    dq_other = swap(dq_send)
    query_grad = small_call(
        join_queries_kernel, bf16(block, q.shape[1]), [SMEM, ANY, ANY], ANY, [dma((2,))]
    )(place, dq_keep, dq_other)

    keep, send = small_call(
        chip_sum_kernel, [f32(block, kv_width)] * 2, [SMEM] + [VMEM] * 3, [VMEM, VMEM], []
    )(place, first, second, swapped)
    got = swap(send)
    same_home, query_grad = lax.optimization_barrier((same_home, query_grad))
    key_grad, value_grad = small_call(
        last_sum_kernel, [bf16(block, kv_width)] * 2, [SMEM] + [VMEM] * 4, [VMEM, VMEM], [], 20
    )(place, keep, same_home, got, cross_home)
    return query_grad, key_grad, value_grad


def solution(mesh):
    rows = P(("groups", "ctx"), None)
    return jax.shard_map(
        body,
        mesh=mesh,
        in_specs=(rows, rows, rows, rows, rows, P(None, ("groups", "ctx")), P("groups")),
        out_specs=(rows, rows, rows),
        check_vma=False,
    )
```

```python
import functools
import math

import jax
import jax.numpy as jnp
from jax import lax
from jax.experimental import pallas as pl
from jax.experimental.pallas import tpu as pltpu
from jax.sharding import PartitionSpec as P

HEAD_WIDTH = 128
KEY_VALUE_HEADS = 4
WINDOW = 896
SCALE = HEAD_WIDTH ** (-0.5)
LOG2E = math.log2(math.e)
HALF = KEY_VALUE_HEADS // 2

ANY = pl.BlockSpec(memory_space=pl.ANY)
VMEM = pl.BlockSpec(memory_space=pltpu.VMEM)
SMEM = pl.BlockSpec(memory_space=pltpu.SMEM)
HBM = pl.BlockSpec(memory_space=pltpu.HBM)
NT = (((1,), (1,)), ((), ()))
NN = (((1,), (0,)), ((), ()))


def dot(a, b, dims):
    return lax.dot_general(a, b, dims, preferred_element_type=jnp.float32)


def shift_pairs(devices, chips):
    first, last = max(0, -2 * chips), min(devices, devices - 2 * chips)
    return [(source, source + 2 * chips) for source in range(first, last)]


def pair_pairs(devices):
    return [(source, source ^ 2) for source in range(devices)]


def partner_pairs(devices):
    return [(source, source ^ 1) for source in range(devices)]


def cross_pairs(devices, chips):
    return [(source, target ^ 1) for source, target in shift_pairs(devices, chips)]


def half_rows(place, block, other):
    which = lax.rem(place[0], 2)
    return pl.ds(pl.multiple_of((1 - which if other else which) * block, 128), block)


def lanes(start, size):
    return pl.ds(pl.multiple_of(start, 128), size)


def weight(cost):
    return pl.CostEstimate(flops=1000 + 1000000000 * cost, bytes_accessed=1000 + 3690000 * cost, transcendentals=0)


def small_call(kernel, out_shape, in_specs, out_specs, scratch, cost=0, vmem=8, aliases=None):
    return pl.pallas_call(
        kernel,
        out_shape=out_shape,
        in_specs=in_specs,
        out_specs=out_specs,
        scratch_shapes=scratch,
        input_output_aliases=aliases or {},
        compiler_params=pltpu.CompilerParams(vmem_limit_bytes=int(vmem * 1024 * 1024)),
        cost_estimate=weight(cost),
    )


def run_copies(pairs, sems):
    copies = [pltpu.make_async_copy(a, b, sems.at[i]) for i, (a, b) in enumerate(pairs)]
    for copy in copies:
        copy.start()
    for copy in copies:
        copy.wait()


def own_keys_kernel(place, k, v, own, sems):
    core = lax.rem(place[0], 2)
    pairs = []
    for g in range(HALF):
        source = lanes((core * HALF + g) * HEAD_WIDTH, HEAD_WIDTH)
        pairs.append((k.at[:, source], own.at[:, pl.ds(2 * g * HEAD_WIDTH, HEAD_WIDTH)]))
        pairs.append((v.at[:, source], own.at[:, pl.ds((2 * g + 1) * HEAD_WIDTH, HEAD_WIDTH)]))
    run_copies(pairs, sems)


def join_keys_kernel(place, own, k_other, v_other, joined):
    core = lax.rem(place[0], 2)
    block = own.shape[0]
    joined[pl.ds(pl.multiple_of(core * block, 128), block), :] = own[...]
    rows = pl.ds(pl.multiple_of((1 - core) * block, 128), block)
    for g in range(HALF):
        source = lanes((core * HALF + g) * HEAD_WIDTH, HEAD_WIDTH)
        joined[rows, 2 * g * HEAD_WIDTH : (2 * g + 1) * HEAD_WIDTH] = k_other[:, source]
        joined[rows, (2 * g + 1) * HEAD_WIDTH : (2 * g + 2) * HEAD_WIDTH] = v_other[:, source]


def stats_kernel(per_group, outputs, grad, norms, stats):
    ones = jnp.ones((8, 2 * HEAD_WIDTH), jnp.bfloat16)
    stats[...] = jnp.zeros_like(stats)
    for group in range(KEY_VALUE_HEADS):
        for r in range(per_group):
            head = group * per_group + r
            cols = slice(head * HEAD_WIDTH, (head + 1) * HEAD_WIDTH)
            product = outputs[:, cols].astype(jnp.float32) * grad[:, cols].astype(jnp.float32)
            high = product.astype(jnp.bfloat16)
            low = (product - high.astype(jnp.float32)).astype(jnp.bfloat16)
            delta = dot(ones, jnp.concatenate([high, low], axis=1), NT)
            stats[group, 8 + r : 9 + r, :] = delta[0:1, :]
            stats[group, r : r + 1, :] = norms[head : head + 1, :] * LOG2E


def tile(distance, row_start, query_rows, add, groups, queries, stats, kv, dkv, dq):
    per_group = queries.shape[1] // 2 // HALF // HEAD_WIDTH
    width = per_group * HEAD_WIDTH
    tokens = queries.shape[0]
    keys = kv.shape[0]
    key_start = row_start - distance * tokens
    q_positions = lax.broadcasted_iota(jnp.int32, (1, query_rows), 1)
    lowest = stats[0, per_group : per_group + 1, :query_rows].astype(jnp.int32)
    needed = jnp.min(stats[0, per_group : per_group + 1, :HEAD_WIDTH]) <= key_start + keys - 1

    @pl.when(needed)
    def _():
        k_positions = key_start + lax.broadcasted_iota(jnp.int32, (keys, query_rows), 0)
        allowed = (k_positions >= lowest) & (k_positions <= q_positions)
        allowed = jnp.concatenate([allowed] * per_group, axis=1)

        def group(g, carry):
            k = kv[:, lanes(2 * g * HEAD_WIDTH, HEAD_WIDTH)]
            v = kv[:, lanes((2 * g + 1) * HEAD_WIDTH, HEAD_WIDTH)]
            first = g * width
            q = jnp.concatenate(
                [queries[:query_rows, lanes(first + r * HEAD_WIDTH, HEAD_WIDTH)] for r in range(per_group)], 0
            )
            first = first + HALF * width
            grad = jnp.concatenate(
                [queries[:query_rows, lanes(first + r * HEAD_WIDTH, HEAD_WIDTH)] for r in range(per_group)], 0
            )
            norm = jnp.concatenate([stats[g, r : r + 1, :query_rows] for r in range(per_group)], 1)
            delta = jnp.concatenate([stats[g, 8 + r : 9 + r, :query_rows] for r in range(per_group)], 1)
            scores = dot(k, q, NT)
            weights = jnp.where(allowed, jnp.exp2(scores * (SCALE * LOG2E) - norm), 0.0)
            dv = dot(weights.astype(jnp.bfloat16), grad, NN)
            through = dot(v, grad, NT)
            ds = (weights * (through - delta)).astype(jnp.bfloat16)
            dk = dot(ds, q, NN)
            part = dot(k.T, ds, NN)
            for r in range(per_group):
                cols = slice(r * tokens, r * tokens + query_rows)
                piece = part[:, r * query_rows : (r + 1) * query_rows]
                dq[g, :, cols] = dq[g, :, cols] + piece if add else piece
            place = g - groups[0]
            dkv[:, lanes(2 * place * HEAD_WIDTH, HEAD_WIDTH)] = (dk * SCALE).astype(dkv.dtype)
            dkv[:, lanes((2 * place + 1) * HEAD_WIDTH, HEAD_WIDTH)] = dv.astype(dkv.dtype)
            return carry

        lax.fori_loop(groups[0], groups[1], group, 0)
        if not add:
            for g in range(HALF):
                if not groups[0] <= g < groups[1]:
                    dq[g] = jnp.zeros_like(dq[g])

    @pl.when(jnp.logical_not(needed))
    def _():
        dkv[...] = jnp.zeros_like(dkv)
        if not add:
            dq[...] = jnp.zeros_like(dq)


def join_queries_in_kernel(
    place, lengths, q, grad, q_other, grad_other, stats_mine, stats_other, queries, stats
):
    core = lax.rem(place[0], 2)
    block = q.shape[0]
    per_group = q.shape[1] // HEAD_WIDTH // KEY_VALUE_HEADS
    size = q.shape[1] // 2
    half = lanes(core * size, size)
    for q_part, grad_part, stats_part, which in (
        (q, grad, stats_mine, core),
        (q_other, grad_other, stats_other, 1 - core),
    ):
        rows = pl.ds(pl.multiple_of(which * block, 128), block)
        queries[rows, :size] = q_part[:, half]
        queries[rows, size:] = grad_part[:, half]
        for g in range(HALF):
            stats[g, :, rows] = stats_part[core * HALF + g]
    start = lax.div(place[0], 2) * 2 * block
    positions = start + lax.broadcasted_iota(jnp.int32, (1, 2 * block), 1)
    lowest = jnp.maximum(positions - (WINDOW - 1), 0)
    end = jnp.int32(0)
    for i in range(lengths.shape[0]):
        end = end + lengths[i]
        lowest = jnp.where(positions >= end, jnp.maximum(lowest, end), lowest)
    stats[0, per_group : per_group + 1, :] = (lowest - start).astype(jnp.float32)


def tile_kernel(config, *refs):
    distance, row_start, query_rows, add, groups = config
    queries, stats, kv = refs[:3]
    dkv, dq = refs[-2:]
    tile(distance, row_start, query_rows, add, groups, queries, stats, kv, dkv, dq)


def tile_call(
    distance, row_start, query_rows, queries, stats, kv, dq, kind=jnp.bfloat16, cost=0, groups=(0, HALF)
):
    add = dq is not None
    tokens, columns = queries.shape
    shape = (HALF, HEAD_WIDTH, columns // 2 // HALF // HEAD_WIDTH * tokens)
    return pl.pallas_call(
        functools.partial(tile_kernel, (distance, row_start, query_rows, add, groups)),
        in_specs=[VMEM] * (4 if add else 3),
        out_specs=[VMEM, VMEM],
        out_shape=[
            jax.ShapeDtypeStruct((kv.shape[0], (groups[1] - groups[0]) * 2 * HEAD_WIDTH), kind),
            jax.ShapeDtypeStruct(shape, jnp.float32),
        ],
        input_output_aliases={3: 1} if add else {},
        compiler_params=pltpu.CompilerParams(vmem_limit_bytes=24 * 1024 * 1024),
        cost_estimate=weight(cost),
    )(queries, stats, kv, *([dq] if add else []))


def split_kernel(place, whole, same, cross):
    for target, other in ((same, False), (cross, True)):
        target[...] = whole[half_rows(place, same.shape[0], other), :]


def gather_kernel(other, place, second, swapped, third, out):
    rows = half_rows(place, out.shape[0], other)
    odd = lax.rem(lax.div(place[0], 2), 2) == 1
    value = second[rows, :] + jnp.where(odd, swapped[rows, :].astype(jnp.float32), 0.0)
    out[...] = value + third[...].astype(jnp.float32)


def pass_on_kernel(other, place, value, fourth, out):
    which = lax.rem(place[0], 2)
    late = (1 - which if other else which) == 1
    out[...] = (value[...] + jnp.where(late, fourth[...].astype(jnp.float32), 0.0)).astype(out.dtype)


def finish_queries_kernel(place, dq, keep, send):
    core = lax.rem(place[0], 2)
    block = keep.shape[0]
    tokens = 2 * block
    per_group = keep.shape[1] // HEAD_WIDTH // HALF
    for g in range(HALF):
        for r in range(per_group):
            cols = slice((g * per_group + r) * HEAD_WIDTH, (g * per_group + r + 1) * HEAD_WIDTH)
            for target, which in ((send, 1 - core), (keep, core)):
                start = r * tokens + which * block
                piece = (dq[g, :, lanes(start, block)] * SCALE).astype(jnp.bfloat16)
                target[:, cols] = piece.T


def join_queries_kernel(place, keep, other, joined, sems):
    core = lax.rem(place[0], 2)
    size = keep.shape[1]
    run_copies(
        [(keep, joined.at[:, lanes(core * size, size)]), (other, joined.at[:, lanes((1 - core) * size, size)])],
        sems,
    )


def chip_sum_kernel(place, first, second, swapped, keep, send):
    even = lax.rem(lax.div(place[0], 2), 2) == 0
    for target, other in ((keep, False), (send, True)):
        rows = half_rows(place, keep.shape[0], other)
        total = jnp.concatenate([first[rows, :], second[rows, :]], axis=1)
        target[...] = total + jnp.where(even, swapped[rows, :].astype(jnp.float32), 0.0)


def last_sum_kernel(place, keep, same, got, cross, key_grad, value_grad):
    core = lax.rem(place[0], 2)
    for mine, home, which in ((keep, same, core), (got, cross, 1 - core)):
        value = (mine[...] + home[...].astype(jnp.float32)).astype(jnp.bfloat16)
        for g in range(HALF):
            target = lanes((which * HALF + g) * HEAD_WIDTH, HEAD_WIDTH)
            key_grad[:, target] = value[:, 2 * g * HEAD_WIDTH : (2 * g + 1) * HEAD_WIDTH]
            value_grad[:, target] = value[:, (2 * g + 1) * HEAD_WIDTH : (2 * g + 2) * HEAD_WIDTH]


def body(q, k, v, outputs, grad, norms, lengths):
    block = q.shape[0]
    tokens = 2 * block
    heads = norms.shape[0]
    per_group = heads // KEY_VALUE_HEADS
    width = per_group * HEAD_WIDTH
    devices = lax.axis_size("ctx")
    place = lax.axis_index("ctx").astype(jnp.int32).reshape(1)
    to_partner = partner_pairs(devices)
    assert -(-(WINDOW - 1) // block) == 7, "window"

    def bf16(*shape):
        return jax.ShapeDtypeStruct(shape, jnp.bfloat16)

    def f32(*shape):
        return jax.ShapeDtypeStruct(shape, jnp.float32)

    def move(array, chips):
        return lax.ppermute(array, "ctx", shift_pairs(devices, chips))

    def swap(array):
        return lax.ppermute(array, "ctx", to_partner)

    dma = pltpu.SemaphoreType.DMA
    kv_width = HALF * 2 * HEAD_WIDTH
    own = small_call(
        own_keys_kernel, bf16(block, kv_width), [SMEM, HBM, HBM], VMEM, [dma((2 * HALF,))], 0, vmem=53.75
    )(place, k, v)
    kv = small_call(
        join_keys_kernel, bf16(tokens, kv_width), [SMEM] + [VMEM] * 3, VMEM, [], 20
    )(place, own, swap(k), swap(v))
    kv2 = move(kv, 2)
    kv1 = move(kv, 1)

    norms, kv = lax.optimization_barrier((norms, kv))
    stats_mine = small_call(
        functools.partial(stats_kernel, per_group),
        f32(KEY_VALUE_HEADS, 16, block),
        [VMEM, VMEM, VMEM],
        VMEM,
        [],
        50,
    )(outputs, grad, norms)
    stats_other = swap(stats_mine)
    q_late, grad_late, kv = lax.optimization_barrier((q, grad, kv))
    q_other, grad_other = swap(q_late), swap(grad_late)
    queries, stats = small_call(
        join_queries_in_kernel,
        [bf16(tokens, q.shape[1]), f32(HALF, 16, tokens)],
        [SMEM, SMEM] + [VMEM] * 6,
        [VMEM] * 2,
        [],
        2,
    )(place, lengths, q, grad, q_other, grad_other, stats_mine, stats_other)
    far = functools.partial(tile_call, queries=queries, stats=stats)
    first, dq = far(0, 0, tokens, kv=kv, dq=None, kind=jnp.float32, groups=(0, 1), cost=0)
    kv2, first = lax.optimization_barrier((kv2, first))
    kv3 = move(kv2, 1)
    kv4 = move(kv2[block:], 2)
    part1, dq = far(1, 0, tokens, kv=kv1, dq=dq, cost=0)
    second, dq = far(0, 0, tokens, kv=kv, dq=dq, kind=jnp.float32, groups=(1, HALF), cost=0)
    swapped = lax.ppermute(part1, "ctx", pair_pairs(devices))
    part3, dq = far(3, 0, tokens, kv=kv3, dq=dq, cost=0)
    third_same, third_cross = small_call(
        split_kernel, [bf16(block, kv_width)] * 2, [SMEM, VMEM], [VMEM, VMEM], []
    )(place, part3)
    third_same = move(third_same, -1)
    third_cross = move(third_cross, -1)
    part4, dq = far(4, block, block, kv=kv4, dq=dq, cost=2)
    part4 = move(part4, -2)
    part2, dq = far(2, 0, tokens, kv=kv2, dq=dq, kind=jnp.float32)
    homes = []
    for other, third in ((False, third_same), (True, third_cross)):
        value = small_call(
            functools.partial(gather_kernel, other),
            f32(block, kv_width),
            [SMEM] + [VMEM] * 3,
            VMEM,
            [],
            0 if other else 0,
        )(place, part2, swapped, third)
        piece = small_call(
            functools.partial(pass_on_kernel, other),
            bf16(block, kv_width),
            [SMEM, VMEM, VMEM],
            VMEM,
            [],
            8 if other else 0,
        )(place, value, part4)
        pairs = (cross_pairs if other else shift_pairs)(devices, -2)
        homes.append(lax.ppermute(piece, "ctx", pairs))
    same_home, cross_home = homes
    dq_keep, dq_send = small_call(
        finish_queries_kernel, [bf16(block, HALF * width)] * 2, [SMEM, VMEM], [VMEM, VMEM], []
    )(place, dq)
    dq_other = swap(dq_send)
    query_grad = small_call(
        join_queries_kernel, bf16(block, q.shape[1]), [SMEM, ANY, ANY], ANY, [dma((2,))]
    )(place, dq_keep, dq_other)

    keep, send = small_call(
        chip_sum_kernel, [f32(block, kv_width)] * 2, [SMEM] + [VMEM] * 3, [VMEM, VMEM], []
    )(place, first, second, swapped)
    got = swap(send)
    same_home, query_grad = lax.optimization_barrier((same_home, query_grad))
    key_grad, value_grad = small_call(
        last_sum_kernel, [bf16(block, kv_width)] * 2, [SMEM] + [VMEM] * 4, [VMEM, VMEM], [], 20
    )(place, keep, same_home, got, cross_home)
    return query_grad, key_grad, value_grad


def solution(mesh):
    rows = P(("groups", "ctx"), None)
    return jax.shard_map(
        body,
        mesh=mesh,
        in_specs=(rows, rows, rows, rows, rows, P(None, ("groups", "ctx")), P("groups")),
        out_specs=(rows, rows, rows),
        check_vma=False,
    )
```

```python
import functools
import math

import jax
import jax.numpy as jnp
from jax import lax
from jax.experimental import pallas as pl
from jax.experimental.pallas import tpu as pltpu
from jax.sharding import PartitionSpec as P

HEAD_WIDTH = 128
KEY_VALUE_HEADS = 4
WINDOW = 896
SCALE = HEAD_WIDTH ** (-0.5)
LOG2E = math.log2(math.e)
HALF = KEY_VALUE_HEADS // 2

ANY = pl.BlockSpec(memory_space=pl.ANY)
VMEM = pl.BlockSpec(memory_space=pltpu.VMEM)
SMEM = pl.BlockSpec(memory_space=pltpu.SMEM)
HBM = pl.BlockSpec(memory_space=pltpu.HBM)
NT = (((1,), (1,)), ((), ()))
NN = (((1,), (0,)), ((), ()))


def dot(a, b, dims):
    return lax.dot_general(a, b, dims, preferred_element_type=jnp.float32)


def shift_pairs(devices, chips):
    first, last = max(0, -2 * chips), min(devices, devices - 2 * chips)
    return [(source, source + 2 * chips) for source in range(first, last)]


def pair_pairs(devices):
    return [(source, source ^ 2) for source in range(devices)]


def partner_pairs(devices):
    return [(source, source ^ 1) for source in range(devices)]


def cross_pairs(devices, chips):
    return [(source, target ^ 1) for source, target in shift_pairs(devices, chips)]


def half_rows(place, block, other):
    which = lax.rem(place[0], 2)
    return pl.ds(pl.multiple_of((1 - which if other else which) * block, 128), block)


def lanes(start, size):
    return pl.ds(pl.multiple_of(start, 128), size)


def weight(cost):
    return pl.CostEstimate(flops=1000 + 1000000000 * cost, bytes_accessed=1000 + 3690000 * cost, transcendentals=0)


def small_call(kernel, out_shape, in_specs, out_specs, scratch, cost=0, vmem=8, aliases=None):
    return pl.pallas_call(
        kernel,
        out_shape=out_shape,
        in_specs=in_specs,
        out_specs=out_specs,
        scratch_shapes=scratch,
        input_output_aliases=aliases or {},
        compiler_params=pltpu.CompilerParams(vmem_limit_bytes=int(vmem * 1024 * 1024)),
        cost_estimate=weight(cost),
    )


def run_copies(pairs, sems):
    copies = [pltpu.make_async_copy(a, b, sems.at[i]) for i, (a, b) in enumerate(pairs)]
    for copy in copies:
        copy.start()
    for copy in copies:
        copy.wait()


def own_keys_kernel(place, k, v, own, sems):
    core = lax.rem(place[0], 2)
    pairs = []
    for g in range(HALF):
        source = lanes((core * HALF + g) * HEAD_WIDTH, HEAD_WIDTH)
        pairs.append((k.at[:, source], own.at[:, pl.ds(2 * g * HEAD_WIDTH, HEAD_WIDTH)]))
        pairs.append((v.at[:, source], own.at[:, pl.ds((2 * g + 1) * HEAD_WIDTH, HEAD_WIDTH)]))
    run_copies(pairs, sems)


def join_keys_kernel(place, own, k_other, v_other, joined):
    core = lax.rem(place[0], 2)
    block = own.shape[0]
    joined[pl.ds(pl.multiple_of(core * block, 128), block), :] = own[...]
    rows = pl.ds(pl.multiple_of((1 - core) * block, 128), block)
    for g in range(HALF):
        source = lanes((core * HALF + g) * HEAD_WIDTH, HEAD_WIDTH)
        joined[rows, 2 * g * HEAD_WIDTH : (2 * g + 1) * HEAD_WIDTH] = k_other[:, source]
        joined[rows, (2 * g + 1) * HEAD_WIDTH : (2 * g + 2) * HEAD_WIDTH] = v_other[:, source]


def stats_kernel(per_group, outputs, grad, norms, stats):
    ones = jnp.ones((8, 2 * HEAD_WIDTH), jnp.bfloat16)
    stats[...] = jnp.zeros_like(stats)
    for group in range(KEY_VALUE_HEADS):
        for r in range(per_group):
            head = group * per_group + r
            cols = slice(head * HEAD_WIDTH, (head + 1) * HEAD_WIDTH)
            product = outputs[:, cols].astype(jnp.float32) * grad[:, cols].astype(jnp.float32)
            high = product.astype(jnp.bfloat16)
            low = (product - high.astype(jnp.float32)).astype(jnp.bfloat16)
            delta = dot(ones, jnp.concatenate([high, low], axis=1), NT)
            stats[group, 8 + r : 9 + r, :] = delta[0:1, :]
            stats[group, r : r + 1, :] = norms[head : head + 1, :] * LOG2E


def tile(distance, row_start, query_rows, add, groups, queries, stats, kv, dkv, dq):
    per_group = queries.shape[1] // 2 // HALF // HEAD_WIDTH
    width = per_group * HEAD_WIDTH
    tokens = queries.shape[0]
    keys = kv.shape[0]
    key_start = row_start - distance * tokens
    q_positions = lax.broadcasted_iota(jnp.int32, (1, query_rows), 1)
    lowest = stats[0, per_group : per_group + 1, :query_rows].astype(jnp.int32)
    needed = jnp.min(stats[0, per_group : per_group + 1, :HEAD_WIDTH]) <= key_start + keys - 1

    @pl.when(needed)
    def _():
        k_positions = key_start + lax.broadcasted_iota(jnp.int32, (keys, query_rows), 0)
        allowed = (k_positions >= lowest) & (k_positions <= q_positions)
        allowed = jnp.concatenate([allowed] * per_group, axis=1)

        def group(g, carry):
            k = kv[:, lanes(2 * g * HEAD_WIDTH, HEAD_WIDTH)]
            v = kv[:, lanes((2 * g + 1) * HEAD_WIDTH, HEAD_WIDTH)]
            first = g * width
            q = jnp.concatenate(
                [queries[:query_rows, lanes(first + r * HEAD_WIDTH, HEAD_WIDTH)] for r in range(per_group)], 0
            )
            first = first + HALF * width
            grad = jnp.concatenate(
                [queries[:query_rows, lanes(first + r * HEAD_WIDTH, HEAD_WIDTH)] for r in range(per_group)], 0
            )
            norm = jnp.concatenate([stats[g, r : r + 1, :query_rows] for r in range(per_group)], 1)
            delta = jnp.concatenate([stats[g, 8 + r : 9 + r, :query_rows] for r in range(per_group)], 1)
            scores = dot(k, q, NT)
            weights = jnp.where(allowed, jnp.exp2(scores * (SCALE * LOG2E) - norm), 0.0)
            dv = dot(weights.astype(jnp.bfloat16), grad, NN)
            through = dot(v, grad, NT)
            ds = (weights * (through - delta)).astype(jnp.bfloat16)
            dk = dot(ds, q, NN)
            part = dot(k.T, ds, NN)
            for r in range(per_group):
                cols = slice(r * tokens, r * tokens + query_rows)
                piece = part[:, r * query_rows : (r + 1) * query_rows]
                dq[g, :, cols] = dq[g, :, cols] + piece if add else piece
            place = g - groups[0]
            dkv[:, lanes(2 * place * HEAD_WIDTH, HEAD_WIDTH)] = (dk * SCALE).astype(dkv.dtype)
            dkv[:, lanes((2 * place + 1) * HEAD_WIDTH, HEAD_WIDTH)] = dv.astype(dkv.dtype)
            return carry

        lax.fori_loop(groups[0], groups[1], group, 0, unroll=True)
        if not add:
            for g in range(HALF):
                if not groups[0] <= g < groups[1]:
                    dq[g] = jnp.zeros_like(dq[g])

    @pl.when(jnp.logical_not(needed))
    def _():
        dkv[...] = jnp.zeros_like(dkv)
        if not add:
            dq[...] = jnp.zeros_like(dq)


def join_queries_in_kernel(
    place, lengths, q, grad, q_other, grad_other, stats_mine, stats_other, queries, stats
):
    core = lax.rem(place[0], 2)
    block = q.shape[0]
    per_group = q.shape[1] // HEAD_WIDTH // KEY_VALUE_HEADS
    size = q.shape[1] // 2
    half = lanes(core * size, size)
    for q_part, grad_part, stats_part, which in (
        (q, grad, stats_mine, core),
        (q_other, grad_other, stats_other, 1 - core),
    ):
        rows = pl.ds(pl.multiple_of(which * block, 128), block)
        queries[rows, :size] = q_part[:, half]
        queries[rows, size:] = grad_part[:, half]
        for g in range(HALF):
            stats[g, :, rows] = stats_part[core * HALF + g]
    start = lax.div(place[0], 2) * 2 * block
    positions = start + lax.broadcasted_iota(jnp.int32, (1, 2 * block), 1)
    lowest = jnp.maximum(positions - (WINDOW - 1), 0)
    end = jnp.int32(0)
    for i in range(lengths.shape[0]):
        end = end + lengths[i]
        lowest = jnp.where(positions >= end, jnp.maximum(lowest, end), lowest)
    stats[0, per_group : per_group + 1, :] = (lowest - start).astype(jnp.float32)


def tile_kernel(config, *refs):
    distance, row_start, query_rows, add, groups = config
    queries, stats, kv = refs[:3]
    dkv, dq = refs[-2:]
    tile(distance, row_start, query_rows, add, groups, queries, stats, kv, dkv, dq)


def tile_call(
    distance, row_start, query_rows, queries, stats, kv, dq, kind=jnp.bfloat16, cost=0, groups=(0, HALF)
):
    add = dq is not None
    tokens, columns = queries.shape
    shape = (HALF, HEAD_WIDTH, columns // 2 // HALF // HEAD_WIDTH * tokens)
    return pl.pallas_call(
        functools.partial(tile_kernel, (distance, row_start, query_rows, add, groups)),
        in_specs=[VMEM] * (4 if add else 3),
        out_specs=[VMEM, VMEM],
        out_shape=[
            jax.ShapeDtypeStruct((kv.shape[0], (groups[1] - groups[0]) * 2 * HEAD_WIDTH), kind),
            jax.ShapeDtypeStruct(shape, jnp.float32),
        ],
        input_output_aliases={3: 1} if add else {},
        compiler_params=pltpu.CompilerParams(vmem_limit_bytes=24 * 1024 * 1024),
        cost_estimate=weight(cost),
    )(queries, stats, kv, *([dq] if add else []))


def split_kernel(place, whole, same, cross):
    for target, other in ((same, False), (cross, True)):
        target[...] = whole[half_rows(place, same.shape[0], other), :]


def gather_kernel(other, place, second, swapped, third, out):
    rows = half_rows(place, out.shape[0], other)
    odd = lax.rem(lax.div(place[0], 2), 2) == 1
    value = second[rows, :] + jnp.where(odd, swapped[rows, :].astype(jnp.float32), 0.0)
    out[...] = value + third[...].astype(jnp.float32)


def pass_on_kernel(other, place, value, fourth, out):
    which = lax.rem(place[0], 2)
    late = (1 - which if other else which) == 1
    out[...] = (value[...] + jnp.where(late, fourth[...].astype(jnp.float32), 0.0)).astype(out.dtype)


def finish_queries_kernel(place, dq, keep, send):
    core = lax.rem(place[0], 2)
    block = keep.shape[0]
    tokens = 2 * block
    per_group = keep.shape[1] // HEAD_WIDTH // HALF
    for g in range(HALF):
        for r in range(per_group):
            cols = slice((g * per_group + r) * HEAD_WIDTH, (g * per_group + r + 1) * HEAD_WIDTH)
            for target, which in ((send, 1 - core), (keep, core)):
                start = r * tokens + which * block
                piece = (dq[g, :, lanes(start, block)] * SCALE).astype(jnp.bfloat16)
                target[:, cols] = piece.T


def join_queries_kernel(place, keep, other, joined, sems):
    core = lax.rem(place[0], 2)
    size = keep.shape[1]
    run_copies(
        [(keep, joined.at[:, lanes(core * size, size)]), (other, joined.at[:, lanes((1 - core) * size, size)])],
        sems,
    )


def chip_sum_kernel(place, first, second, swapped, keep, send):
    even = lax.rem(lax.div(place[0], 2), 2) == 0
    for target, other in ((keep, False), (send, True)):
        rows = half_rows(place, keep.shape[0], other)
        total = jnp.concatenate([first[rows, :], second[rows, :]], axis=1)
        target[...] = total + jnp.where(even, swapped[rows, :].astype(jnp.float32), 0.0)


def last_sum_kernel(place, keep, same, got, cross, key_grad, value_grad):
    core = lax.rem(place[0], 2)
    for mine, home, which in ((keep, same, core), (got, cross, 1 - core)):
        value = (mine[...] + home[...].astype(jnp.float32)).astype(jnp.bfloat16)
        for g in range(HALF):
            target = lanes((which * HALF + g) * HEAD_WIDTH, HEAD_WIDTH)
            key_grad[:, target] = value[:, 2 * g * HEAD_WIDTH : (2 * g + 1) * HEAD_WIDTH]
            value_grad[:, target] = value[:, (2 * g + 1) * HEAD_WIDTH : (2 * g + 2) * HEAD_WIDTH]


def body(q, k, v, outputs, grad, norms, lengths):
    block = q.shape[0]
    tokens = 2 * block
    heads = norms.shape[0]
    per_group = heads // KEY_VALUE_HEADS
    width = per_group * HEAD_WIDTH
    devices = lax.axis_size("ctx")
    place = lax.axis_index("ctx").astype(jnp.int32).reshape(1)
    to_partner = partner_pairs(devices)
    assert -(-(WINDOW - 1) // block) == 7, "window"

    def bf16(*shape):
        return jax.ShapeDtypeStruct(shape, jnp.bfloat16)

    def f32(*shape):
        return jax.ShapeDtypeStruct(shape, jnp.float32)

    def move(array, chips):
        return lax.ppermute(array, "ctx", shift_pairs(devices, chips))

    def swap(array):
        return lax.ppermute(array, "ctx", to_partner)

    dma = pltpu.SemaphoreType.DMA
    kv_width = HALF * 2 * HEAD_WIDTH
    own = small_call(
        own_keys_kernel, bf16(block, kv_width), [SMEM, HBM, HBM], VMEM, [dma((2 * HALF,))], 0, vmem=53.75
    )(place, k, v)
    kv = small_call(
        join_keys_kernel, bf16(tokens, kv_width), [SMEM] + [VMEM] * 3, VMEM, [], 20
    )(place, own, swap(k), swap(v))
    kv2 = move(kv, 2)
    kv1 = move(kv, 1)

    norms, kv = lax.optimization_barrier((norms, kv))
    stats_mine = small_call(
        functools.partial(stats_kernel, per_group),
        f32(KEY_VALUE_HEADS, 16, block),
        [VMEM, VMEM, VMEM],
        VMEM,
        [],
        50,
    )(outputs, grad, norms)
    stats_other = swap(stats_mine)
    q_late, grad_late, kv = lax.optimization_barrier((q, grad, kv))
    q_other, grad_other = swap(q_late), swap(grad_late)
    queries, stats = small_call(
        join_queries_in_kernel,
        [bf16(tokens, q.shape[1]), f32(HALF, 16, tokens)],
        [SMEM, SMEM] + [VMEM] * 6,
        [VMEM] * 2,
        [],
        2,
    )(place, lengths, q, grad, q_other, grad_other, stats_mine, stats_other)
    far = functools.partial(tile_call, queries=queries, stats=stats)
    first, dq = far(0, 0, tokens, kv=kv, dq=None, kind=jnp.float32, groups=(0, 1), cost=0)
    kv2, first = lax.optimization_barrier((kv2, first))
    kv3 = move(kv2, 1)
    kv4 = move(kv2[block:], 2)
    part1, dq = far(1, 0, tokens, kv=kv1, dq=dq, cost=0)
    second, dq = far(0, 0, tokens, kv=kv, dq=dq, kind=jnp.float32, groups=(1, HALF), cost=0)
    swapped = lax.ppermute(part1, "ctx", pair_pairs(devices))
    part3, dq = far(3, 0, tokens, kv=kv3, dq=dq, cost=0)
    third_same, third_cross = small_call(
        split_kernel, [bf16(block, kv_width)] * 2, [SMEM, VMEM], [VMEM, VMEM], []
    )(place, part3)
    third_same = move(third_same, -1)
    third_cross = move(third_cross, -1)
    part4, dq = far(4, block, block, kv=kv4, dq=dq, cost=2)
    part4 = move(part4, -2)
    part2, dq = far(2, 0, tokens, kv=kv2, dq=dq, kind=jnp.float32)
    homes = []
    for other, third in ((False, third_same), (True, third_cross)):
        value = small_call(
            functools.partial(gather_kernel, other),
            f32(block, kv_width),
            [SMEM] + [VMEM] * 3,
            VMEM,
            [],
            0 if other else 0,
        )(place, part2, swapped, third)
        piece = small_call(
            functools.partial(pass_on_kernel, other),
            bf16(block, kv_width),
            [SMEM, VMEM, VMEM],
            VMEM,
            [],
            8 if other else 0,
        )(place, value, part4)
        pairs = (cross_pairs if other else shift_pairs)(devices, -2)
        homes.append(lax.ppermute(piece, "ctx", pairs))
    same_home, cross_home = homes
    dq_keep, dq_send = small_call(
        finish_queries_kernel, [bf16(block, HALF * width)] * 2, [SMEM, VMEM], [VMEM, VMEM], []
    )(place, dq)
    dq_other = swap(dq_send)
    query_grad = small_call(
        join_queries_kernel, bf16(block, q.shape[1]), [SMEM, ANY, ANY], ANY, [dma((2,))]
    )(place, dq_keep, dq_other)

    keep, send = small_call(
        chip_sum_kernel, [f32(block, kv_width)] * 2, [SMEM] + [VMEM] * 3, [VMEM, VMEM], []
    )(place, first, second, swapped)
    got = swap(send)
    same_home, query_grad = lax.optimization_barrier((same_home, query_grad))
    key_grad, value_grad = small_call(
        last_sum_kernel, [bf16(block, kv_width)] * 2, [SMEM] + [VMEM] * 4, [VMEM, VMEM], [], 20
    )(place, keep, same_home, got, cross_home)
    return query_grad, key_grad, value_grad


def solution(mesh):
    rows = P(("groups", "ctx"), None)
    return jax.shard_map(
        body,
        mesh=mesh,
        in_specs=(rows, rows, rows, rows, rows, P(None, ("groups", "ctx")), P("groups")),
        out_specs=(rows, rows, rows),
        check_vma=False,
    )
```

```python
import functools
import math

import jax
import jax.numpy as jnp
from jax import lax
from jax.experimental import pallas as pl
from jax.experimental.pallas import tpu as pltpu
from jax.sharding import PartitionSpec as P

HEAD_WIDTH = 128
KEY_VALUE_HEADS = 4
WINDOW = 896
SCALE = HEAD_WIDTH ** (-0.5)
LOG2E = math.log2(math.e)
HALF = KEY_VALUE_HEADS // 2

ANY = pl.BlockSpec(memory_space=pl.ANY)
VMEM = pl.BlockSpec(memory_space=pltpu.VMEM)
SMEM = pl.BlockSpec(memory_space=pltpu.SMEM)
HBM = pl.BlockSpec(memory_space=pltpu.HBM)
NT = (((1,), (1,)), ((), ()))
NN = (((1,), (0,)), ((), ()))


def dot(a, b, dims):
    return lax.dot_general(a, b, dims, preferred_element_type=jnp.float32)


def shift_pairs(devices, chips):
    first, last = max(0, -2 * chips), min(devices, devices - 2 * chips)
    return [(source, source + 2 * chips) for source in range(first, last)]


def pair_pairs(devices):
    return [(source, source ^ 2) for source in range(devices)]


def partner_pairs(devices):
    return [(source, source ^ 1) for source in range(devices)]


def cross_pairs(devices, chips):
    return [(source, target ^ 1) for source, target in shift_pairs(devices, chips)]


def half_rows(place, block, other):
    which = lax.rem(place[0], 2)
    return pl.ds(pl.multiple_of((1 - which if other else which) * block, 128), block)


def lanes(start, size):
    return pl.ds(pl.multiple_of(start, 128), size)


def weight(cost):
    return pl.CostEstimate(flops=1000 + 1000000000 * cost, bytes_accessed=1000 + 3690000 * cost, transcendentals=0)


def small_call(kernel, out_shape, in_specs, out_specs, scratch, cost=0, vmem=8, aliases=None):
    return pl.pallas_call(
        kernel,
        out_shape=out_shape,
        in_specs=in_specs,
        out_specs=out_specs,
        scratch_shapes=scratch,
        input_output_aliases=aliases or {},
        compiler_params=pltpu.CompilerParams(vmem_limit_bytes=int(vmem * 1024 * 1024)),
        cost_estimate=weight(cost),
    )


def run_copies(pairs, sems):
    copies = [pltpu.make_async_copy(a, b, sems.at[i]) for i, (a, b) in enumerate(pairs)]
    for copy in copies:
        copy.start()
    for copy in copies:
        copy.wait()


def own_keys_kernel(place, k, v, own, sems):
    core = lax.rem(place[0], 2)
    pairs = []
    for g in range(HALF):
        source = lanes((core * HALF + g) * HEAD_WIDTH, HEAD_WIDTH)
        pairs.append((k.at[:, source], own.at[:, pl.ds(2 * g * HEAD_WIDTH, HEAD_WIDTH)]))
        pairs.append((v.at[:, source], own.at[:, pl.ds((2 * g + 1) * HEAD_WIDTH, HEAD_WIDTH)]))
    run_copies(pairs, sems)


def join_keys_kernel(place, own, k_other, v_other, joined):
    core = lax.rem(place[0], 2)
    block = own.shape[0]
    joined[pl.ds(pl.multiple_of(core * block, 128), block), :] = own[...]
    rows = pl.ds(pl.multiple_of((1 - core) * block, 128), block)
    for g in range(HALF):
        source = lanes((core * HALF + g) * HEAD_WIDTH, HEAD_WIDTH)
        joined[rows, 2 * g * HEAD_WIDTH : (2 * g + 1) * HEAD_WIDTH] = k_other[:, source]
        joined[rows, (2 * g + 1) * HEAD_WIDTH : (2 * g + 2) * HEAD_WIDTH] = v_other[:, source]


def stats_kernel(per_group, outputs, grad, norms, stats):
    ones = jnp.ones((8, 2 * HEAD_WIDTH), jnp.bfloat16)
    stats[...] = jnp.zeros_like(stats)
    for group in range(KEY_VALUE_HEADS):
        for r in range(per_group):
            head = group * per_group + r
            cols = slice(head * HEAD_WIDTH, (head + 1) * HEAD_WIDTH)
            product = outputs[:, cols].astype(jnp.float32) * grad[:, cols].astype(jnp.float32)
            high = product.astype(jnp.bfloat16)
            low = (product - high.astype(jnp.float32)).astype(jnp.bfloat16)
            delta = dot(ones, jnp.concatenate([high, low], axis=1), NT)
            stats[group, 8 + r : 9 + r, :] = delta[0:1, :]
            stats[group, r : r + 1, :] = norms[head : head + 1, :] * LOG2E


def tile(distance, row_start, query_rows, add, groups, queries, stats, kv, dkv, dq):
    per_group = queries.shape[1] // 2 // HALF // HEAD_WIDTH
    width = per_group * HEAD_WIDTH
    tokens = queries.shape[0]
    keys = kv.shape[0]
    key_start = row_start - distance * tokens
    q_positions = lax.broadcasted_iota(jnp.int32, (1, query_rows), 1)
    lowest = stats[0, per_group : per_group + 1, :query_rows].astype(jnp.int32)
    needed = jnp.min(stats[0, per_group : per_group + 1, :HEAD_WIDTH]) <= key_start + keys - 1

    @pl.when(needed)
    def _():
        k_positions = key_start + lax.broadcasted_iota(jnp.int32, (keys, query_rows), 0)
        allowed = (k_positions >= lowest) & (k_positions <= q_positions)
        allowed = jnp.concatenate([allowed] * per_group, axis=1)

        def group(g, carry):
            k = kv[:, lanes(2 * g * HEAD_WIDTH, HEAD_WIDTH)]
            v = kv[:, lanes((2 * g + 1) * HEAD_WIDTH, HEAD_WIDTH)]
            first = g * width
            q = jnp.concatenate(
                [queries[:query_rows, lanes(first + r * HEAD_WIDTH, HEAD_WIDTH)] for r in range(per_group)], 0
            )
            first = first + HALF * width
            grad = jnp.concatenate(
                [queries[:query_rows, lanes(first + r * HEAD_WIDTH, HEAD_WIDTH)] for r in range(per_group)], 0
            )
            norm = jnp.concatenate([stats[g, r : r + 1, :query_rows] for r in range(per_group)], 1)
            delta = jnp.concatenate([stats[g, 8 + r : 9 + r, :query_rows] for r in range(per_group)], 1)
            scores = dot(k, q, NT)
            weights = jnp.where(allowed, jnp.exp2(scores * (SCALE * LOG2E) - norm), 0.0)
            dv = dot(weights.astype(jnp.bfloat16), grad, NN)
            through = dot(v, grad, NT)
            ds = (weights * (through - delta)).astype(jnp.bfloat16)
            dk = dot(ds, q, NN)
            part = dot(k.T, ds, NN)
            for r in range(per_group):
                cols = slice(r * tokens, r * tokens + query_rows)
                piece = part[:, r * query_rows : (r + 1) * query_rows]
                dq[g, :, cols] = dq[g, :, cols] + piece if add else piece
            place = g - groups[0]
            dkv[:, lanes(2 * place * HEAD_WIDTH, HEAD_WIDTH)] = (dk * SCALE).astype(dkv.dtype)
            dkv[:, lanes((2 * place + 1) * HEAD_WIDTH, HEAD_WIDTH)] = dv.astype(dkv.dtype)
            return carry

        lax.fori_loop(groups[0], groups[1], group, 0, unroll=True)
        if not add:
            for g in range(HALF):
                if not groups[0] <= g < groups[1]:
                    dq[g] = jnp.zeros_like(dq[g])

    @pl.when(jnp.logical_not(needed))
    def _():
        dkv[...] = jnp.zeros_like(dkv)
        if not add:
            dq[...] = jnp.zeros_like(dq)


def join_queries_in_kernel(
    place, lengths, q, grad, q_other, grad_other, stats_mine, stats_other, queries, stats
):
    core = lax.rem(place[0], 2)
    block = q.shape[0]
    per_group = q.shape[1] // HEAD_WIDTH // KEY_VALUE_HEADS
    size = q.shape[1] // 2
    half = lanes(core * size, size)
    for q_part, grad_part, stats_part, which in (
        (q, grad, stats_mine, core),
        (q_other, grad_other, stats_other, 1 - core),
    ):
        rows = pl.ds(pl.multiple_of(which * block, 128), block)
        queries[rows, :size] = q_part[:, half]
        queries[rows, size:] = grad_part[:, half]
        for g in range(HALF):
            stats[g, :, rows] = stats_part[core * HALF + g]
    start = lax.div(place[0], 2) * 2 * block
    positions = start + lax.broadcasted_iota(jnp.int32, (1, 2 * block), 1)
    lowest = jnp.maximum(positions - (WINDOW - 1), 0)
    end = jnp.zeros((1, 1), jnp.int32)
    for i in range(lengths.shape[1]):
        end = end + lengths[:, i : i + 1]
        lowest = jnp.where(positions >= end, jnp.maximum(lowest, end), lowest)
    stats[0, per_group : per_group + 1, :] = (lowest - start).astype(jnp.float32)


def tile_kernel(config, *refs):
    distance, row_start, query_rows, add, groups = config
    queries, stats, kv = refs[:3]
    dkv, dq = refs[-2:]
    tile(distance, row_start, query_rows, add, groups, queries, stats, kv, dkv, dq)


def tile_call(
    distance, row_start, query_rows, queries, stats, kv, dq, kind=jnp.bfloat16, cost=0, groups=(0, HALF)
):
    add = dq is not None
    tokens, columns = queries.shape
    shape = (HALF, HEAD_WIDTH, columns // 2 // HALF // HEAD_WIDTH * tokens)
    return pl.pallas_call(
        functools.partial(tile_kernel, (distance, row_start, query_rows, add, groups)),
        in_specs=[VMEM] * (4 if add else 3),
        out_specs=[VMEM, VMEM],
        out_shape=[
            jax.ShapeDtypeStruct((kv.shape[0], (groups[1] - groups[0]) * 2 * HEAD_WIDTH), kind),
            jax.ShapeDtypeStruct(shape, jnp.float32),
        ],
        input_output_aliases={3: 1} if add else {},
        compiler_params=pltpu.CompilerParams(vmem_limit_bytes=24 * 1024 * 1024),
        cost_estimate=weight(cost),
    )(queries, stats, kv, *([dq] if add else []))


def split_kernel(place, whole, same, cross):
    for target, other in ((same, False), (cross, True)):
        target[...] = whole[half_rows(place, same.shape[0], other), :]


def gather_kernel(other, place, second, swapped, third, out):
    rows = half_rows(place, out.shape[0], other)
    odd = lax.rem(lax.div(place[0], 2), 2) == 1
    value = second[rows, :] + jnp.where(odd, swapped[rows, :].astype(jnp.float32), 0.0)
    out[...] = value + third[...].astype(jnp.float32)


def pass_on_kernel(other, place, value, fourth, out):
    which = lax.rem(place[0], 2)
    late = (1 - which if other else which) == 1
    out[...] = (value[...] + jnp.where(late, fourth[...].astype(jnp.float32), 0.0)).astype(out.dtype)


def finish_queries_kernel(place, dq, keep, send):
    core = lax.rem(place[0], 2)
    block = keep.shape[0]
    tokens = 2 * block
    per_group = keep.shape[1] // HEAD_WIDTH // HALF
    for g in range(HALF):
        for r in range(per_group):
            cols = slice((g * per_group + r) * HEAD_WIDTH, (g * per_group + r + 1) * HEAD_WIDTH)
            for target, which in ((send, 1 - core), (keep, core)):
                start = r * tokens + which * block
                piece = (dq[g, :, lanes(start, block)] * SCALE).astype(jnp.bfloat16)
                target[:, cols] = piece.T


def join_queries_kernel(place, keep, other, joined, sems):
    core = lax.rem(place[0], 2)
    size = keep.shape[1]
    run_copies(
        [(keep, joined.at[:, lanes(core * size, size)]), (other, joined.at[:, lanes((1 - core) * size, size)])],
        sems,
    )


def chip_sum_kernel(place, first, second, swapped, keep, send):
    even = lax.rem(lax.div(place[0], 2), 2) == 0
    for target, other in ((keep, False), (send, True)):
        rows = half_rows(place, keep.shape[0], other)
        total = jnp.concatenate([first[rows, :], second[rows, :]], axis=1)
        target[...] = total + jnp.where(even, swapped[rows, :].astype(jnp.float32), 0.0)


def last_sum_kernel(place, keep, same, got, cross, key_grad, value_grad):
    core = lax.rem(place[0], 2)
    for mine, home, which in ((keep, same, core), (got, cross, 1 - core)):
        value = (mine[...] + home[...].astype(jnp.float32)).astype(jnp.bfloat16)
        for g in range(HALF):
            target = lanes((which * HALF + g) * HEAD_WIDTH, HEAD_WIDTH)
            key_grad[:, target] = value[:, 2 * g * HEAD_WIDTH : (2 * g + 1) * HEAD_WIDTH]
            value_grad[:, target] = value[:, (2 * g + 1) * HEAD_WIDTH : (2 * g + 2) * HEAD_WIDTH]


def body(q, k, v, outputs, grad, norms, lengths):
    block = q.shape[0]
    tokens = 2 * block
    heads = norms.shape[0]
    per_group = heads // KEY_VALUE_HEADS
    width = per_group * HEAD_WIDTH
    devices = lax.axis_size("ctx")
    place = lax.axis_index("ctx").astype(jnp.int32).reshape(1)
    to_partner = partner_pairs(devices)
    assert -(-(WINDOW - 1) // block) == 7, "window"

    def bf16(*shape):
        return jax.ShapeDtypeStruct(shape, jnp.bfloat16)

    def f32(*shape):
        return jax.ShapeDtypeStruct(shape, jnp.float32)

    def move(array, chips):
        return lax.ppermute(array, "ctx", shift_pairs(devices, chips))

    def swap(array):
        return lax.ppermute(array, "ctx", to_partner)

    dma = pltpu.SemaphoreType.DMA
    kv_width = HALF * 2 * HEAD_WIDTH
    own = small_call(
        own_keys_kernel, bf16(block, kv_width), [SMEM, HBM, HBM], VMEM, [dma((2 * HALF,))], 0, vmem=53.75
    )(place, k, v)
    kv = small_call(
        join_keys_kernel, bf16(tokens, kv_width), [SMEM] + [VMEM] * 3, VMEM, [], 20
    )(place, own, swap(k), swap(v))
    kv2 = move(kv, 2)
    kv1 = move(kv, 1)

    norms, kv = lax.optimization_barrier((norms, kv))
    stats_mine = small_call(
        functools.partial(stats_kernel, per_group),
        f32(KEY_VALUE_HEADS, 16, block),
        [VMEM, VMEM, VMEM],
        VMEM,
        [],
        50,
    )(outputs, grad, norms)
    stats_other = swap(stats_mine)
    q_late, grad_late, kv = lax.optimization_barrier((q, grad, kv))
    q_other, grad_other = swap(q_late), swap(grad_late)
    queries, stats = small_call(
        join_queries_in_kernel,
        [bf16(tokens, q.shape[1]), f32(HALF, 16, tokens)],
        [SMEM] + [VMEM] * 7,
        [VMEM] * 2,
        [],
        2,
    )(place, lengths.reshape(1, -1), q, grad, q_other, grad_other, stats_mine, stats_other)
    far = functools.partial(tile_call, queries=queries, stats=stats)
    first, dq = far(0, 0, tokens, kv=kv, dq=None, kind=jnp.float32, groups=(0, 1), cost=0)
    kv2, first = lax.optimization_barrier((kv2, first))
    kv3 = move(kv2, 1)
    kv4 = move(kv2[block:], 2)
    part1, dq = far(1, 0, tokens, kv=kv1, dq=dq, cost=0)
    second, dq = far(0, 0, tokens, kv=kv, dq=dq, kind=jnp.float32, groups=(1, HALF), cost=0)
    swapped = lax.ppermute(part1, "ctx", pair_pairs(devices))
    part3, dq = far(3, 0, tokens, kv=kv3, dq=dq, cost=0)
    third_same, third_cross = small_call(
        split_kernel, [bf16(block, kv_width)] * 2, [SMEM, VMEM], [VMEM, VMEM], []
    )(place, part3)
    third_same = move(third_same, -1)
    third_cross = move(third_cross, -1)
    part4, dq = far(4, block, block, kv=kv4, dq=dq, cost=2)
    part4 = move(part4, -2)
    part2, dq = far(2, 0, tokens, kv=kv2, dq=dq, kind=jnp.float32)
    homes = []
    for other, third in ((False, third_same), (True, third_cross)):
        value = small_call(
            functools.partial(gather_kernel, other),
            f32(block, kv_width),
            [SMEM] + [VMEM] * 3,
            VMEM,
            [],
            0 if other else 1,
        )(place, part2, swapped, third)
        piece = small_call(
            functools.partial(pass_on_kernel, other),
            bf16(block, kv_width),
            [SMEM, VMEM, VMEM],
            VMEM,
            [],
            8 if other else 0,
        )(place, value, part4)
        pairs = (cross_pairs if other else shift_pairs)(devices, -2)
        homes.append(lax.ppermute(piece, "ctx", pairs))
    same_home, cross_home = homes
    dq_keep, dq_send = small_call(
        finish_queries_kernel, [bf16(block, HALF * width)] * 2, [SMEM, VMEM], [VMEM, VMEM], []
    )(place, dq)
    dq_other = swap(dq_send)
    query_grad = small_call(
        join_queries_kernel, bf16(block, q.shape[1]), [SMEM, ANY, ANY], ANY, [dma((2,))]
    )(place, dq_keep, dq_other)

    keep, send = small_call(
        chip_sum_kernel, [f32(block, kv_width)] * 2, [SMEM] + [VMEM] * 3, [VMEM, VMEM], []
    )(place, first, second, swapped)
    got = swap(send)
    same_home, query_grad = lax.optimization_barrier((same_home, query_grad))
    key_grad, value_grad = small_call(
        last_sum_kernel, [bf16(block, kv_width)] * 2, [SMEM] + [VMEM] * 4, [VMEM, VMEM], [], 20
    )(place, keep, same_home, got, cross_home)
    return query_grad, key_grad, value_grad


def solution(mesh):
    rows = P(("groups", "ctx"), None)
    return jax.shard_map(
        body,
        mesh=mesh,
        in_specs=(rows, rows, rows, rows, rows, P(None, ("groups", "ctx")), P("groups")),
        out_specs=(rows, rows, rows),
        check_vma=False,
    )
```

```python
import functools
import math

import jax
import jax.numpy as jnp
from jax import lax
from jax.experimental import pallas as pl
from jax.experimental.pallas import tpu as pltpu
from jax.sharding import PartitionSpec as P

HEAD_WIDTH = 128
KEY_VALUE_HEADS = 4
WINDOW = 896
SCALE = HEAD_WIDTH ** (-0.5)
LOG2E = math.log2(math.e)
HALF = KEY_VALUE_HEADS // 2

ANY = pl.BlockSpec(memory_space=pl.ANY)
VMEM = pl.BlockSpec(memory_space=pltpu.VMEM)
SMEM = pl.BlockSpec(memory_space=pltpu.SMEM)
HBM = pl.BlockSpec(memory_space=pltpu.HBM)
NT = (((1,), (1,)), ((), ()))
NN = (((1,), (0,)), ((), ()))


def dot(a, b, dims):
    return lax.dot_general(a, b, dims, preferred_element_type=jnp.float32)


def shift_pairs(devices, chips):
    first, last = max(0, -2 * chips), min(devices, devices - 2 * chips)
    return [(source, source + 2 * chips) for source in range(first, last)]


def pair_pairs(devices):
    return [(source, source ^ 2) for source in range(devices)]


def partner_pairs(devices):
    return [(source, source ^ 1) for source in range(devices)]


def cross_pairs(devices, chips):
    return [(source, target ^ 1) for source, target in shift_pairs(devices, chips)]


def half_rows(place, block, other):
    which = lax.rem(place[0], 2)
    return pl.ds(pl.multiple_of((1 - which if other else which) * block, 128), block)


def lanes(start, size):
    return pl.ds(pl.multiple_of(start, 128), size)


def weight(cost):
    return pl.CostEstimate(flops=1000 + 1000000000 * cost, bytes_accessed=1000 + 3690000 * cost, transcendentals=0)


def small_call(kernel, out_shape, in_specs, out_specs, scratch, cost=0, vmem=8, aliases=None):
    return pl.pallas_call(
        kernel,
        out_shape=out_shape,
        in_specs=in_specs,
        out_specs=out_specs,
        scratch_shapes=scratch,
        input_output_aliases=aliases or {},
        compiler_params=pltpu.CompilerParams(vmem_limit_bytes=int(vmem * 1024 * 1024)),
        cost_estimate=weight(cost),
    )


def run_copies(pairs, sems):
    copies = [pltpu.make_async_copy(a, b, sems.at[i]) for i, (a, b) in enumerate(pairs)]
    for copy in copies:
        copy.start()
    for copy in copies:
        copy.wait()


def own_keys_kernel(place, k, v, own, sems):
    core = lax.rem(place[0], 2)
    pairs = []
    for g in range(HALF):
        source = lanes((core * HALF + g) * HEAD_WIDTH, HEAD_WIDTH)
        pairs.append((k.at[:, source], own.at[:, pl.ds(2 * g * HEAD_WIDTH, HEAD_WIDTH)]))
        pairs.append((v.at[:, source], own.at[:, pl.ds((2 * g + 1) * HEAD_WIDTH, HEAD_WIDTH)]))
    run_copies(pairs, sems)


def join_keys_kernel(place, own, k_other, v_other, joined):
    core = lax.rem(place[0], 2)
    block = own.shape[0]
    joined[pl.ds(pl.multiple_of(core * block, 128), block), :] = own[...]
    rows = pl.ds(pl.multiple_of((1 - core) * block, 128), block)
    for g in range(HALF):
        source = lanes((core * HALF + g) * HEAD_WIDTH, HEAD_WIDTH)
        joined[rows, 2 * g * HEAD_WIDTH : (2 * g + 1) * HEAD_WIDTH] = k_other[:, source]
        joined[rows, (2 * g + 1) * HEAD_WIDTH : (2 * g + 2) * HEAD_WIDTH] = v_other[:, source]


def stats_kernel(per_group, outputs, grad, norms, stats):
    ones = jnp.ones((8, 2 * HEAD_WIDTH), jnp.bfloat16)
    stats[...] = jnp.zeros_like(stats)
    for group in range(KEY_VALUE_HEADS):
        for r in range(per_group):
            head = group * per_group + r
            cols = slice(head * HEAD_WIDTH, (head + 1) * HEAD_WIDTH)
            product = outputs[:, cols].astype(jnp.float32) * grad[:, cols].astype(jnp.float32)
            high = product.astype(jnp.bfloat16)
            low = (product - high.astype(jnp.float32)).astype(jnp.bfloat16)
            delta = dot(ones, jnp.concatenate([high, low], axis=1), NT)
            stats[group, 8 + r : 9 + r, :] = delta[0:1, :]
            stats[group, r : r + 1, :] = norms[head : head + 1, :] * LOG2E


def tile(distance, row_start, query_rows, add, groups, queries, stats, kv, dkv, dq):
    per_group = queries.shape[1] // 2 // HALF // HEAD_WIDTH
    width = per_group * HEAD_WIDTH
    tokens = queries.shape[0]
    keys = kv.shape[0]
    key_start = row_start - distance * tokens
    q_positions = lax.broadcasted_iota(jnp.int32, (1, query_rows), 1)
    lowest = stats[0, per_group : per_group + 1, :query_rows].astype(jnp.int32)
    needed = jnp.min(stats[0, per_group : per_group + 1, :HEAD_WIDTH]) <= key_start + keys - 1

    @pl.when(needed)
    def _():
        k_positions = key_start + lax.broadcasted_iota(jnp.int32, (keys, query_rows), 0)
        allowed = (k_positions >= lowest) & (k_positions <= q_positions)
        allowed = jnp.concatenate([allowed] * per_group, axis=1)

        def group(g, carry):
            k = kv[:, lanes(2 * g * HEAD_WIDTH, HEAD_WIDTH)]
            v = kv[:, lanes((2 * g + 1) * HEAD_WIDTH, HEAD_WIDTH)]
            first = g * width
            q = jnp.concatenate(
                [queries[:query_rows, lanes(first + r * HEAD_WIDTH, HEAD_WIDTH)] for r in range(per_group)], 0
            )
            first = first + HALF * width
            grad = jnp.concatenate(
                [queries[:query_rows, lanes(first + r * HEAD_WIDTH, HEAD_WIDTH)] for r in range(per_group)], 0
            )
            norm = jnp.concatenate([stats[g, r : r + 1, :query_rows] for r in range(per_group)], 1)
            delta = jnp.concatenate([stats[g, 8 + r : 9 + r, :query_rows] for r in range(per_group)], 1)
            scores = dot(k, q, NT)
            weights = jnp.where(allowed, jnp.exp2(scores * (SCALE * LOG2E) - norm), 0.0)
            dv = dot(weights.astype(jnp.bfloat16), grad, NN)
            through = dot(v, grad, NT)
            ds = (weights * (through - delta)).astype(jnp.bfloat16)
            dk = dot(ds, q, NN)
            part = dot(k.T, ds, NN)
            for r in range(per_group):
                cols = slice(r * tokens, r * tokens + query_rows)
                piece = part[:, r * query_rows : (r + 1) * query_rows]
                dq[g, :, cols] = dq[g, :, cols] + piece if add else piece
            place = g - groups[0]
            dkv[:, lanes(2 * place * HEAD_WIDTH, HEAD_WIDTH)] = (dk * SCALE).astype(dkv.dtype)
            dkv[:, lanes((2 * place + 1) * HEAD_WIDTH, HEAD_WIDTH)] = dv.astype(dkv.dtype)
            return carry

        lax.fori_loop(groups[0], groups[1], group, 0, unroll=True)
        if not add:
            for g in range(HALF):
                if not groups[0] <= g < groups[1]:
                    dq[g] = jnp.zeros_like(dq[g])

    @pl.when(jnp.logical_not(needed))
    def _():
        dkv[...] = jnp.zeros_like(dkv)
        if not add:
            dq[...] = jnp.zeros_like(dq)


def join_queries_in_kernel(
    place, lengths, q, grad, q_other, grad_other, stats_mine, stats_other, queries, stats
):
    core = lax.rem(place[0], 2)
    block = q.shape[0]
    per_group = q.shape[1] // HEAD_WIDTH // KEY_VALUE_HEADS
    size = q.shape[1] // 2
    half = lanes(core * size, size)
    for q_part, grad_part, stats_part, which in (
        (q, grad, stats_mine, core),
        (q_other, grad_other, stats_other, 1 - core),
    ):
        rows = pl.ds(pl.multiple_of(which * block, 128), block)
        queries[rows, :size] = q_part[:, half]
        queries[rows, size:] = grad_part[:, half]
        for g in range(HALF):
            stats[g, :, rows] = stats_part[core * HALF + g]
    start = lax.div(place[0], 2) * 2 * block
    positions = start + lax.broadcasted_iota(jnp.int32, (1, 2 * block), 1)
    lowest = jnp.maximum(positions - (WINDOW - 1), 0)
    end = jnp.zeros((1, 1), jnp.int32)
    for i in range(lengths.shape[1]):
        end = end + lengths[:, i : i + 1]
        lowest = jnp.where(positions >= end, jnp.maximum(lowest, end), lowest)
    stats[0, per_group : per_group + 1, :] = (lowest - start).astype(jnp.float32)


def tile_kernel(config, *refs):
    distance, row_start, query_rows, add, groups = config
    queries, stats, kv = refs[:3]
    dkv, dq = refs[-2:]
    tile(distance, row_start, query_rows, add, groups, queries, stats, kv, dkv, dq)


def tile_call(
    distance, row_start, query_rows, queries, stats, kv, dq, kind=jnp.bfloat16, cost=0, groups=(0, HALF)
):
    add = dq is not None
    tokens, columns = queries.shape
    shape = (HALF, HEAD_WIDTH, columns // 2 // HALF // HEAD_WIDTH * tokens)
    return pl.pallas_call(
        functools.partial(tile_kernel, (distance, row_start, query_rows, add, groups)),
        in_specs=[VMEM] * (4 if add else 3),
        out_specs=[VMEM, VMEM],
        out_shape=[
            jax.ShapeDtypeStruct((kv.shape[0], (groups[1] - groups[0]) * 2 * HEAD_WIDTH), kind),
            jax.ShapeDtypeStruct(shape, jnp.float32),
        ],
        input_output_aliases={3: 1} if add else {},
        compiler_params=pltpu.CompilerParams(vmem_limit_bytes=24 * 1024 * 1024),
        cost_estimate=weight(cost),
    )(queries, stats, kv, *([dq] if add else []))


def split_kernel(place, whole, same, cross):
    for target, other in ((same, False), (cross, True)):
        target[...] = whole[half_rows(place, same.shape[0], other), :]


def gather_kernel(other, place, second, swapped, third, out):
    rows = half_rows(place, out.shape[0], other)
    odd = lax.rem(lax.div(place[0], 2), 2) == 1
    value = second[rows, :] + jnp.where(odd, swapped[rows, :].astype(jnp.float32), 0.0)
    out[...] = value + third[...].astype(jnp.float32)


def pass_on_kernel(other, place, value, fourth, out):
    which = lax.rem(place[0], 2)
    late = (1 - which if other else which) == 1
    out[...] = (value[...] + jnp.where(late, fourth[...].astype(jnp.float32), 0.0)).astype(out.dtype)


def second_half_kernel(place, second, swapped, third, fourth, out):
    rows = half_rows(place, out.shape[0], True)
    odd = lax.rem(lax.div(place[0], 2), 2) == 1
    value = second[rows, :] + jnp.where(odd, swapped[rows, :].astype(jnp.float32), 0.0)
    value = value + third[...].astype(jnp.float32)
    late = lax.rem(place[0], 2) == 0
    out[...] = (value + jnp.where(late, fourth[...].astype(jnp.float32), 0.0)).astype(out.dtype)


def finish_queries_kernel(place, dq, keep, send):
    core = lax.rem(place[0], 2)
    block = keep.shape[0]
    tokens = 2 * block
    per_group = keep.shape[1] // HEAD_WIDTH // HALF
    for g in range(HALF):
        for r in range(per_group):
            cols = slice((g * per_group + r) * HEAD_WIDTH, (g * per_group + r + 1) * HEAD_WIDTH)
            for target, which in ((send, 1 - core), (keep, core)):
                start = r * tokens + which * block
                piece = (dq[g, :, lanes(start, block)] * SCALE).astype(jnp.bfloat16)
                target[:, cols] = piece.T


def join_queries_kernel(place, keep, other, joined, sems):
    core = lax.rem(place[0], 2)
    size = keep.shape[1]
    run_copies(
        [(keep, joined.at[:, lanes(core * size, size)]), (other, joined.at[:, lanes((1 - core) * size, size)])],
        sems,
    )


def chip_sum_kernel(place, first, second, swapped, keep, send):
    even = lax.rem(lax.div(place[0], 2), 2) == 0
    for target, other in ((keep, False), (send, True)):
        rows = half_rows(place, keep.shape[0], other)
        total = jnp.concatenate([first[rows, :], second[rows, :]], axis=1)
        target[...] = total + jnp.where(even, swapped[rows, :].astype(jnp.float32), 0.0)


def last_sum_kernel(place, keep, same, got, cross, key_grad, value_grad):
    core = lax.rem(place[0], 2)
    for mine, home, which in ((keep, same, core), (got, cross, 1 - core)):
        value = (mine[...] + home[...].astype(jnp.float32)).astype(jnp.bfloat16)
        for g in range(HALF):
            target = lanes((which * HALF + g) * HEAD_WIDTH, HEAD_WIDTH)
            key_grad[:, target] = value[:, 2 * g * HEAD_WIDTH : (2 * g + 1) * HEAD_WIDTH]
            value_grad[:, target] = value[:, (2 * g + 1) * HEAD_WIDTH : (2 * g + 2) * HEAD_WIDTH]


def body(q, k, v, outputs, grad, norms, lengths):
    block = q.shape[0]
    tokens = 2 * block
    heads = norms.shape[0]
    per_group = heads // KEY_VALUE_HEADS
    width = per_group * HEAD_WIDTH
    devices = lax.axis_size("ctx")
    place = lax.axis_index("ctx").astype(jnp.int32).reshape(1)
    to_partner = partner_pairs(devices)
    assert -(-(WINDOW - 1) // block) == 7, "window"

    def bf16(*shape):
        return jax.ShapeDtypeStruct(shape, jnp.bfloat16)

    def f32(*shape):
        return jax.ShapeDtypeStruct(shape, jnp.float32)

    def move(array, chips):
        return lax.ppermute(array, "ctx", shift_pairs(devices, chips))

    def swap(array):
        return lax.ppermute(array, "ctx", to_partner)

    dma = pltpu.SemaphoreType.DMA
    kv_width = HALF * 2 * HEAD_WIDTH
    own = small_call(
        own_keys_kernel, bf16(block, kv_width), [SMEM, HBM, HBM], VMEM, [dma((2 * HALF,))], 0, vmem=53.75
    )(place, k, v)
    kv = small_call(
        join_keys_kernel, bf16(tokens, kv_width), [SMEM] + [VMEM] * 3, VMEM, [], 20
    )(place, own, swap(k), swap(v))
    kv2 = move(kv, 2)
    kv1 = move(kv, 1)

    norms, kv = lax.optimization_barrier((norms, kv))
    stats_mine = small_call(
        functools.partial(stats_kernel, per_group),
        f32(KEY_VALUE_HEADS, 16, block),
        [VMEM, VMEM, VMEM],
        VMEM,
        [],
        50,
    )(outputs, grad, norms)
    stats_other = swap(stats_mine)
    q_late, grad_late, kv = lax.optimization_barrier((q, grad, kv))
    q_other, grad_other = swap(q_late), swap(grad_late)
    queries, stats = small_call(
        join_queries_in_kernel,
        [bf16(tokens, q.shape[1]), f32(HALF, 16, tokens)],
        [SMEM] + [VMEM] * 7,
        [VMEM] * 2,
        [],
        2,
    )(place, lengths.reshape(1, -1), q, grad, q_other, grad_other, stats_mine, stats_other)
    far = functools.partial(tile_call, queries=queries, stats=stats)
    first, dq = far(0, 0, tokens, kv=kv, dq=None, kind=jnp.float32, groups=(0, 1), cost=0)
    kv2, first = lax.optimization_barrier((kv2, first))
    kv3 = move(kv2, 1)
    kv4 = move(kv2[block:], 2)
    part1, dq = far(1, 0, tokens, kv=kv1, dq=dq, cost=0)
    second, dq = far(0, 0, tokens, kv=kv, dq=dq, kind=jnp.float32, groups=(1, HALF), cost=0)
    swapped = lax.ppermute(part1, "ctx", pair_pairs(devices))
    part3, dq = far(3, 0, tokens, kv=kv3, dq=dq, cost=0)
    third_same, third_cross = small_call(
        split_kernel, [bf16(block, kv_width)] * 2, [SMEM, VMEM], [VMEM, VMEM], []
    )(place, part3)
    third_same = move(third_same, -1)
    third_cross = move(third_cross, -1)
    part4, dq = far(4, block, block, kv=kv4, dq=dq, cost=2)
    part4 = move(part4, -2)
    part2, dq = far(2, 0, tokens, kv=kv2, dq=dq, kind=jnp.float32)
    homes = []
    value = small_call(
        functools.partial(gather_kernel, False), f32(block, kv_width), [SMEM] + [VMEM] * 3, VMEM, [], 1
    )(place, part2, swapped, third_same)
    piece = small_call(
        functools.partial(pass_on_kernel, False), bf16(block, kv_width), [SMEM, VMEM, VMEM], VMEM, []
    )(place, value, part4)
    homes.append(lax.ppermute(piece, "ctx", shift_pairs(devices, -2)))
    piece = small_call(
        second_half_kernel, bf16(block, kv_width), [SMEM] + [VMEM] * 4, VMEM, [], 8
    )(place, part2, swapped, third_cross, part4)
    homes.append(lax.ppermute(piece, "ctx", cross_pairs(devices, -2)))
    same_home, cross_home = homes
    dq_keep, dq_send = small_call(
        finish_queries_kernel, [bf16(block, HALF * width)] * 2, [SMEM, VMEM], [VMEM, VMEM], []
    )(place, dq)
    dq_other = swap(dq_send)
    query_grad = small_call(
        join_queries_kernel, bf16(block, q.shape[1]), [SMEM, ANY, ANY], ANY, [dma((2,))]
    )(place, dq_keep, dq_other)

    keep, send = small_call(
        chip_sum_kernel, [f32(block, kv_width)] * 2, [SMEM] + [VMEM] * 3, [VMEM, VMEM], []
    )(place, first, second, swapped)
    got = swap(send)
    same_home, query_grad = lax.optimization_barrier((same_home, query_grad))
    key_grad, value_grad = small_call(
        last_sum_kernel, [bf16(block, kv_width)] * 2, [SMEM] + [VMEM] * 4, [VMEM, VMEM], [], 20
    )(place, keep, same_home, got, cross_home)
    return query_grad, key_grad, value_grad


def solution(mesh):
    rows = P(("groups", "ctx"), None)
    return jax.shard_map(
        body,
        mesh=mesh,
        in_specs=(rows, rows, rows, rows, rows, P(None, ("groups", "ctx")), P("groups")),
        out_specs=(rows, rows, rows),
        check_vma=False,
    )
```
